128 devices in a mesh: lon: 8 (over z, x_lo), lat: 16 (over y, x_hi, core).
Axes of the slice: x: 4 (x_hi: 2, x_lo: 2; x = x_hi * 2 + x_lo), y: 4, z: 4, core: 2. Of those that a mesh axis runs over, the one named last changes fastest.
Arguments:
- monthly_field: bfloat16 [512, 240, 1440], P(('lon', 'lat')), may hold values from -8 to 8
- half_width: int32 [240], P('lat'), may hold values from 1 to 64, as said below
- land_mask: int32 [240, 1440], P('lat', 'lon'), may hold values 0 or 1
Outputs:
- patterns: bfloat16 [512, 240, 1440], P(None, 'lat', 'lon')
- whitener: float32 [512, 512], replicated
The draws below stay inside these ranges and needn't reach their ends.
Inputs may be any that keep to these rules, and one draw needn't show every extreme that they name: `half_width`: some grid row has a half-width of exactly 64.
All inputs are finite; a program needn't handle non-finite values. No bound on the sum of `land_mask` on one device may be relied on, other than what follows from the above.
Results may differ from the reference program's by a relative error of at most 0.0079.
Values may be sent and summed in bfloat16 or wider, within the bound.
No kernel may reach another device: no remote copies, remote signals or barrier semaphores. Data moves between devices by JAX's collectives and lax.ppermute only.
A program may use at most 128 MiB of HBM per device.

```python
import math
import jax
import jax.numpy as jnp
from jax import lax

MONTHS = 512
LAT_DEV = 15
LON_DEV = 180
HMAX = 64
HL = 2
ITERS = 8
NLAT = 240
NLON = 1440


def draw_monthly_field(key, part):
    key = jax.random.fold_in(key, 11)
    subkeys = jax.random.split(key, 1)
    values = jnp.clip(jax.random.normal(subkeys[0], (MONTHS, NLAT, NLON), jnp.float32), -6.0, 6.0)
    return values.astype(jnp.bfloat16)


def draw_half_width(key, part):
    key = jax.random.fold_in(key, 5)
    subkeys = jax.random.split(key, 2)
    widths = jax.random.randint(subkeys[0], (NLAT,), 1, HMAX + 1)
    chosen = jax.random.randint(subkeys[1], (), 0, NLAT)
    return jnp.where(jnp.arange(NLAT) == chosen, HMAX, widths).astype(jnp.int32)


def place_ends(entries, key, least, top_value):
    shape = entries.shape
    index_at = [jax.random.randint(jax.random.fold_in(key, axis), (), 0, shape[axis]) for axis in range(len(shape))]
    entries = entries.at[tuple(index_at)].set(least)
    longest = shape.index(max(shape))
    index_at[longest] = (index_at[longest] + 1) % shape[longest]
    return entries.at[tuple(index_at)].set(top_value)


def setup_inputs(seed: int = 0) -> dict:
    key_of = jax.random.split(jax.random.key(seed), 4)
    monthly_field = draw_monthly_field(jax.random.fold_in(key_of[3], 71), 0)
    half_width = draw_half_width(jax.random.fold_in(key_of[3], 71), 0)
    land_mask = place_ends((jax.random.randint(key_of[2], (NLAT, NLON), 0, 10) < 7).astype(jnp.int32), jax.random.fold_in(key_of[2], 1), 0, 1)
    return dict(monthly_field=monthly_field, half_width=half_width, land_mask=land_mask)


def gauss_band(widths, half_span, band_cols):
    offsets = (jnp.arange(band_cols + 2 * half_span)[:, None] - half_span - jnp.arange(band_cols)[None, :]).astype(jnp.float32)
    reach = widths.astype(jnp.float32)
    spread = 0.5 * reach
    tap_offsets = jnp.arange(-half_span, half_span + 1).astype(jnp.float32)
    tap_values = jnp.exp(-(tap_offsets[None, :] * tap_offsets[None, :]) / (2.0 * spread[:, None] * spread[:, None]))
    tap_values = tap_values * (jnp.abs(tap_offsets)[None, :] <= reach[:, None]).astype(jnp.float32)
    tap_total = lax.optimization_barrier(jnp.sum(tap_values, axis=1))
    inside = (jnp.abs(offsets)[None] <= reach[:, None, None]).astype(jnp.float32)
    square = offsets[None] * offsets[None]
    band = jnp.exp(-square / (2.0 * spread[:, None, None] * spread[:, None, None])) * inside / tap_total[:, None, None]
    return band.astype(jnp.bfloat16)

def wrap_windows(source, band_cols, half_span):
    blocks = source.reshape(source.shape[:-1] + (source.shape[-1] // band_cols, band_cols))
    before = jnp.roll(blocks, 1, axis=-2)[..., band_cols - half_span:]
    after = jnp.roll(blocks, -1, axis=-2)[..., :half_span]
    return jnp.concatenate([before, blocks, after], axis=-1)

def pole_windows(source, band_rows, half_span):
    blocks = source.reshape(source.shape[0], source.shape[1] // band_rows, band_rows, source.shape[2])
    zeros_block = jnp.zeros_like(blocks[:, :1])
    before = jnp.concatenate([zeros_block, blocks[:, :-1]], axis=1)[:, :, band_rows - half_span:]
    after = jnp.concatenate([blocks[:, 1:], zeros_block], axis=1)[:, :, :half_span]
    return jnp.concatenate([before, blocks, after], axis=2)

def smooth_months(months_block, widths):
    band_lon = gauss_band(widths, HMAX, LON_DEV).astype(jnp.float32)
    windows = wrap_windows(months_block, LON_DEV, HMAX).astype(jnp.float32)
    lonpass = jnp.einsum('mrbj,rjk->mrbk', windows, band_lon).astype(jnp.bfloat16).reshape(months_block.shape)
    band_lat = gauss_band(jnp.full((1,), HL, jnp.int32), HL, LAT_DEV)[0].astype(jnp.float32)
    lat_windows = pole_windows(lonpass, LAT_DEV, HL).astype(jnp.float32)
    smoothed = jnp.einsum('mbin,io->mbon', lat_windows, band_lat)
    return smoothed.astype(jnp.bfloat16).reshape(months_block.shape)

def reference(monthly_field, half_width, land_mask):
    blocks = monthly_field.reshape(MONTHS // 16, 16, NLAT, NLON)
    smoothed = lax.map(lambda months_block: smooth_months(months_block, half_width), blocks).reshape(monthly_field.shape)
    mean_field = lax.optimization_barrier(jnp.mean(smoothed.astype(jnp.float32), axis=0))
    latitude = math.pi * ((jnp.arange(NLAT).astype(jnp.float32) + 0.5) / NLAT - 0.5)
    weight = jnp.sqrt(jnp.cos(latitude))[:, None] * land_mask.astype(jnp.float32)
    anomaly = ((smoothed.astype(jnp.float32) - mean_field) * weight).astype(jnp.bfloat16)
    rows_first = jnp.moveaxis(anomaly, 1, 0)

    def add_row(running, lat_row):
        return (running + jnp.dot(lat_row, lat_row.T, preferred_element_type=jnp.float32), None)
    gram, unused = lax.scan(add_row, jnp.zeros((MONTHS, MONTHS), jnp.float32), rows_first)
    frobenius = jnp.sqrt(jnp.sum(gram * gram) + 1e-06)
    identity = jnp.eye(MONTHS, dtype=jnp.float32)
    iterate_y = gram / frobenius
    iterate_z = identity
    for sweep in range(ITERS):
        factor = 1.5 * identity - 0.5 * jnp.dot(iterate_z, iterate_y, precision=lax.Precision.HIGHEST)
        iterate_y = jnp.dot(iterate_y, factor, precision=lax.Precision.HIGHEST)
        iterate_z = jnp.dot(factor, iterate_z, precision=lax.Precision.HIGHEST)
    whitener = iterate_z * jnp.sqrt(float(NLAT * NLON) / frobenius)
    whitener_b = whitener.astype(jnp.bfloat16)
    pattern_rows = lax.map(lambda lat_row: jnp.dot(whitener_b, lat_row, preferred_element_type=jnp.float32).astype(jnp.bfloat16), rows_first)
    patterns = jnp.moveaxis(pattern_rows, 0, 1)
    return (patterns, whitener)
```

```python
import math

import jax
import jax.numpy as jnp
import numpy as np
from jax import lax
from jax.experimental import pallas as pl
from jax.experimental.pallas import tpu as pltpu
from jax.sharding import PartitionSpec as P

HMAX = 64
HL = 2
ITERS = 8
BOTH = ("lon", "lat")
N_LON = 8
N_LAT = 16
NLAT = 240
NLON = 1440
MONTHS = 512
MON_DEV = 4
LAT_DEV = 15
LON_DEV = 180
LANES = 128
GROUPS = 22
SECOND = 56
TAIL = 112
CHUNK = MON_DEV * GROUPS
WINDOWS = MON_DEV * N_LON
SROWS = 3 * WINDOWS
SSTRIDE = 97
VSTRIDE = 89
BLOCKS = [(i, j) for i in range(4) for j in range(i, 4)]
PACK = len(BLOCKS)
VMEM_LIMIT = 60 * 1024 * 1024


def lat_taps():
    offsets = np.arange(-HL, HL + 1).astype(np.float32)
    taps = np.exp(-(offsets * offsets) / np.float32(2.0)).astype(np.float32)
    taps = taps / taps.sum(dtype=np.float32)
    return [float(t) for t in taps.astype(jnp.bfloat16).astype(np.float32)]


def smooth_kernel(widths, field, out, taps, windows, passed, staged):
    lane8 = lax.broadcasted_iota(jnp.int32, (8, LANES), 1)
    sub8 = lax.broadcasted_iota(jnp.int32, (8, LANES), 0)

    def build_taps(i, carry):
        reach = jnp.zeros((8, LANES), jnp.int32)
        for s in range(8):
            reach = jnp.where(sub8 == s, widths[i * 8 + s], reach)
        reach = reach.astype(jnp.float32)
        spread = 0.5 * reach
        offset = (lane8 - HMAX).astype(jnp.float32)
        value = jnp.exp(-(offset * offset) / (2.0 * spread * spread))
        value = jnp.where(jnp.abs(offset) <= reach, value, 0.0)
        total = jnp.sum(value, axis=1, keepdims=True) + value[:, 0:1]
        value = (value / total).astype(jnp.bfloat16).astype(jnp.float32)
        taps[pl.ds(pl.multiple_of(i * 8, 8), 8), :] = value
        return carry

    lax.fori_loop(0, NLAT // 8, build_taps, 0)

    def build_windows(i, carry):
        for m in range(MON_DEV):
            rows = field[m, pl.ds(pl.multiple_of(i * 16, 16), 16), :].astype(jnp.float32)
            ring = jnp.concatenate([rows, rows[:, :224]], axis=1)
            for l in range(N_LON):
                for j in range(3):
                    start = LON_DEV * l - HMAX + LANES * j
                    start = start + NLON if start < 0 else start
                    piece = ring[:, start : start + LANES]
                    for half in range(2):
                        first = (i * 16 + half * 8) * SSTRIDE + j * WINDOWS + m * N_LON + l
                        windows[pl.ds(first, 8, stride=SSTRIDE), :] = piece[half * 8 : half * 8 + 8]
        return carry

    lax.fori_loop(0, NLAT // 16, build_windows, 0)

    edge = jnp.zeros((HL, 2 * WINDOWS, LANES), jnp.float32)
    passed[0:HL] = edge
    passed[NLAT + HL : NLAT + 2 * HL] = edge
    sub = lax.broadcasted_iota(jnp.int32, (LANES, LANES), 0)
    lane = lax.broadcasted_iota(jnp.int32, (LANES, LANES), 1)

    def lon_row(r, carry):
        lhs = windows[pl.ds(r * SSTRIDE, SROWS), :].astype(jnp.bfloat16)
        spread_taps = jnp.broadcast_to(taps[pl.ds(r, 1), :], (LANES, LANES))
        ring = pltpu.roll(spread_taps, 0, 1, stride=1, stride_axis=0)
        top = jnp.where(sub >= lane, ring, 0.0).astype(jnp.bfloat16)
        bottom = jnp.where(sub <= lane, ring, 0.0).astype(jnp.bfloat16)
        left = jnp.concatenate([lhs[: 2 * WINDOWS], lhs[WINDOWS:]], axis=1)
        right = jnp.concatenate([top, bottom], axis=0)
        res = jnp.dot(left, right, preferred_element_type=jnp.float32)
        passed[r + HL] = res.astype(jnp.bfloat16).astype(jnp.float32)
        return carry

    lax.fori_loop(0, NLAT, lon_row, 0, unroll=4)

    w0, w1, w2 = lat_taps()[:3]
    laneb = lax.broadcasted_iota(jnp.int32, (WINDOWS, LANES), 1)

    def lat_band(b, carry):
        def smoothed(rr, lo, hi):
            r = b * LAT_DEV + rr
            outer = passed[r, lo:hi] + passed[r + 4, lo:hi]
            inner = passed[r + 1, lo:hi] + passed[r + 3, lo:hi]
            return w0 * outer + w1 * inner + w2 * passed[r + 2, lo:hi]

        def put(g, value):
            for m in range(MON_DEV):
                staged[pl.ds(m * GROUPS + g, N_LON, stride=VSTRIDE), :] = value[8 * m : 8 * m + 8]

        for rr in range(LAT_DEV):
            put(rr, smoothed(rr, 0, WINDOWS))
        last = smoothed(LAT_DEV - 1, WINDOWS, 2 * WINDOWS)
        for q in range(7):
            even = smoothed(2 * q, WINDOWS, 2 * WINDOWS)
            odd = smoothed(2 * q + 1, WINDOWS, 2 * WINDOWS)
            value = jnp.where(laneb < SECOND, even, pltpu.roll(odd, SECOND, 1))
            if q < 4:
                tail = pltpu.roll(last, TAIL - 16 * q, 1)
                value = jnp.where(laneb < TAIL, value, tail)
            put(LAT_DEV + q, value)
        for l in range(N_LON):
            out[l * N_LAT + b] = staged[l * VSTRIDE : l * VSTRIDE + CHUNK, :].astype(jnp.bfloat16)
        return carry

    lax.fori_loop(0, N_LAT, lat_band, 0)


def smooth(widths, field):
    return pl.pallas_call(
        smooth_kernel,
        out_shape=jax.ShapeDtypeStruct((N_LON * N_LAT, CHUNK, LANES), jnp.bfloat16),
        in_specs=[
            pl.BlockSpec(memory_space=pltpu.SMEM),
            pl.BlockSpec(memory_space=pltpu.VMEM),
        ],
        out_specs=pl.BlockSpec(memory_space=pltpu.VMEM),
        scratch_shapes=[
            pltpu.VMEM((NLAT, LANES), jnp.float32),
            pltpu.VMEM((NLAT * SSTRIDE + 8, LANES), jnp.float32),
            pltpu.VMEM((NLAT + 2 * HL, 2 * WINDOWS, LANES), jnp.float32),
            pltpu.VMEM((N_LON * VSTRIDE + 8, LANES), jnp.float32),
        ],
        compiler_params=pltpu.CompilerParams(vmem_limit_bytes=VMEM_LIMIT),
        name="smooth",
    )(widths, field)


def gram_kernel(landed, weight, packed, anomaly, wide):
    def widen(s, carry):
        wide[pl.ds(pl.multiple_of(s * CHUNK, 8), CHUNK), :] = landed[s].astype(jnp.float32)
        return carry

    lax.fori_loop(0, N_LON * N_LAT, widen, 0, unroll=4)
    lane = lax.broadcasted_iota(jnp.int32, (1, LANES), 1)
    for g in range(GROUPS):
        if g < LAT_DEV:
            scale = weight[g : g + 1, :LANES]
        else:
            q = g - LAT_DEV
            scale = weight[2 * q : 2 * q + 1, LANES:]
            scale = scale + pltpu.roll(weight[2 * q + 1 : 2 * q + 2, LANES:], SECOND, 1)
            if q < 4:
                last = weight[LAT_DEV - 1 : LAT_DEV, LANES:]
                last = jnp.where((lane >= 16 * q) & (lane < 16 * q + 16), last, 0.0)
                scale = scale + pltpu.roll(last, TAIL - 16 * q, 1)
        cells = wide[pl.ds(g, MONTHS, stride=GROUPS), :]
        mean = jnp.sum(cells, axis=0, keepdims=True) * (1.0 / MONTHS)
        anomaly[:, g * LANES : (g + 1) * LANES] = ((cells - mean) * scale).astype(jnp.bfloat16)
    half = MONTHS // 2
    for i, j in ((0, 0), (0, 1), (1, 1)):
        block = lax.dot_general(
            anomaly[i * half : (i + 1) * half, :],
            anomaly[j * half : (j + 1) * half, :],
            (((1,), (1,)), ((), ())),
            preferred_element_type=jnp.float32,
        )
        for n, (bi, bj) in enumerate(BLOCKS):
            if bi // 2 == i and bj // 2 == j:
                a, c = (bi % 2) * LANES, (bj % 2) * LANES
                packed[pl.ds(n, LANES, stride=PACK), :] = block[a : a + LANES, c : c + LANES]


def gram_terms(landed, weight):
    return pl.pallas_call(
        gram_kernel,
        out_shape=(
            jax.ShapeDtypeStruct((LANES * PACK, LANES), jnp.float32),
            jax.ShapeDtypeStruct((MONTHS, GROUPS * LANES), jnp.bfloat16),
        ),
        in_specs=[pl.BlockSpec(memory_space=pltpu.VMEM)] * 2,
        out_specs=(pl.BlockSpec(memory_space=pltpu.VMEM),) * 2,
        scratch_shapes=[pltpu.VMEM((N_LON * N_LAT * CHUNK, LANES), jnp.float32)],
        compiler_params=pltpu.CompilerParams(vmem_limit_bytes=VMEM_LIMIT),
        name="gram_terms",
    )(landed, weight)


def add_kernel(terms, out):
    step = 4 * PACK
    total = terms[0:step, :]
    for s in range(1, LANES // 4):
        total = total + terms[s * step : (s + 1) * step, :]
    row = total[0:PACK] + total[PACK : 2 * PACK] + total[2 * PACK : 3 * PACK] + total[3 * PACK :]
    total = jnp.concatenate([row] * 4, axis=0)
    for s in range(LANES // 4):
        out[s * step : (s + 1) * step, :] = total


def add_terms(terms):
    return pl.pallas_call(
        add_kernel,
        out_shape=jax.ShapeDtypeStruct(terms.shape, jnp.float32),
        in_specs=[pl.BlockSpec(memory_space=pltpu.VMEM)],
        out_specs=pl.BlockSpec(memory_space=pltpu.VMEM),
        name="add_terms",
    )(terms)


STEP = (2.25, -2.4375, 1.6875, -0.5625, 0.0625)
ROWB = 256


def root_kernel(packed, anomaly, patterns, whitener, *scratch):
    (wh, wl), (sh, sl), (hh, hl), (ph, pl_), (zh, zl) = [scratch[2 * k : 2 * k + 2] for k in range(5)]
    for n, (bi, bj) in enumerate(BLOCKS):
        block = packed[pl.ds(n, LANES, stride=PACK), :]
        whitener[bi * LANES : (bi + 1) * LANES, bj * LANES : (bj + 1) * LANES] = block
        if bi != bj:
            whitener[bj * LANES : (bj + 1) * LANES, bi * LANES : (bi + 1) * LANES] = block.T
    gram = whitener[...]
    squares = jnp.sum(gram * gram, axis=0, keepdims=True)
    frobenius = jnp.sqrt(jnp.sum(squares, axis=1, keepdims=True) + 1e-06)
    final_scale = jnp.sqrt(float(NLAT * NLON) / frobenius)

    def split(hi, lo, rows, value):
        high = value.astype(jnp.bfloat16)
        hi[rows, :] = high
        lo[rows, :] = (value - high.astype(jnp.float32)).astype(jnp.bfloat16)

    def join(hi, lo, rows):
        return hi[rows, :].astype(jnp.float32) + lo[rows, :].astype(jnp.float32)

    def product(ah, al, bh, bl, rows):
        return (
            jnp.dot(ah[rows, :], bh[...], preferred_element_type=jnp.float32)
            + jnp.dot(ah[rows, :], bl[...], preferred_element_type=jnp.float32)
            + jnp.dot(al[rows, :], bh[...], preferred_element_type=jnp.float32)
        )

    def plus_eye(value, start, scale):
        row = lax.broadcasted_iota(jnp.int32, value.shape, 0) + start
        column = lax.broadcasted_iota(jnp.int32, value.shape, 1)
        return jnp.where(row == column, value + scale, value)

    split(wh, wl, pl.ds(0, MONTHS), gram / frobenius)
    starts = [k * ROWB for k in range(MONTHS // ROWB)]
    c0, c1, c2, c3, c4 = STEP
    last = ITERS // 2 - 1

    def double_step(k, carry):
        for start in starts:
            rows = pl.ds(start, ROWB)
            square = product(wh, wl, wh, wl, rows)
            split(sh, sl, rows, square)
            split(hh, hl, rows, plus_eye(c3 * join(wh, wl, rows) + c4 * square, start, c2))
        for start in starts:
            rows = pl.ds(start, ROWB)
            value = product(sh, sl, hh, hl, rows) + c1 * join(wh, wl, rows)
            split(ph, pl_, rows, plus_eye(value, start, c0))

        @pl.when(k == 0)
        def _():
            zh[...] = ph[...]
            zl[...] = pl_[...]

        @pl.when(k > 0)
        def _():
            for start in starts:
                rows = pl.ds(start, ROWB)
                value = product(zh, zl, ph, pl_, rows)
                split(zh, zl, rows, value)
                whitener[rows, :] = value * final_scale

        @pl.when(k < last)
        def _():
            for start in starts:
                rows = pl.ds(start, ROWB)
                split(sh, sl, rows, product(wh, wl, ph, pl_, rows))
            for start in starts:
                rows = pl.ds(start, ROWB)
                split(wh, wl, rows, product(sh, sl, ph, pl_, rows))

        return carry

    lax.fori_loop(0, last + 1, double_step, 0)

    sh[...] = whitener[...].astype(jnp.bfloat16)
    for g in range(GROUPS):
        value = lax.dot_general(
            anomaly[:, g * LANES : (g + 1) * LANES],
            sh[...],
            (((0,), (1,)), ((), ())),
            preferred_element_type=jnp.float32,
        ).astype(jnp.bfloat16)
        if g < LAT_DEV:
            patterns[g, 0:LANES, :] = value
        else:
            q = g - LAT_DEV
            patterns[2 * q, LANES:, :] = value[0 : LON_DEV - LANES]
            patterns[2 * q + 1, LANES:, :] = value[SECOND : SECOND + LON_DEV - LANES]
            if q < 4:
                first = LANES + 16 * q
                size = min(16, LON_DEV - first)
                patterns[LAT_DEV - 1, first : first + size, :] = value[TAIL : TAIL + size]


def root_and_patterns(packed, anomaly):
    return pl.pallas_call(
        root_kernel,
        out_shape=(
            jax.ShapeDtypeStruct((LAT_DEV, LON_DEV, MONTHS), jnp.bfloat16),
            jax.ShapeDtypeStruct((MONTHS, MONTHS), jnp.float32),
        ),
        in_specs=[pl.BlockSpec(memory_space=pltpu.VMEM)] * 2,
        out_specs=(pl.BlockSpec(memory_space=pltpu.VMEM),) * 2,
        scratch_shapes=[pltpu.VMEM((MONTHS, MONTHS), jnp.bfloat16)] * 10,
        compiler_params=pltpu.CompilerParams(vmem_limit_bytes=VMEM_LIMIT),
        name="root_and_patterns",
    )(packed, anomaly)


def exchange(pieces):
    return lax.all_to_all(pieces, BOTH, split_axis=0, concat_axis=0, tiled=True)


def exchange_packed(packed):
    pieces = packed.reshape(N_LON * N_LAT, PACK // 2, 2, LANES)
    return exchange(pieces).reshape(packed.shape)


def local(monthly_field, half_width, land_mask):
    widths = lax.all_gather(half_width, "lat", axis=0, tiled=True)
    landed = exchange(smooth(widths, monthly_field))
    row_index = lax.axis_index("lat") * LAT_DEV + jnp.arange(LAT_DEV)
    latitude = math.pi * ((row_index.astype(jnp.float32) + 0.5) / NLAT - 0.5)
    weight = jnp.sqrt(jnp.cos(latitude))[:, None] * land_mask.astype(jnp.float32)
    weight = jnp.pad(weight, ((0, 0), (0, 2 * LANES - LON_DEV)))
    packed, anomaly = gram_terms(landed, weight)
    packed = exchange_packed(packed)
    packed = exchange_packed(add_terms(packed))
    patterns, whitener = root_and_patterns(packed, anomaly)
    return (jnp.transpose(patterns, (2, 0, 1)), whitener)


def solution(mesh):
    placed = (P(("lon", "lat"), None, None), P("lat"), P("lat", "lon"))
    return jax.shard_map(
        local, mesh=mesh, in_specs=placed, out_specs=(P(None, "lat", "lon"), P()), check_vma=False
    )
```

```python
import math

import jax
import jax.numpy as jnp
import numpy as np
from jax import lax
from jax.experimental import pallas as pl
from jax.experimental.pallas import tpu as pltpu
from jax.sharding import PartitionSpec as P

HMAX = 64
HL = 2
ITERS = 8
BOTH = ("lon", "lat")
N_LON = 8
N_LAT = 16
NLAT = 240
NLON = 1440
MONTHS = 512
MON_DEV = 4
LAT_DEV = 15
LON_DEV = 180
LANES = 128
GROUPS = 22
SECOND = 56
TAIL = 112
CHUNK = MON_DEV * GROUPS
WINDOWS = MON_DEV * N_LON
SROWS = 3 * WINDOWS
SSTRIDE = 97
VSTRIDE = 89
BLOCKS = [(i, j) for i in range(4) for j in range(i, 4)]
PACK = len(BLOCKS)
VMEM_LIMIT = 60 * 1024 * 1024


def lat_taps():
    offsets = np.arange(-HL, HL + 1).astype(np.float32)
    taps = np.exp(-(offsets * offsets) / np.float32(2.0)).astype(np.float32)
    taps = taps / taps.sum(dtype=np.float32)
    return [float(t) for t in taps.astype(jnp.bfloat16).astype(np.float32)]


def windows_kernel(field, out, staged):
    for m in range(MON_DEV):
        rows = field[m].astype(jnp.float32)
        ring = jnp.concatenate([rows, rows[:, :224]], axis=1)
        for l in range(N_LON):
            for j in range(3):
                start = LON_DEV * l - HMAX + LANES * j
                start = start + NLON if start < 0 else start
                piece = ring[:, start : start + LANES]
                for half in range(2):
                    first = half * 8 * SSTRIDE + j * WINDOWS + m * N_LON + l
                    staged[pl.ds(first, 8, stride=SSTRIDE), :] = piece[half * 8 : half * 8 + 8]
    for r in range(16):
        out[r] = staged[r * SSTRIDE : r * SSTRIDE + SROWS, :].astype(jnp.bfloat16)


def cut_windows(field):
    return pl.pallas_call(
        windows_kernel,
        grid=(NLAT // 16,),
        out_shape=jax.ShapeDtypeStruct((NLAT, SROWS, LANES), jnp.bfloat16),
        in_specs=[pl.BlockSpec((MON_DEV, 16, NLON), lambda i: (0, i, 0))],
        out_specs=pl.BlockSpec((16, SROWS, LANES), lambda i: (i, 0, 0)),
        scratch_shapes=[pltpu.VMEM((16 * SSTRIDE + 8, LANES), jnp.float32)],
        compiler_params=pltpu.CompilerParams(vmem_limit_bytes=VMEM_LIMIT),
        cost_estimate=pl.CostEstimate(flops=30000000, bytes_accessed=9000000, transcendentals=0),
        name="cut_windows",
    )(field)


def smooth_kernel(widths, windows, out, taps, passed, staged):
    b = pl.program_id(0)

    @pl.when(b == 0)
    def _():
        lane8 = lax.broadcasted_iota(jnp.int32, (8, LANES), 1)
        sub8 = lax.broadcasted_iota(jnp.int32, (8, LANES), 0)
        offset = (lane8 - HMAX).astype(jnp.float32)

        def build_taps(i, carry):
            reach = jnp.zeros((8, LANES), jnp.int32)
            for s in range(8):
                r = i * 8 + s
                reach = jnp.where(sub8 == s, widths[r // LAT_DEV, r % LAT_DEV], reach)
            reach = reach.astype(jnp.float32)
            spread = 0.5 * reach
            value = jnp.exp(-(offset * offset) / (2.0 * spread * spread))
            value = jnp.where(jnp.abs(offset) <= reach, value, 0.0)
            total = jnp.sum(value, axis=1, keepdims=True) + value[:, 0:1]
            value = (value / total).astype(jnp.bfloat16).astype(jnp.float32)
            taps[pl.ds(pl.multiple_of(i * 8, 8), 8), :] = value
            return carry

        lax.fori_loop(0, NLAT // 8, build_taps, 0, unroll=10)
        edge = jnp.zeros((HL, 2 * WINDOWS, LANES), jnp.float32)
        passed[0:HL] = edge
        passed[NLAT + HL : NLAT + 2 * HL] = edge

    @pl.when(b < N_LAT)
    def _():
        sub = lax.broadcasted_iota(jnp.int32, (LANES, LANES), 0)
        lane = lax.broadcasted_iota(jnp.int32, (LANES, LANES), 1)
        upper = jnp.where(sub >= lane, 1.0, 0.0).astype(jnp.bfloat16)
        lower = jnp.where(sub <= lane, 1.0, 0.0).astype(jnp.bfloat16)
        for rr in range(LAT_DEV):
            r = b * LAT_DEV + rr
            lhs = windows[rr]
            spread_taps = jnp.broadcast_to(taps[pl.ds(r, 1), :], (LANES, LANES))
            ring = pltpu.roll(spread_taps, 0, 1, stride=1, stride_axis=0).astype(jnp.bfloat16)
            left = jnp.concatenate([lhs[: 2 * WINDOWS], lhs[WINDOWS:]], axis=1)
            right = jnp.concatenate([ring * upper, ring * lower], axis=0)
            res = jnp.dot(left, right, preferred_element_type=jnp.float32)
            passed[r + HL] = res.astype(jnp.bfloat16).astype(jnp.float32)

    @pl.when(b > 0)
    def _():
        w0, w1, w2 = lat_taps()[:3]
        laneb = lax.broadcasted_iota(jnp.int32, (WINDOWS, LANES), 1)

        def smoothed(rr, lo, hi):
            r = (b - 1) * LAT_DEV + rr
            outer = passed[r, lo:hi] + passed[r + 4, lo:hi]
            inner = passed[r + 1, lo:hi] + passed[r + 3, lo:hi]
            return w0 * outer + w1 * inner + w2 * passed[r + 2, lo:hi]

        def put(g, value):
            for m in range(MON_DEV):
                staged[pl.ds(m * GROUPS + g, N_LON, stride=VSTRIDE), :] = value[8 * m : 8 * m + 8]

        for rr in range(LAT_DEV):
            put(rr, smoothed(rr, 0, WINDOWS))
        last = smoothed(LAT_DEV - 1, WINDOWS, 2 * WINDOWS)
        for q in range(7):
            even = smoothed(2 * q, WINDOWS, 2 * WINDOWS)
            odd = smoothed(2 * q + 1, WINDOWS, 2 * WINDOWS)
            value = jnp.where(laneb < SECOND, even, pltpu.roll(odd, SECOND, 1))
            if q < 4:
                tail = pltpu.roll(last, TAIL - 16 * q, 1)
                value = jnp.where(laneb < TAIL, value, tail)
            put(LAT_DEV + q, value)
        for l in range(N_LON):
            out[l, 0] = staged[l * VSTRIDE : l * VSTRIDE + CHUNK, :].astype(jnp.bfloat16)


def smooth(widths, windows):
    out = pl.pallas_call(
        smooth_kernel,
        grid=(N_LAT + 1,),
        out_shape=jax.ShapeDtypeStruct((N_LON, N_LAT, CHUNK, LANES), jnp.bfloat16),
        in_specs=[
            pl.BlockSpec(memory_space=pltpu.SMEM),
            pl.BlockSpec((LAT_DEV, SROWS, LANES), lambda b: (jnp.minimum(b, N_LAT - 1), 0, 0)),
        ],
        out_specs=pl.BlockSpec((N_LON, 1, CHUNK, LANES), lambda b: (0, jnp.maximum(b - 1, 0), 0, 0)),
        scratch_shapes=[
            pltpu.VMEM((NLAT, LANES), jnp.float32),
            pltpu.VMEM((NLAT + 2 * HL, 2 * WINDOWS, LANES), jnp.float32),
            pltpu.VMEM((N_LON * VSTRIDE + 8, LANES), jnp.float32),
        ],
        compiler_params=pltpu.CompilerParams(vmem_limit_bytes=VMEM_LIMIT),
        name="smooth",
    )(widths, windows)
    return out.reshape(N_LON * N_LAT, CHUNK, LANES)


def gram_kernel(landed_hbm, weight, packed, anomaly_hbm, landed, wide, anomaly, in_sems, out_sem):
    parts = 4
    size = N_LON * N_LAT // parts
    copies = [
        pltpu.make_async_copy(
            landed_hbm.at[k * size : (k + 1) * size], landed.at[k * size : (k + 1) * size], in_sems.at[k]
        )
        for k in range(parts)
    ]
    for copy in copies:
        copy.start()

    def widen(s, carry):
        wide[pl.ds(pl.multiple_of(s * CHUNK, 8), CHUNK), :] = landed[s].astype(jnp.float32)
        return carry

    for k in range(parts):
        copies[k].wait()
        lax.fori_loop(k * size, (k + 1) * size, widen, 0, unroll=4)
    lane = lax.broadcasted_iota(jnp.int32, (1, LANES), 1)
    for g in range(GROUPS):
        if g < LAT_DEV:
            scale = weight[g : g + 1, :LANES]
        else:
            q = g - LAT_DEV
            scale = weight[2 * q : 2 * q + 1, LANES:]
            scale = scale + pltpu.roll(weight[2 * q + 1 : 2 * q + 2, LANES:], SECOND, 1)
            if q < 4:
                last = weight[LAT_DEV - 1 : LAT_DEV, LANES:]
                last = jnp.where((lane >= 16 * q) & (lane < 16 * q + 16), last, 0.0)
                scale = scale + pltpu.roll(last, TAIL - 16 * q, 1)
        cells = wide[pl.ds(g, MONTHS, stride=GROUPS), :]
        mean = jnp.sum(cells, axis=0, keepdims=True) * (1.0 / MONTHS)
        anomaly[:, g * LANES : (g + 1) * LANES] = ((cells - mean) * scale).astype(jnp.bfloat16)
    store = pltpu.make_async_copy(anomaly, anomaly_hbm, out_sem)
    store.start()
    half = MONTHS // 2
    for i, j in ((0, 0), (0, 1), (1, 1)):
        block = lax.dot_general(
            anomaly[i * half : (i + 1) * half, :],
            anomaly[j * half : (j + 1) * half, :],
            (((1,), (1,)), ((), ())),
            preferred_element_type=jnp.float32,
        )
        for n, (bi, bj) in enumerate(BLOCKS):
            if bi // 2 == i and bj // 2 == j:
                a, c = (bi % 2) * LANES, (bj % 2) * LANES
                packed[pl.ds(n, LANES, stride=PACK), :] = block[a : a + LANES, c : c + LANES]
    store.wait()


def gram_terms(landed, weight):
    return pl.pallas_call(
        gram_kernel,
        out_shape=(
            jax.ShapeDtypeStruct((LANES * PACK, LANES), jnp.float32),
            jax.ShapeDtypeStruct((MONTHS, GROUPS * LANES), jnp.bfloat16),
        ),
        in_specs=[pl.BlockSpec(memory_space=pl.ANY), pl.BlockSpec(memory_space=pltpu.VMEM)],
        out_specs=(pl.BlockSpec(memory_space=pltpu.VMEM), pl.BlockSpec(memory_space=pl.ANY)),
        scratch_shapes=[
            pltpu.VMEM((N_LON * N_LAT, CHUNK, LANES), jnp.bfloat16),
            pltpu.VMEM((N_LON * N_LAT * CHUNK, LANES), jnp.float32),
            pltpu.VMEM((MONTHS, GROUPS * LANES), jnp.bfloat16),
            pltpu.SemaphoreType.DMA((4,)),
            pltpu.SemaphoreType.DMA,
        ],
        compiler_params=pltpu.CompilerParams(vmem_limit_bytes=32 * 1024 * 1024),
        name="gram_terms",
    )(landed, weight)


def add_kernel(terms, out):
    step = 4 * PACK
    total = terms[0:step, :]
    for s in range(1, LANES // 4):
        total = total + terms[s * step : (s + 1) * step, :]
    row = total[0:PACK] + total[PACK : 2 * PACK] + total[2 * PACK : 3 * PACK] + total[3 * PACK :]
    total = jnp.concatenate([row] * 4, axis=0)
    for s in range(LANES // 4):
        out[s * step : (s + 1) * step, :] = total


def add_terms(terms):
    return pl.pallas_call(
        add_kernel,
        out_shape=jax.ShapeDtypeStruct(terms.shape, jnp.float32),
        in_specs=[pl.BlockSpec(memory_space=pltpu.VMEM)],
        out_specs=pl.BlockSpec(memory_space=pltpu.VMEM),
        compiler_params=pltpu.CompilerParams(vmem_limit_bytes=8 * 1024 * 1024),
        name="add_terms",
    )(terms)


STEP = (2.25, -2.4375, 1.6875, -0.5625, 0.0625)
ROWB = 256
MIRROR = True


def root_kernel(packed, anomaly_hbm, patterns_hbm, whitener_hbm, anomaly, patterns, whitener, ws, hs, ps, ss, zs, wb, in_sem, out_sems):
    fetch = pltpu.make_async_copy(anomaly_hbm, anomaly, in_sem)
    fetch.start()
    for n, (bi, bj) in enumerate(BLOCKS):
        block = packed[pl.ds(n, LANES, stride=PACK), :]
        whitener[bi * LANES : (bi + 1) * LANES, bj * LANES : (bj + 1) * LANES] = block
        if bi != bj:
            whitener[bj * LANES : (bj + 1) * LANES, bi * LANES : (bi + 1) * LANES] = block.T
    gram = whitener[...]
    squares = jnp.sum(gram * gram, axis=0, keepdims=True)
    frobenius = jnp.sqrt(jnp.sum(squares, axis=1, keepdims=True) + 1e-06)
    final_scale = jnp.sqrt(float(NLAT * NLON) / frobenius)

    def split(ref, start, value):
        size = value.shape[0]
        high = value.astype(jnp.bfloat16)
        ref[start : start + size, :] = high
        ref[MONTHS + start : MONTHS + start + size, :] = (value - high.astype(jnp.float32)).astype(jnp.bfloat16)
        if ref.shape[0] == 3 * MONTHS:
            ref[2 * MONTHS + start : 2 * MONTHS + start + size, :] = high

    def join(ref, start):
        high = ref[start : start + ROWB, :].astype(jnp.float32)
        return high + ref[MONTHS + start : MONTHS + start + ROWB, :].astype(jnp.float32)

    def product(left, right):
        def rows(start):
            high = left[start : start + ROWB, :]
            low = left[MONTHS + start : MONTHS + start + ROWB, :]
            return jnp.concatenate([high, high, low], axis=1)

        upper = jnp.dot(rows(0), right[...], preferred_element_type=jnp.float32)
        if not MIRROR:
            return upper, jnp.dot(rows(ROWB), right[...], preferred_element_type=jnp.float32)
        corner = jnp.dot(rows(ROWB), right[:, ROWB:], preferred_element_type=jnp.float32)
        return upper, jnp.concatenate([upper[:, ROWB:].T, corner], axis=1)

    def plus_eye(value, start, scale):
        row = lax.broadcasted_iota(jnp.int32, value.shape, 0) + start
        column = lax.broadcasted_iota(jnp.int32, value.shape, 1)
        return jnp.where(row == column, value + scale, value)

    split(ws, 0, gram / frobenius)
    c0, c1, c2, c3, c4 = STEP
    last = ITERS // 2 - 1

    def double_step(k, carry):
        for n, square in enumerate(product(ws, ws)):
            start = n * ROWB
            split(ss, start, square)
            split(hs, start, plus_eye(c3 * join(ws, start) + c4 * square, start, c2))
        for n, value in enumerate(product(ss, hs)):
            start = n * ROWB
            split(ps, start, plus_eye(value + c1 * join(ws, start), start, c0))

        @pl.when(k == 0)
        def _():
            zs[...] = ps[0 : 2 * MONTHS, :]

        @pl.when(k > 0)
        def _():
            for n, value in enumerate(product(zs, ps)):
                split(zs, n * ROWB, value)
                whitener[n * ROWB : (n + 1) * ROWB, :] = value * final_scale

        @pl.when(k < last)
        def _():
            for n, value in enumerate(product(ws, ps)):
                split(ss, n * ROWB, value)
            for n, value in enumerate(product(ss, ps)):
                split(ws, n * ROWB, value)

        return carry

    lax.fori_loop(0, last + 1, double_step, 0)
    copies = [pltpu.make_async_copy(whitener, whitener_hbm, out_sems.at[LAT_DEV])]
    copies[0].start()
    wb[...] = whitener[...].astype(jnp.bfloat16)
    fetch.wait()

    def group(g):
        return lax.dot_general(
            anomaly[:, g * LANES : (g + 1) * LANES],
            wb[...],
            (((0,), (1,)), ((), ())),
            preferred_element_type=jnp.float32,
        ).astype(jnp.bfloat16)

    def finish(r):
        copy = pltpu.make_async_copy(patterns.at[r], patterns_hbm.at[r], out_sems.at[r])
        copy.start()
        copies.append(copy)

    for q in range(7):
        value = group(LAT_DEV + q)
        patterns[2 * q, LANES:, :] = value[0 : LON_DEV - LANES]
        patterns[2 * q + 1, LANES:, :] = value[SECOND : SECOND + LON_DEV - LANES]
        if q < 4:
            first = LANES + 16 * q
            size = min(16, LON_DEV - first)
            patterns[LAT_DEV - 1, first : first + size, :] = value[TAIL : TAIL + size]
        for r in (2 * q, 2 * q + 1):
            patterns[r, 0:LANES, :] = group(r)
            finish(r)
    patterns[LAT_DEV - 1, 0:LANES, :] = group(LAT_DEV - 1)
    finish(LAT_DEV - 1)
    for copy in copies:
        copy.wait()


def root_and_patterns(packed, anomaly):
    return pl.pallas_call(
        root_kernel,
        out_shape=(
            jax.ShapeDtypeStruct((LAT_DEV, LON_DEV, MONTHS), jnp.bfloat16),
            jax.ShapeDtypeStruct((MONTHS, MONTHS), jnp.float32),
        ),
        in_specs=[pl.BlockSpec(memory_space=pltpu.VMEM), pl.BlockSpec(memory_space=pl.ANY)],
        out_specs=(pl.BlockSpec(memory_space=pl.ANY),) * 2,
        scratch_shapes=[
            pltpu.VMEM((MONTHS, GROUPS * LANES), jnp.bfloat16),
            pltpu.VMEM((LAT_DEV, LON_DEV, MONTHS), jnp.bfloat16),
            pltpu.VMEM((MONTHS, MONTHS), jnp.float32),
            pltpu.VMEM((3 * MONTHS, MONTHS), jnp.bfloat16),
            pltpu.VMEM((3 * MONTHS, MONTHS), jnp.bfloat16),
            pltpu.VMEM((3 * MONTHS, MONTHS), jnp.bfloat16),
            pltpu.VMEM((2 * MONTHS, MONTHS), jnp.bfloat16),
            pltpu.VMEM((2 * MONTHS, MONTHS), jnp.bfloat16),
            pltpu.VMEM((MONTHS, MONTHS), jnp.bfloat16),
            pltpu.SemaphoreType.DMA,
            pltpu.SemaphoreType.DMA((LAT_DEV + 1,)),
        ],
        compiler_params=pltpu.CompilerParams(vmem_limit_bytes=32 * 1024 * 1024),
        name="root_and_patterns",
    )(packed, anomaly)


def exchange(pieces):
    return lax.all_to_all(pieces, BOTH, split_axis=0, concat_axis=0, tiled=True)


def exchange_packed(packed):
    pieces = packed.reshape(N_LON * N_LAT, PACK // 2, 2, LANES)
    return exchange(pieces).reshape(packed.shape)


def local(monthly_field, half_width, land_mask):
    widths = jnp.pad(half_width, (0, LANES - LAT_DEV))
    widths = jnp.broadcast_to(widths, (N_LAT, 1, LANES))
    widths = lax.all_to_all(widths, "lat", split_axis=0, concat_axis=0, tiled=True)
    windows = cut_windows(monthly_field)
    landed = exchange(smooth(widths.reshape(N_LAT, LANES), windows))
    row_index = lax.axis_index("lat") * LAT_DEV + jnp.arange(LAT_DEV)
    latitude = math.pi * ((row_index.astype(jnp.float32) + 0.5) / NLAT - 0.5)
    weight = jnp.sqrt(jnp.cos(latitude))[:, None] * land_mask.astype(jnp.float32)
    weight = jnp.pad(weight, ((0, 0), (0, 2 * LANES - LON_DEV)))
    packed, anomaly = gram_terms(landed, weight)
    packed = exchange_packed(packed)
    packed = exchange_packed(add_terms(packed))
    patterns, whitener = root_and_patterns(packed, anomaly)
    return (jnp.transpose(patterns, (2, 0, 1)), whitener)


def solution(mesh):
    placed = (P(("lon", "lat"), None, None), P("lat"), P("lat", "lon"))
    return jax.shard_map(
        local, mesh=mesh, in_specs=placed, out_specs=(P(None, "lat", "lon"), P()), check_vma=False
    )
```

```python
import functools
import math

import jax
import jax.numpy as jnp
import numpy as np
from jax import lax
from jax.experimental import pallas as pl
from jax.experimental.pallas import tpu as pltpu
from jax.sharding import PartitionSpec as P

HMAX = 64
HL = 2
ITERS = 8
BOTH = ("lon", "lat")
N_LON = 8
N_LAT = 16
NLAT = 240
NLON = 1440
MONTHS = 512
MON_DEV = 4
LAT_DEV = 15
LON_DEV = 180
LANES = 128
GROUPS = 22
SECOND = 56
TAIL = 112
CHUNK = MON_DEV * GROUPS
WINDOWS = MON_DEV * N_LON
SROWS = 3 * WINDOWS
SSTRIDE = 97
VSTRIDE = 89
FRONT = 8
BLOCKS = [(i, j) for i in range(4) for j in range(i, 4)]
PACK = len(BLOCKS)
VMEM_LIMIT = 60 * 1024 * 1024


def lat_taps():
    offsets = np.arange(-HL, HL + 1).astype(np.float32)
    taps = np.exp(-(offsets * offsets) / np.float32(2.0)).astype(np.float32)
    taps = taps / taps.sum(dtype=np.float32)
    return [float(t) for t in taps.astype(jnp.bfloat16).astype(np.float32)]


def windows_kernel(first_step, field_hbm, out_hbm, field, windows, staged, in_sems, out_sems):
    steps = windows.shape[0] // 16

    def fetch(i):
        rows = pl.ds(pl.multiple_of(i * 16, 16), 16)
        source = pl.ds(pl.multiple_of((first_step + i) * 16, 16), 16)
        return pltpu.make_async_copy(field_hbm.at[:, source, :], field.at[:, rows, :], in_sems.at[i])

    def store(i):
        rows = pl.ds(pl.multiple_of(i * 16, 16), 16)
        return pltpu.make_async_copy(windows.at[rows], out_hbm.at[rows], out_sems.at[i])

    for i in range(steps):
        fetch(i).start()

    def step(i, carry):
        fetch(i).wait()
        for m in range(MON_DEV):
            rows = field[m, pl.ds(pl.multiple_of(i * 16, 16), 16), :].astype(jnp.float32)
            ring = jnp.concatenate([rows, rows[:, :224]], axis=1)
            for l in range(N_LON):
                for j in range(3):
                    start = LON_DEV * l - HMAX + LANES * j
                    start = start + NLON if start < 0 else start
                    piece = ring[:, start : start + LANES]
                    for half in range(2):
                        first = half * 8 * SSTRIDE + j * WINDOWS + m * N_LON + l
                        staged[pl.ds(first, 8, stride=SSTRIDE), :] = piece[half * 8 : half * 8 + 8]
        for r in range(16):
            windows[i * 16 + r] = staged[r * SSTRIDE : r * SSTRIDE + SROWS, :].astype(jnp.bfloat16)
        store(i).start()
        return carry

    lax.fori_loop(0, steps, step, 0)
    for i in range(steps):
        store(i).wait()


def cut_windows(field, first_step, steps):
    return pl.pallas_call(
        functools.partial(windows_kernel, first_step),
        out_shape=jax.ShapeDtypeStruct((steps * 16, SROWS, LANES), jnp.bfloat16),
        in_specs=[pl.BlockSpec(memory_space=pl.ANY)],
        out_specs=pl.BlockSpec(memory_space=pl.ANY),
        scratch_shapes=[
            pltpu.VMEM((MON_DEV, steps * 16, NLON), jnp.bfloat16),
            pltpu.VMEM((steps * 16, SROWS, LANES), jnp.bfloat16),
            pltpu.VMEM((16 * SSTRIDE + 8, LANES), jnp.float32),
            pltpu.SemaphoreType.DMA((steps,)),
            pltpu.SemaphoreType.DMA((steps,)),
        ],
        compiler_params=pltpu.CompilerParams(vmem_limit_bytes=VMEM_LIMIT),
        cost_estimate=pl.CostEstimate(flops=3000000000, bytes_accessed=9000000, transcendentals=0),
        name="cut_windows",
    )(field)


def smooth_kernel(chip, *refs):
    quads, refs = refs[:4], refs[4:]
    (front, back, out_hbm, windows, out, taps, passed, staged, widths, in_sems, out_sems) = refs

    def fetch(i):
        rows = pl.ds(i * 16, 16)
        if i < FRONT:
            return pltpu.make_async_copy(front.at[rows], windows.at[rows], in_sems.at[i])
        return pltpu.make_async_copy(back.at[pl.ds((i - FRONT) * 16, 16)], windows.at[rows], in_sems.at[i])

    def arrived(i):
        rows = pl.ds(pl.multiple_of(i * 16, 16), 16)
        pltpu.make_async_copy(windows.at[rows], windows.at[rows], in_sems.at[i]).wait()

    def store(b):
        return pltpu.make_async_copy(out.at[:, b], out_hbm.at[:, b], out_sems.at[b])

    for i in range(NLAT // 16):
        fetch(i).start()
    for k in range(4):
        for j in range(4):
            first = ((k ^ chip[0]) * 4 + j) * LAT_DEV
            for rr in range(LAT_DEV):
                widths[first + rr] = quads[k][j, rr]
    lane8 = lax.broadcasted_iota(jnp.int32, (8, LANES), 1)
    sub8 = lax.broadcasted_iota(jnp.int32, (8, LANES), 0)
    offset = (lane8 - HMAX).astype(jnp.float32)

    def build_taps(i, carry):
        reach = jnp.zeros((8, LANES), jnp.int32)
        for s in range(8):
            r = i * 8 + s
            reach = jnp.where(sub8 == s, widths[r], reach)
        reach = reach.astype(jnp.float32)
        spread = 0.5 * reach
        value = jnp.exp(-(offset * offset) / (2.0 * spread * spread))
        value = jnp.where(jnp.abs(offset) <= reach, value, 0.0)
        total = jnp.sum(value, axis=1, keepdims=True) + value[:, 0:1]
        value = (value / total).astype(jnp.bfloat16).astype(jnp.float32)
        taps[pl.ds(pl.multiple_of(i * 8, 8), 8), :] = value
        return carry

    lax.fori_loop(0, NLAT // 8, build_taps, 0, unroll=10)
    edge = jnp.zeros((HL, 2 * WINDOWS, LANES), jnp.float32)
    passed[0:HL] = edge
    passed[NLAT + HL : NLAT + 2 * HL] = edge
    sub = lax.broadcasted_iota(jnp.int32, (LANES, LANES), 0)
    lane = lax.broadcasted_iota(jnp.int32, (LANES, LANES), 1)
    upper = jnp.where(sub >= lane, 1.0, 0.0).astype(jnp.bfloat16)
    lower = jnp.where(sub <= lane, 1.0, 0.0).astype(jnp.bfloat16)

    def lon_band(b):
        for rr in range(LAT_DEV):
            r = b * LAT_DEV + rr
            lhs = windows[r]
            spread_taps = jnp.broadcast_to(taps[pl.ds(r, 1), :], (LANES, LANES))
            ring = pltpu.roll(spread_taps, 0, 1, stride=1, stride_axis=0).astype(jnp.bfloat16)
            left = jnp.concatenate([lhs[: 2 * WINDOWS], lhs[WINDOWS:]], axis=1)
            right = jnp.concatenate([ring * upper, ring * lower], axis=0)
            res = jnp.dot(left, right, preferred_element_type=jnp.float32)
            passed[r + HL] = res.astype(jnp.bfloat16).astype(jnp.float32)

    w0, w1, w2 = lat_taps()[:3]
    laneb = lax.broadcasted_iota(jnp.int32, (WINDOWS, LANES), 1)

    def lat_band(b):
        def smoothed(rr, lo, hi):
            r = b * LAT_DEV + rr
            outer = passed[r, lo:hi] + passed[r + 4, lo:hi]
            inner = passed[r + 1, lo:hi] + passed[r + 3, lo:hi]
            return w0 * outer + w1 * inner + w2 * passed[r + 2, lo:hi]

        def put(g, value):
            for m in range(MON_DEV):
                staged[pl.ds(m * GROUPS + g, N_LON, stride=VSTRIDE), :] = value[8 * m : 8 * m + 8]

        for rr in range(LAT_DEV):
            put(rr, smoothed(rr, 0, WINDOWS))
        last = smoothed(LAT_DEV - 1, WINDOWS, 2 * WINDOWS)
        for q in range(7):
            even = smoothed(2 * q, WINDOWS, 2 * WINDOWS)
            odd = smoothed(2 * q + 1, WINDOWS, 2 * WINDOWS)
            value = jnp.where(laneb < SECOND, even, pltpu.roll(odd, SECOND, 1))
            if q < 4:
                tail = pltpu.roll(last, TAIL - 16 * q, 1)
                value = jnp.where(laneb < TAIL, value, tail)
            put(LAT_DEV + q, value)
        for l in range(N_LON):
            out[l, b] = staged[l * VSTRIDE : l * VSTRIDE + CHUNK, :].astype(jnp.bfloat16)

    arrived(0)
    lon_band(0)

    def band(b, carry):
        arrived(b)
        lon_band(b)
        lat_band(b - 1)
        store(b - 1).start()
        return carry

    lax.fori_loop(1, N_LAT - 1, band, 0)
    lon_band(N_LAT - 1)
    for b in (N_LAT - 2, N_LAT - 1):
        lat_band(b)
        store(b).start()
    for b in range(N_LAT):
        store(b).wait()


def smooth(chip, quads, front, back):
    out = pl.pallas_call(
        smooth_kernel,
        out_shape=jax.ShapeDtypeStruct((N_LON, N_LAT, CHUNK, LANES), jnp.bfloat16),
        in_specs=[pl.BlockSpec(memory_space=pltpu.SMEM)] * 5 + [pl.BlockSpec(memory_space=pl.ANY)] * 2,
        out_specs=pl.BlockSpec(memory_space=pl.ANY),
        scratch_shapes=[
            pltpu.VMEM((NLAT, SROWS, LANES), jnp.bfloat16),
            pltpu.VMEM((N_LON, N_LAT, CHUNK, LANES), jnp.bfloat16),
            pltpu.VMEM((NLAT, LANES), jnp.float32),
            pltpu.VMEM((NLAT + 2 * HL, 2 * WINDOWS, LANES), jnp.float32),
            pltpu.VMEM((N_LON * VSTRIDE + 8, LANES), jnp.float32),
            pltpu.SMEM((NLAT,), jnp.int32),
            pltpu.SemaphoreType.DMA((NLAT // 16,)),
            pltpu.SemaphoreType.DMA((N_LAT,)),
        ],
        compiler_params=pltpu.CompilerParams(vmem_limit_bytes=VMEM_LIMIT),
        name="smooth",
    )(chip, *quads, front, back)
    return out.reshape(N_LON * N_LAT, CHUNK, LANES)


def gram_kernel(landed_hbm, weight, packed, anomaly_hbm, landed, wide, anomaly, in_sems, out_sem):
    parts = 4
    size = N_LON * N_LAT // parts
    copies = [
        pltpu.make_async_copy(
            landed_hbm.at[k * size : (k + 1) * size], landed.at[k * size : (k + 1) * size], in_sems.at[k]
        )
        for k in range(parts)
    ]
    for copy in copies:
        copy.start()

    def widen(s, carry):
        wide[pl.ds(pl.multiple_of(s * CHUNK, 8), CHUNK), :] = landed[s].astype(jnp.float32)
        return carry

    for k in range(parts):
        copies[k].wait()
        lax.fori_loop(k * size, (k + 1) * size, widen, 0, unroll=4)
    lane = lax.broadcasted_iota(jnp.int32, (1, LANES), 1)
    for g in range(GROUPS):
        if g < LAT_DEV:
            scale = weight[g : g + 1, :LANES]
        else:
            q = g - LAT_DEV
            scale = weight[2 * q : 2 * q + 1, LANES:]
            scale = scale + pltpu.roll(weight[2 * q + 1 : 2 * q + 2, LANES:], SECOND, 1)
            if q < 4:
                last = weight[LAT_DEV - 1 : LAT_DEV, LANES:]
                last = jnp.where((lane >= 16 * q) & (lane < 16 * q + 16), last, 0.0)
                scale = scale + pltpu.roll(last, TAIL - 16 * q, 1)
        cells = wide[pl.ds(g, MONTHS, stride=GROUPS), :]
        mean = jnp.sum(cells, axis=0, keepdims=True) * (1.0 / MONTHS)
        anomaly[:, g * LANES : (g + 1) * LANES] = ((cells - mean) * scale).astype(jnp.bfloat16)
    store = pltpu.make_async_copy(anomaly, anomaly_hbm, out_sem)
    store.start()
    half = MONTHS // 2
    for i, j in ((0, 0), (0, 1), (1, 1)):
        block = lax.dot_general(
            anomaly[i * half : (i + 1) * half, :],
            anomaly[j * half : (j + 1) * half, :],
            (((1,), (1,)), ((), ())),
            preferred_element_type=jnp.float32,
        )
        for n, (bi, bj) in enumerate(BLOCKS):
            if bi // 2 == i and bj // 2 == j:
                a, c = (bi % 2) * LANES, (bj % 2) * LANES
                packed[pl.ds(n, LANES, stride=PACK), :] = block[a : a + LANES, c : c + LANES]
    store.wait()


def gram_terms(landed, weight):
    return pl.pallas_call(
        gram_kernel,
        out_shape=(
            jax.ShapeDtypeStruct((LANES * PACK, LANES), jnp.float32),
            jax.ShapeDtypeStruct((MONTHS, GROUPS * LANES), jnp.bfloat16),
        ),
        in_specs=[pl.BlockSpec(memory_space=pl.ANY), pl.BlockSpec(memory_space=pltpu.VMEM)],
        out_specs=(pl.BlockSpec(memory_space=pltpu.VMEM), pl.BlockSpec(memory_space=pl.ANY)),
        scratch_shapes=[
            pltpu.VMEM((N_LON * N_LAT, CHUNK, LANES), jnp.bfloat16),
            pltpu.VMEM((N_LON * N_LAT * CHUNK, LANES), jnp.float32),
            pltpu.VMEM((MONTHS, GROUPS * LANES), jnp.bfloat16),
            pltpu.SemaphoreType.DMA((4,)),
            pltpu.SemaphoreType.DMA,
        ],
        compiler_params=pltpu.CompilerParams(vmem_limit_bytes=32 * 1024 * 1024),
        name="gram_terms",
    )(landed, weight)


def add_kernel(terms, out):
    step = 4 * PACK
    total = terms[0:step, :]
    for s in range(1, LANES // 4):
        total = total + terms[s * step : (s + 1) * step, :]
    row = total[0:PACK] + total[PACK : 2 * PACK] + total[2 * PACK : 3 * PACK] + total[3 * PACK :]
    total = jnp.concatenate([row] * 4, axis=0)
    for s in range(LANES // 4):
        out[s * step : (s + 1) * step, :] = total


def add_terms(terms):
    return pl.pallas_call(
        add_kernel,
        out_shape=jax.ShapeDtypeStruct(terms.shape, jnp.float32),
        in_specs=[pl.BlockSpec(memory_space=pltpu.VMEM)],
        out_specs=pl.BlockSpec(memory_space=pltpu.VMEM),
        compiler_params=pltpu.CompilerParams(vmem_limit_bytes=8 * 1024 * 1024),
        name="add_terms",
    )(terms)


STEP = (2.25, -2.4375, 1.6875, -0.5625, 0.0625)
ROWB = 256
MIRROR = True


def root_kernel(packed, anomaly_hbm, patterns_hbm, whitener_hbm, anomaly, patterns, whitener, ws, hs, ps, ss, zs, wb, in_sem, out_sems):
    fetch = pltpu.make_async_copy(anomaly_hbm, anomaly, in_sem)
    fetch.start()
    for n, (bi, bj) in enumerate(BLOCKS):
        block = packed[pl.ds(n, LANES, stride=PACK), :]
        whitener[bi * LANES : (bi + 1) * LANES, bj * LANES : (bj + 1) * LANES] = block
        if bi != bj:
            whitener[bj * LANES : (bj + 1) * LANES, bi * LANES : (bi + 1) * LANES] = block.T
    gram = whitener[...]
    squares = jnp.sum(gram * gram, axis=0, keepdims=True)
    frobenius = jnp.sqrt(jnp.sum(squares, axis=1, keepdims=True) + 1e-06)
    final_scale = jnp.sqrt(float(NLAT * NLON) / frobenius)

    def split(ref, start, value):
        size = value.shape[0]
        high = value.astype(jnp.bfloat16)
        ref[start : start + size, :] = high
        ref[MONTHS + start : MONTHS + start + size, :] = (value - high.astype(jnp.float32)).astype(jnp.bfloat16)
        if ref.shape[0] == 3 * MONTHS:
            ref[2 * MONTHS + start : 2 * MONTHS + start + size, :] = high

    def join(ref, start):
        high = ref[start : start + ROWB, :].astype(jnp.float32)
        return high + ref[MONTHS + start : MONTHS + start + ROWB, :].astype(jnp.float32)

    def product(left, right):
        def rows(start):
            high = left[start : start + ROWB, :]
            low = left[MONTHS + start : MONTHS + start + ROWB, :]
            return jnp.concatenate([high, high, low], axis=1)

        upper = jnp.dot(rows(0), right[...], preferred_element_type=jnp.float32)
        if not MIRROR:
            return upper, jnp.dot(rows(ROWB), right[...], preferred_element_type=jnp.float32)
        corner = jnp.dot(rows(ROWB), right[:, ROWB:], preferred_element_type=jnp.float32)
        return upper, jnp.concatenate([upper[:, ROWB:].T, corner], axis=1)

    def plus_eye(value, start, scale):
        row = lax.broadcasted_iota(jnp.int32, value.shape, 0) + start
        column = lax.broadcasted_iota(jnp.int32, value.shape, 1)
        return jnp.where(row == column, value + scale, value)

    split(ws, 0, gram / frobenius)
    c0, c1, c2, c3, c4 = STEP
    last = ITERS // 2 - 1

    def double_step(k, carry):
        for n, square in enumerate(product(ws, ws)):
            start = n * ROWB
            split(ss, start, square)
            split(hs, start, plus_eye(c3 * join(ws, start) + c4 * square, start, c2))
        for n, value in enumerate(product(ss, hs)):
            start = n * ROWB
            split(ps, start, plus_eye(value + c1 * join(ws, start), start, c0))

        @pl.when(k == 0)
        def _():
            zs[...] = ps[0 : 2 * MONTHS, :]

        @pl.when(k > 0)
        def _():
            for n, value in enumerate(product(zs, ps)):
                split(zs, n * ROWB, value)
                whitener[n * ROWB : (n + 1) * ROWB, :] = value * final_scale

        @pl.when(k < last)
        def _():
            for n, value in enumerate(product(ws, ps)):
                split(ss, n * ROWB, value)
            for n, value in enumerate(product(ss, ps)):
                split(ws, n * ROWB, value)

        return carry

    lax.fori_loop(0, last + 1, double_step, 0)
    copies = [pltpu.make_async_copy(whitener, whitener_hbm, out_sems.at[LAT_DEV])]
    copies[0].start()
    wb[...] = whitener[...].astype(jnp.bfloat16)
    fetch.wait()

    def group(g):
        return lax.dot_general(
            anomaly[:, g * LANES : (g + 1) * LANES],
            wb[...],
            (((0,), (1,)), ((), ())),
            preferred_element_type=jnp.float32,
        ).astype(jnp.bfloat16)

    def finish(r):
        copy = pltpu.make_async_copy(patterns.at[r], patterns_hbm.at[r], out_sems.at[r])
        copy.start()
        copies.append(copy)

    for q in range(7):
        value = group(LAT_DEV + q)
        patterns[2 * q, LANES:, :] = value[0 : LON_DEV - LANES]
        patterns[2 * q + 1, LANES:, :] = value[SECOND : SECOND + LON_DEV - LANES]
        if q < 4:
            first = LANES + 16 * q
            size = min(16, LON_DEV - first)
            patterns[LAT_DEV - 1, first : first + size, :] = value[TAIL : TAIL + size]
        for r in (2 * q, 2 * q + 1):
            patterns[r, 0:LANES, :] = group(r)
            finish(r)
    patterns[LAT_DEV - 1, 0:LANES, :] = group(LAT_DEV - 1)
    finish(LAT_DEV - 1)
    for copy in copies:
        copy.wait()


def root_and_patterns(packed, anomaly):
    return pl.pallas_call(
        root_kernel,
        out_shape=(
            jax.ShapeDtypeStruct((LAT_DEV, LON_DEV, MONTHS), jnp.bfloat16),
            jax.ShapeDtypeStruct((MONTHS, MONTHS), jnp.float32),
        ),
        in_specs=[pl.BlockSpec(memory_space=pltpu.VMEM), pl.BlockSpec(memory_space=pl.ANY)],
        out_specs=(pl.BlockSpec(memory_space=pl.ANY),) * 2,
        scratch_shapes=[
            pltpu.VMEM((MONTHS, GROUPS * LANES), jnp.bfloat16),
            pltpu.VMEM((LAT_DEV, LON_DEV, MONTHS), jnp.bfloat16),
            pltpu.VMEM((MONTHS, MONTHS), jnp.float32),
            pltpu.VMEM((3 * MONTHS, MONTHS), jnp.bfloat16),
            pltpu.VMEM((3 * MONTHS, MONTHS), jnp.bfloat16),
            pltpu.VMEM((3 * MONTHS, MONTHS), jnp.bfloat16),
            pltpu.VMEM((2 * MONTHS, MONTHS), jnp.bfloat16),
            pltpu.VMEM((2 * MONTHS, MONTHS), jnp.bfloat16),
            pltpu.VMEM((MONTHS, MONTHS), jnp.bfloat16),
            pltpu.SemaphoreType.DMA,
            pltpu.SemaphoreType.DMA((LAT_DEV + 1,)),
        ],
        compiler_params=pltpu.CompilerParams(vmem_limit_bytes=32 * 1024 * 1024),
        name="root_and_patterns",
    )(packed, anomaly)


def exchange(pieces):
    return lax.all_to_all(pieces, BOTH, split_axis=0, concat_axis=0, tiled=True)


def exchange_packed(packed):
    pieces = packed.reshape(N_LON * N_LAT, PACK // 2, 2, LANES)
    return exchange(pieces).reshape(packed.shape)


def swap(x, k):
    return lax.ppermute(x, "lat", [(i, i ^ k) for i in range(N_LAT)])


def gather_widths(half_width):
    own = jnp.pad(half_width, (0, LANES - LAT_DEV)).reshape(1, LANES)
    rows = [own] + [swap(own, k) for k in (1, 2, 3)]
    place = lax.axis_index("lat") & 3
    at = jnp.arange(4, dtype=jnp.int32).reshape(4, 1)
    quad = jnp.zeros((4, LANES), jnp.int32)
    for k in range(4):
        quad = jnp.where(at == (place ^ k), rows[k], quad)
    return quad


def local(monthly_field, half_width, land_mask):
    quad = gather_widths(half_width)
    front = cut_windows(monthly_field, 0, FRONT)
    field, quad = lax.optimization_barrier((monthly_field, quad))
    quads = [quad] + [swap(quad, 4 * k) for k in (1, 2, 3)]
    back = cut_windows(field, FRONT, NLAT // 16 - FRONT)
    chip = (lax.axis_index("lat") >> 2).reshape(1)
    landed = exchange(smooth(chip, quads, front, back))
    row_index = lax.axis_index("lat") * LAT_DEV + jnp.arange(LAT_DEV)
    latitude = math.pi * ((row_index.astype(jnp.float32) + 0.5) / NLAT - 0.5)
    weight = jnp.sqrt(jnp.cos(latitude))[:, None] * land_mask.astype(jnp.float32)
    weight = jnp.pad(weight, ((0, 0), (0, 2 * LANES - LON_DEV)))
    packed, anomaly = gram_terms(landed, weight)
    packed = exchange_packed(packed)
    packed = exchange_packed(add_terms(packed))
    patterns, whitener = root_and_patterns(packed, anomaly)
    return (jnp.transpose(patterns, (2, 0, 1)), whitener)


def solution(mesh):
    placed = (P(("lon", "lat"), None, None), P("lat"), P("lat", "lon"))
    return jax.shard_map(
        local, mesh=mesh, in_specs=placed, out_specs=(P(None, "lat", "lon"), P()), check_vma=False
    )
```

```python
import functools
import math

import jax
import jax.numpy as jnp
import numpy as np
from jax import lax
from jax.experimental import pallas as pl
from jax.experimental.pallas import tpu as pltpu
from jax.sharding import Mesh
from jax.sharding import PartitionSpec as P

HMAX = 64
HL = 2
ITERS = 8
LAT = ("chip", "core")
BOTH = ("lon", "chip", "core")
SAME_CORE = ("lon", "chip")
HALF = 64
N_LON = 8
N_LAT = 16
NLAT = 240
NLON = 1440
MONTHS = 512
MON_DEV = 4
LAT_DEV = 15
LON_DEV = 180
LANES = 128
GROUPS = 22
SECOND = 56
TAIL = 112
CHUNK = MON_DEV * GROUPS
WINDOWS = MON_DEV * N_LON
SROWS = 3 * WINDOWS
SSTRIDE = 97
VSTRIDE = 89
FRONT = 8
BLOCKS = [(i, j) for i in range(4) for j in range(i, 4)]
PACK = len(BLOCKS)
VMEM_LIMIT = 60 * 1024 * 1024


def lat_taps():
    offsets = np.arange(-HL, HL + 1).astype(np.float32)
    taps = np.exp(-(offsets * offsets) / np.float32(2.0)).astype(np.float32)
    taps = taps / taps.sum(dtype=np.float32)
    return [float(t) for t in taps.astype(jnp.bfloat16).astype(np.float32)]


def windows_kernel(first_step, field_hbm, out_hbm, field, windows, staged, in_sems, out_sems):
    steps = windows.shape[0] // 16
    lane16 = lax.broadcasted_iota(jnp.int32, (16, LANES), 1)

    def fetch(i):
        rows = pl.ds(pl.multiple_of(i * 16, 16), 16)
        source = pl.ds(pl.multiple_of((first_step + i) * 16, 16), 16)
        return pltpu.make_async_copy(field_hbm.at[:, source, :], field.at[:, rows, :], in_sems.at[i])

    def store(i):
        rows = pl.ds(pl.multiple_of(i * 16, 16), 16)
        return pltpu.make_async_copy(windows.at[rows], out_hbm.at[rows], out_sems.at[i])

    for i in range(steps):
        fetch(i).start()

    def step(i, carry):
        fetch(i).wait()
        for m in range(MON_DEV):
            rows = field[m, pl.ds(pl.multiple_of(i * 16, 16), 16), :]
            ring = jnp.concatenate([rows, rows[:, :352]], axis=1)
            for l in range(N_LON):
                start = (LON_DEV * l - HMAX) % NLON
                first_tile, shift = start // LANES, start % LANES
                tiles = [ring[:, t * LANES : (t + 1) * LANES] for t in range(first_tile, first_tile + 4)]
                if shift:
                    tiles = [pltpu.roll(t, LANES - shift, 1) for t in tiles]
                for j in range(3):
                    piece = jnp.where(lane16 < LANES - shift, tiles[j], tiles[j + 1]) if shift else tiles[j]
                    piece = piece.astype(jnp.float32)
                    for half in range(2):
                        first = half * 8 * SSTRIDE + j * WINDOWS + m * N_LON + l
                        staged[pl.ds(first, 8, stride=SSTRIDE), :] = piece[half * 8 : half * 8 + 8]
        for r in range(16):
            windows[i * 16 + r] = staged[r * SSTRIDE : r * SSTRIDE + SROWS, :].astype(jnp.bfloat16)
        store(i).start()
        return carry

    lax.fori_loop(0, steps, step, 0)
    for i in range(steps):
        store(i).wait()


def cut_windows(field, first_step, steps):
    return pl.pallas_call(
        functools.partial(windows_kernel, first_step),
        out_shape=jax.ShapeDtypeStruct((steps * 16, SROWS, LANES), jnp.bfloat16),
        in_specs=[pl.BlockSpec(memory_space=pl.ANY)],
        out_specs=pl.BlockSpec(memory_space=pl.ANY),
        scratch_shapes=[
            pltpu.VMEM((MON_DEV, steps * 16, NLON), jnp.bfloat16),
            pltpu.VMEM((steps * 16, SROWS, LANES), jnp.bfloat16),
            pltpu.VMEM((16 * SSTRIDE + 8, LANES), jnp.float32),
            pltpu.SemaphoreType.DMA((steps,)),
            pltpu.SemaphoreType.DMA((steps,)),
        ],
        compiler_params=pltpu.CompilerParams(vmem_limit_bytes=VMEM_LIMIT),
        cost_estimate=pl.CostEstimate(flops=3000000000, bytes_accessed=9000000, transcendentals=0),
        name="cut_windows",
    )(field)


def smooth_kernel(chip, *refs):
    quads, refs = refs[:4], refs[4:]
    (front, back, out_hbm, windows, out, taps, passed, staged, widths, in_sems, out_sems) = refs

    def fetch(i):
        rows = pl.ds(i * 16, 16)
        if i < FRONT:
            return pltpu.make_async_copy(front.at[rows], windows.at[rows], in_sems.at[i])
        return pltpu.make_async_copy(back.at[pl.ds((i - FRONT) * 16, 16)], windows.at[rows], in_sems.at[i])

    def arrived(i):
        rows = pl.ds(pl.multiple_of(i * 16, 16), 16)
        pltpu.make_async_copy(windows.at[rows], windows.at[rows], in_sems.at[i]).wait()

    def store(b):
        return pltpu.make_async_copy(out.at[:, b], out_hbm.at[:, b], out_sems.at[b])

    for i in range(NLAT // 16):
        fetch(i).start()
    for k in range(4):
        for j in range(4):
            first = ((k ^ chip[0]) * 4 + j) * LAT_DEV
            for rr in range(LAT_DEV):
                widths[first + rr] = quads[k][j, rr]
    lane8 = lax.broadcasted_iota(jnp.int32, (8, LANES), 1)
    sub8 = lax.broadcasted_iota(jnp.int32, (8, LANES), 0)
    offset = (lane8 - HMAX).astype(jnp.float32)

    def build_taps(i, carry):
        reach = jnp.zeros((8, LANES), jnp.int32)
        for s in range(8):
            r = i * 8 + s
            reach = jnp.where(sub8 == s, widths[r], reach)
        reach = reach.astype(jnp.float32)
        spread = 0.5 * reach
        value = jnp.exp(-(offset * offset) / (2.0 * spread * spread))
        value = jnp.where(jnp.abs(offset) <= reach, value, 0.0)
        total = jnp.sum(value, axis=1, keepdims=True) + value[:, 0:1]
        value = (value / total).astype(jnp.bfloat16).astype(jnp.float32)
        taps[pl.ds(pl.multiple_of(i * 8, 8), 8), :] = value
        return carry

    lax.fori_loop(0, NLAT // 8, build_taps, 0, unroll=10)
    edge = jnp.zeros((HL, 2 * WINDOWS, LANES), jnp.float32)
    passed[0:HL] = edge
    passed[NLAT + HL : NLAT + 2 * HL] = edge
    sub = lax.broadcasted_iota(jnp.int32, (LANES, LANES), 0)
    lane = lax.broadcasted_iota(jnp.int32, (LANES, LANES), 1)
    upper = jnp.where(sub >= lane, 1.0, 0.0).astype(jnp.bfloat16)
    lower = jnp.where(sub <= lane, 1.0, 0.0).astype(jnp.bfloat16)

    def lon_band(b):
        for rr in range(LAT_DEV):
            r = b * LAT_DEV + rr
            lhs = windows[r]
            spread_taps = jnp.broadcast_to(taps[pl.ds(r, 1), :], (LANES, LANES))
            ring = pltpu.roll(spread_taps, 0, 1, stride=1, stride_axis=0).astype(jnp.bfloat16)
            left = jnp.concatenate([lhs[: 2 * WINDOWS], lhs[WINDOWS:]], axis=1)
            right = jnp.concatenate([ring * upper, ring * lower], axis=0)
            res = jnp.dot(left, right, preferred_element_type=jnp.float32)
            passed[r + HL] = res.astype(jnp.bfloat16).astype(jnp.float32)

    w0, w1, w2 = lat_taps()[:3]
    laneb = lax.broadcasted_iota(jnp.int32, (WINDOWS, LANES), 1)

    def lat_band(b):
        def smoothed(rr, lo, hi):
            r = b * LAT_DEV + rr
            outer = passed[r, lo:hi] + passed[r + 4, lo:hi]
            inner = passed[r + 1, lo:hi] + passed[r + 3, lo:hi]
            return w0 * outer + w1 * inner + w2 * passed[r + 2, lo:hi]

        def put(g, value):
            for m in range(MON_DEV):
                staged[pl.ds(m * GROUPS + g, N_LON, stride=VSTRIDE), :] = value[8 * m : 8 * m + 8]

        for rr in range(LAT_DEV):
            put(rr, smoothed(rr, 0, WINDOWS))
        last = smoothed(LAT_DEV - 1, WINDOWS, 2 * WINDOWS)
        for q in range(7):
            even = smoothed(2 * q, WINDOWS, 2 * WINDOWS)
            odd = smoothed(2 * q + 1, WINDOWS, 2 * WINDOWS)
            value = jnp.where(laneb < SECOND, even, pltpu.roll(odd, SECOND, 1))
            if q < 4:
                tail = pltpu.roll(last, TAIL - 16 * q, 1)
                value = jnp.where(laneb < TAIL, value, tail)
            put(LAT_DEV + q, value)
        for l in range(N_LON):
            out[l, b] = staged[l * VSTRIDE : l * VSTRIDE + CHUNK, :].astype(jnp.bfloat16)

    arrived(0)
    lon_band(0)

    def band(b, carry):
        arrived(b)
        lon_band(b)
        lat_band(b - 1)
        store(b - 1).start()
        return carry

    lax.fori_loop(1, N_LAT - 1, band, 0)
    lon_band(N_LAT - 1)
    for b in (N_LAT - 2, N_LAT - 1):
        lat_band(b)
        store(b).start()
    for b in range(N_LAT):
        store(b).wait()


def smooth(chip, quads, front, back):
    out = pl.pallas_call(
        smooth_kernel,
        out_shape=jax.ShapeDtypeStruct((N_LON, N_LAT, CHUNK, LANES), jnp.bfloat16),
        in_specs=[pl.BlockSpec(memory_space=pltpu.SMEM)] * 5 + [pl.BlockSpec(memory_space=pl.ANY)] * 2,
        out_specs=pl.BlockSpec(memory_space=pl.ANY),
        scratch_shapes=[
            pltpu.VMEM((NLAT, SROWS, LANES), jnp.bfloat16),
            pltpu.VMEM((N_LON, N_LAT, CHUNK, LANES), jnp.bfloat16),
            pltpu.VMEM((NLAT, LANES), jnp.float32),
            pltpu.VMEM((NLAT + 2 * HL, 2 * WINDOWS, LANES), jnp.float32),
            pltpu.VMEM((N_LON * VSTRIDE + 8, LANES), jnp.float32),
            pltpu.SMEM((NLAT,), jnp.int32),
            pltpu.SemaphoreType.DMA((NLAT // 16,)),
            pltpu.SemaphoreType.DMA((N_LAT,)),
        ],
        compiler_params=pltpu.CompilerParams(vmem_limit_bytes=VMEM_LIMIT),
        name="smooth",
    )(chip, *quads, front, back)
    return out.reshape(N_LON * N_LAT, CHUNK, LANES)


def gram_kernel(core, landed_hbm, weight, mine, theirs, anomaly_hbm, landed, wide, anomaly, square, in_sems, out_sem):
    parts = 4
    size = N_LON * N_LAT // parts
    copies = [
        pltpu.make_async_copy(
            landed_hbm.at[k * size : (k + 1) * size], landed.at[k * size : (k + 1) * size], in_sems.at[k]
        )
        for k in range(parts)
    ]
    for copy in copies:
        copy.start()

    def widen(s, carry):
        wide[pl.ds(pl.multiple_of(s * CHUNK, 8), CHUNK), :] = landed[s].astype(jnp.float32)
        return carry

    for k in range(parts):
        copies[k].wait()
        lax.fori_loop(k * size, (k + 1) * size, widen, 0, unroll=4)
    lane = lax.broadcasted_iota(jnp.int32, (1, LANES), 1)
    for g in range(GROUPS):
        if g < LAT_DEV:
            scale = weight[g : g + 1, :LANES]
        else:
            q = g - LAT_DEV
            scale = weight[2 * q : 2 * q + 1, LANES:]
            scale = scale + pltpu.roll(weight[2 * q + 1 : 2 * q + 2, LANES:], SECOND, 1)
            if q < 4:
                last = weight[LAT_DEV - 1 : LAT_DEV, LANES:]
                last = jnp.where((lane >= 16 * q) & (lane < 16 * q + 16), last, 0.0)
                scale = scale + pltpu.roll(last, TAIL - 16 * q, 1)
        cells = wide[pl.ds(g, MONTHS, stride=GROUPS), :]
        mean = jnp.sum(cells, axis=0, keepdims=True) * (1.0 / MONTHS)
        anomaly[:, g * LANES : (g + 1) * LANES] = ((cells - mean) * scale).astype(jnp.bfloat16)
    store = pltpu.make_async_copy(anomaly, anomaly_hbm, out_sem)
    store.start()
    for i, j in ((0, 0), (0, 1), (1, 1)):
        block = lax.dot_general(
            anomaly[i * ROWB : (i + 1) * ROWB, :],
            anomaly[j * ROWB : (j + 1) * ROWB, :],
            (((1,), (1,)), ((), ())),
            preferred_element_type=jnp.float32,
        )
        for n, (bi, bj) in enumerate(BLOCKS):
            if bi // 2 == i and bj // 2 == j:
                a, c = (bi % 2) * LANES, (bj % 2) * LANES
                square[...] = block[a : a + LANES, c : c + LANES]
                for ref, half in ((mine, core[0]), (theirs, 1 - core[0])):
                    rows = pl.ds(pl.multiple_of(half * HALF, HALF), HALF)
                    ref[pl.ds(n, HALF, stride=PACK), :] = square[rows, :]
    store.wait()


def gram_terms(core, landed, weight):
    part = jax.ShapeDtypeStruct((HALF * PACK, LANES), jnp.float32)
    return pl.pallas_call(
        gram_kernel,
        out_shape=(part, part, jax.ShapeDtypeStruct((MONTHS, GROUPS * LANES), jnp.bfloat16)),
        in_specs=[
            pl.BlockSpec(memory_space=pltpu.SMEM),
            pl.BlockSpec(memory_space=pl.ANY),
            pl.BlockSpec(memory_space=pltpu.VMEM),
        ],
        out_specs=(pl.BlockSpec(memory_space=pltpu.VMEM),) * 2 + (pl.BlockSpec(memory_space=pl.ANY),),
        scratch_shapes=[
            pltpu.VMEM((N_LON * N_LAT, CHUNK, LANES), jnp.bfloat16),
            pltpu.VMEM((N_LON * N_LAT * CHUNK, LANES), jnp.float32),
            pltpu.VMEM((MONTHS, GROUPS * LANES), jnp.bfloat16),
            pltpu.VMEM((LANES, LANES), jnp.float32),
            pltpu.SemaphoreType.DMA((4,)),
            pltpu.SemaphoreType.DMA,
        ],
        compiler_params=pltpu.CompilerParams(vmem_limit_bytes=32 * 1024 * 1024),
        name="gram_terms",
    )(core, landed, weight)


def turn_kernel(anomaly, turned):
    for g in range(GROUPS):
        turned[g * LANES : (g + 1) * LANES, :] = anomaly[:, g * LANES : (g + 1) * LANES].T


def turn(anomaly):
    return pl.pallas_call(
        turn_kernel,
        out_shape=jax.ShapeDtypeStruct((GROUPS * LANES, MONTHS), jnp.bfloat16),
        in_specs=[pl.BlockSpec(memory_space=pltpu.VMEM)],
        out_specs=pl.BlockSpec(memory_space=pltpu.VMEM),
        compiler_params=pltpu.CompilerParams(vmem_limit_bytes=16 * 1024 * 1024),
        cost_estimate=pl.CostEstimate(flops=2000000000, bytes_accessed=6000000, transcendentals=0),
        name="turn",
    )(anomaly)


def add_kernel(terms, out):
    step = 4 * PACK
    total = terms[0:step, :]
    for s in range(1, HALF // 4):
        total = total + terms[s * step : (s + 1) * step, :]
    row = total[0:PACK] + total[PACK : 2 * PACK] + total[2 * PACK : 3 * PACK] + total[3 * PACK :]
    total = jnp.concatenate([row] * 4, axis=0)
    for s in range(HALF // 4):
        out[s * step : (s + 1) * step, :] = total


def add_terms(terms):
    return pl.pallas_call(
        add_kernel,
        out_shape=jax.ShapeDtypeStruct(terms.shape, jnp.float32),
        in_specs=[pl.BlockSpec(memory_space=pltpu.VMEM)],
        out_specs=pl.BlockSpec(memory_space=pltpu.VMEM),
        compiler_params=pltpu.CompilerParams(vmem_limit_bytes=8 * 1024 * 1024),
        name="add_terms",
    )(terms)


STEP = (2.25, -2.4375, 1.6875, -0.5625, 0.0625)
ROWB = 256
MIRROR = True


def root_kernel(core, mine, theirs, anomaly_hbm, patterns_hbm, whitener_hbm, anomaly, patterns, whitener, ws, hs, ps, ss, zs, wb, in_sem, out_sems):
    fetch = pltpu.make_async_copy(anomaly_hbm, anomaly, in_sem)
    fetch.start()
    for n, (bi, bj) in enumerate(BLOCKS):
        for ref, half in ((mine, core[0]), (theirs, 1 - core[0])):
            rows = pl.ds(pl.multiple_of(bi * LANES + half * HALF, HALF), HALF)
            whitener[rows, bj * LANES : (bj + 1) * LANES] = ref[pl.ds(n, HALF, stride=PACK), :]
        if bi != bj:
            block = whitener[bi * LANES : (bi + 1) * LANES, bj * LANES : (bj + 1) * LANES]
            whitener[bj * LANES : (bj + 1) * LANES, bi * LANES : (bi + 1) * LANES] = block.T
    gram = whitener[...]
    squares = jnp.sum(gram * gram, axis=0, keepdims=True)
    frobenius = jnp.sqrt(jnp.sum(squares, axis=1, keepdims=True) + 1e-06)
    final_scale = jnp.sqrt(float(NLAT * NLON) / frobenius)

    def split(ref, start, value):
        size = value.shape[0]
        high = value.astype(jnp.bfloat16)
        ref[start : start + size, :] = high
        ref[MONTHS + start : MONTHS + start + size, :] = (value - high.astype(jnp.float32)).astype(jnp.bfloat16)
        if ref.shape[0] == 3 * MONTHS:
            ref[2 * MONTHS + start : 2 * MONTHS + start + size, :] = high

    def join(ref, start):
        high = ref[start : start + ROWB, :].astype(jnp.float32)
        return high + ref[MONTHS + start : MONTHS + start + ROWB, :].astype(jnp.float32)

    def product(left, right):
        def rows(start):
            high = left[start : start + ROWB, :]
            low = left[MONTHS + start : MONTHS + start + ROWB, :]
            return jnp.concatenate([high, high, low], axis=1)

        upper = jnp.dot(rows(0), right[...], preferred_element_type=jnp.float32)
        if not MIRROR:
            return upper, jnp.dot(rows(ROWB), right[...], preferred_element_type=jnp.float32)
        corner = jnp.dot(rows(ROWB), right[:, ROWB:], preferred_element_type=jnp.float32)
        return upper, jnp.concatenate([upper[:, ROWB:].T, corner], axis=1)

    def plus_eye(value, start, scale):
        row = lax.broadcasted_iota(jnp.int32, value.shape, 0) + start
        column = lax.broadcasted_iota(jnp.int32, value.shape, 1)
        return jnp.where(row == column, value + scale, value)

    split(ws, 0, gram / frobenius)
    c0, c1, c2, c3, c4 = STEP
    last = ITERS // 2 - 1

    def double_step(k):
        for n, square in enumerate(product(ws, ws)):
            start = n * ROWB
            split(ss, start, square)
            split(hs, start, plus_eye(c3 * join(ws, start) + c4 * square, start, c2))
        for n, value in enumerate(product(ss, hs)):
            start = n * ROWB
            split(ps, start, plus_eye(value + c1 * join(ws, start), start, c0))

        if k == 0:
            zs[...] = ps[0 : 2 * MONTHS, :]

        if k > 0:
            for n, value in enumerate(product(zs, ps)):
                split(zs, n * ROWB, value)
                whitener[n * ROWB : (n + 1) * ROWB, :] = value * final_scale

        if k < last:
            for n, value in enumerate(product(ws, ps)):
                split(ss, n * ROWB, value)
            for n, value in enumerate(product(ss, ps)):
                split(ws, n * ROWB, value)

    for k in range(last + 1):
        double_step(k)
    copies = [pltpu.make_async_copy(whitener, whitener_hbm, out_sems.at[LAT_DEV])]
    copies[0].start()
    wb[...] = whitener[...].astype(jnp.bfloat16)
    fetch.wait()

    def group(g):
        return lax.dot_general(
            anomaly[g * LANES : (g + 1) * LANES, :],
            wb[...],
            (((1,), (1,)), ((), ())),
            preferred_element_type=jnp.float32,
        ).astype(jnp.bfloat16)

    def finish(r):
        copy = pltpu.make_async_copy(patterns.at[r], patterns_hbm.at[r], out_sems.at[r])
        copy.start()
        copies.append(copy)

    for q in range(7):
        value = group(LAT_DEV + q)
        patterns[2 * q, LANES:, :] = value[0 : LON_DEV - LANES]
        patterns[2 * q + 1, LANES:, :] = value[SECOND : SECOND + LON_DEV - LANES]
        if q < 4:
            first = LANES + 16 * q
            size = min(16, LON_DEV - first)
            patterns[LAT_DEV - 1, first : first + size, :] = value[TAIL : TAIL + size]
        for r in (2 * q, 2 * q + 1):
            patterns[r, 0:LANES, :] = group(r)
            finish(r)
    patterns[LAT_DEV - 1, 0:LANES, :] = group(LAT_DEV - 1)
    finish(LAT_DEV - 1)
    for copy in copies:
        copy.wait()


def root_and_patterns(core, mine, theirs, turned):
    return pl.pallas_call(
        root_kernel,
        out_shape=(
            jax.ShapeDtypeStruct((LAT_DEV, LON_DEV, MONTHS), jnp.bfloat16),
            jax.ShapeDtypeStruct((MONTHS, MONTHS), jnp.float32),
        ),
        in_specs=[
            pl.BlockSpec(memory_space=pltpu.SMEM),
            pl.BlockSpec(memory_space=pltpu.VMEM),
            pl.BlockSpec(memory_space=pltpu.VMEM),
            pl.BlockSpec(memory_space=pl.ANY),
        ],
        out_specs=(pl.BlockSpec(memory_space=pl.ANY),) * 2,
        scratch_shapes=[
            pltpu.VMEM((GROUPS * LANES, MONTHS), jnp.bfloat16),
            pltpu.VMEM((LAT_DEV, LON_DEV, MONTHS), jnp.bfloat16),
            pltpu.VMEM((MONTHS, MONTHS), jnp.float32),
            pltpu.VMEM((3 * MONTHS, MONTHS), jnp.bfloat16),
            pltpu.VMEM((3 * MONTHS, MONTHS), jnp.bfloat16),
            pltpu.VMEM((3 * MONTHS, MONTHS), jnp.bfloat16),
            pltpu.VMEM((2 * MONTHS, MONTHS), jnp.bfloat16),
            pltpu.VMEM((2 * MONTHS, MONTHS), jnp.bfloat16),
            pltpu.VMEM((MONTHS, MONTHS), jnp.bfloat16),
            pltpu.SemaphoreType.DMA,
            pltpu.SemaphoreType.DMA((LAT_DEV + 1,)),
        ],
        compiler_params=pltpu.CompilerParams(vmem_limit_bytes=32 * 1024 * 1024),
        name="root_and_patterns",
    )(core, mine, theirs, turned)


def exchange(pieces, axes):
    return lax.all_to_all(pieces, axes, split_axis=0, concat_axis=0, tiled=True)


def exchange_packed(packed):
    pieces = packed.reshape(HALF, PACK // 2, 2, LANES)
    return exchange(pieces, SAME_CORE).reshape(packed.shape)


def swap_cores(x):
    return lax.ppermute(x, "core", [(0, 1), (1, 0)])


def swap(x, k):
    return lax.ppermute(x, LAT, [(i, i ^ k) for i in range(N_LAT)])


def gather_widths(half_width):
    own = jnp.pad(half_width, (0, LANES - LAT_DEV)).reshape(1, LANES)
    rows = [own] + [swap(own, k) for k in (1, 2, 3)]
    place = lax.axis_index(LAT) & 3
    at = jnp.arange(4, dtype=jnp.int32).reshape(4, 1)
    quad = jnp.zeros((4, LANES), jnp.int32)
    for k in range(4):
        quad = jnp.where(at == (place ^ k), rows[k], quad)
    return quad


def local(monthly_field, half_width, land_mask):
    quad = gather_widths(half_width)
    front = cut_windows(monthly_field, 0, FRONT)
    field, quad = lax.optimization_barrier((monthly_field, quad))
    quads = [quad] + [swap(quad, 4 * k) for k in (1, 2, 3)]
    back = cut_windows(field, FRONT, NLAT // 16 - FRONT)
    chip = (lax.axis_index(LAT) >> 2).reshape(1)
    landed = exchange(smooth(chip, quads, front, back), BOTH)
    row_index = lax.axis_index(LAT) * LAT_DEV + jnp.arange(LAT_DEV)
    latitude = math.pi * ((row_index.astype(jnp.float32) + 0.5) / NLAT - 0.5)
    weight = jnp.sqrt(jnp.cos(latitude))[:, None] * land_mask.astype(jnp.float32)
    weight = jnp.pad(weight, ((0, 0), (0, 2 * LANES - LON_DEV)))
    core = lax.axis_index("core").reshape(1)
    mine, theirs, anomaly = gram_terms(core, landed, weight)
    terms = exchange_packed(mine + swap_cores(theirs))
    turned = turn(anomaly)
    mine = exchange_packed(add_terms(terms))
    patterns, whitener = root_and_patterns(core, mine, swap_cores(mine), turned)
    return (jnp.transpose(patterns, (2, 0, 1)), whitener)


def solution(mesh):
    fine = Mesh(mesh.devices.reshape(N_LON, N_LAT // 2, 2), BOTH)
    placed = (P(BOTH, None, None), P(LAT), P(LAT, "lon"))
    return jax.shard_map(
        local, mesh=fine, in_specs=placed, out_specs=(P(None, LAT, "lon"), P()), check_vma=False
    )
```

```python
import math

import jax
import jax.numpy as jnp
import numpy as np
from jax import lax
from jax.experimental import pallas as pl
from jax.experimental.pallas import tpu as pltpu
from jax.sharding import Mesh
from jax.sharding import PartitionSpec as P

HMAX = 64
HL = 2
ITERS = 8
LAT = ("chip", "core")
BOTH = ("lon", "chip", "core")
SAME_CORE = ("lon", "chip")
HALF = 64
N_LON = 8
N_LAT = 16
NLAT = 240
NLON = 1440
MONTHS = 512
MON_DEV = 4
LAT_DEV = 15
LON_DEV = 180
LANES = 128
GROUPS = 22
SECOND = 56
TAIL = 112
CHUNK = MON_DEV * GROUPS
WINDOWS = MON_DEV * N_LON
SROWS = 3 * WINDOWS
SSTRIDE = 97
VSTRIDE = 89
BLOCKS = [(i, j) for i in range(4) for j in range(i, 4)]
PACK = len(BLOCKS)
VMEM_LIMIT = 60 * 1024 * 1024


def lat_taps():
    offsets = np.arange(-HL, HL + 1).astype(np.float32)
    taps = np.exp(-(offsets * offsets) / np.float32(2.0)).astype(np.float32)
    taps = taps / taps.sum(dtype=np.float32)
    return [float(t) for t in taps.astype(jnp.bfloat16).astype(np.float32)]


def windows_kernel(field_hbm, out_hbm, field, windows, staged, in_sems, out_sems):
    steps = windows.shape[0] // 16
    lane16 = lax.broadcasted_iota(jnp.int32, (16, LANES), 1)

    def fetch(i):
        rows = pl.ds(pl.multiple_of(i * 16, 16), 16)
        return pltpu.make_async_copy(field_hbm.at[:, rows, :], field.at[:, rows, :], in_sems.at[i])

    def store(i):
        rows = pl.ds(pl.multiple_of(i * 16, 16), 16)
        return pltpu.make_async_copy(windows.at[rows], out_hbm.at[rows], out_sems.at[i])

    for i in range(steps):
        fetch(i).start()

    def step(i, carry):
        fetch(i).wait()
        for m in range(MON_DEV):
            rows = field[m, pl.ds(pl.multiple_of(i * 16, 16), 16), :]
            ring = jnp.concatenate([rows, rows[:, :352]], axis=1)
            for l in range(N_LON):
                start = (LON_DEV * l - HMAX) % NLON
                first_tile, shift = start // LANES, start % LANES
                tiles = [ring[:, t * LANES : (t + 1) * LANES] for t in range(first_tile, first_tile + 4)]
                if shift:
                    tiles = [pltpu.roll(t, LANES - shift, 1) for t in tiles]
                for j in range(3):
                    piece = jnp.where(lane16 < LANES - shift, tiles[j], tiles[j + 1]) if shift else tiles[j]
                    piece = piece.astype(jnp.float32)
                    for half in range(2):
                        first = half * 8 * SSTRIDE + j * WINDOWS + m * N_LON + l
                        staged[pl.ds(first, 8, stride=SSTRIDE), :] = piece[half * 8 : half * 8 + 8]
        for r in range(16):
            windows[i * 16 + r] = staged[r * SSTRIDE : r * SSTRIDE + SROWS, :].astype(jnp.bfloat16)
        store(i).start()
        return carry

    lax.fori_loop(0, steps, step, 0)
    for i in range(steps):
        store(i).wait()


def cut_windows(field):
    steps = NLAT // 16
    return pl.pallas_call(
        windows_kernel,
        out_shape=jax.ShapeDtypeStruct((steps * 16, SROWS, LANES), jnp.bfloat16),
        in_specs=[pl.BlockSpec(memory_space=pl.ANY)],
        out_specs=pl.BlockSpec(memory_space=pl.ANY),
        scratch_shapes=[
            pltpu.VMEM((MON_DEV, steps * 16, NLON), jnp.bfloat16),
            pltpu.VMEM((steps * 16, SROWS, LANES), jnp.bfloat16),
            pltpu.VMEM((16 * SSTRIDE + 8, LANES), jnp.float32),
            pltpu.SemaphoreType.DMA((steps,)),
            pltpu.SemaphoreType.DMA((steps,)),
        ],
        compiler_params=pltpu.CompilerParams(vmem_limit_bytes=VMEM_LIMIT),
        cost_estimate=pl.CostEstimate(flops=3000000000, bytes_accessed=9000000, transcendentals=0),
        name="cut_windows",
    )(field)


def smooth_kernel(widths, windows_hbm, out_hbm, windows, out, taps, passed, staged, in_sems, out_sems):

    def fetch(i):
        rows = pl.ds(pl.multiple_of(i * 16, 16), 16)
        return pltpu.make_async_copy(windows_hbm.at[rows], windows.at[rows], in_sems.at[i])

    def store(b):
        return pltpu.make_async_copy(out.at[:, b], out_hbm.at[:, b], out_sems.at[b])

    for i in range(NLAT // 16):
        fetch(i).start()
    lane8 = lax.broadcasted_iota(jnp.int32, (8, LANES), 1)
    sub8 = lax.broadcasted_iota(jnp.int32, (8, LANES), 0)
    offset = (lane8 - HMAX).astype(jnp.float32)

    def build_taps(i, carry):
        reach = jnp.zeros((8, LANES), jnp.int32)
        for s in range(8):
            r = i * 8 + s
            reach = jnp.where(sub8 == s, widths[r // LAT_DEV, r % LAT_DEV], reach)
        reach = reach.astype(jnp.float32)
        spread = 0.5 * reach
        value = jnp.exp(-(offset * offset) / (2.0 * spread * spread))
        value = jnp.where(jnp.abs(offset) <= reach, value, 0.0)
        total = jnp.sum(value, axis=1, keepdims=True) + value[:, 0:1]
        value = (value / total).astype(jnp.bfloat16).astype(jnp.float32)
        taps[pl.ds(pl.multiple_of(i * 8, 8), 8), :] = value
        return carry

    lax.fori_loop(0, NLAT // 8, build_taps, 0, unroll=10)
    edge = jnp.zeros((HL, 2 * WINDOWS, LANES), jnp.float32)
    passed[0:HL] = edge
    passed[NLAT + HL : NLAT + 2 * HL] = edge
    sub = lax.broadcasted_iota(jnp.int32, (LANES, LANES), 0)
    lane = lax.broadcasted_iota(jnp.int32, (LANES, LANES), 1)
    upper = jnp.where(sub >= lane, 1.0, 0.0).astype(jnp.bfloat16)
    lower = jnp.where(sub <= lane, 1.0, 0.0).astype(jnp.bfloat16)

    def lon_band(b):
        for rr in range(LAT_DEV):
            r = b * LAT_DEV + rr
            lhs = windows[r]
            spread_taps = jnp.broadcast_to(taps[pl.ds(r, 1), :], (LANES, LANES))
            ring = pltpu.roll(spread_taps, 0, 1, stride=1, stride_axis=0).astype(jnp.bfloat16)
            left = jnp.concatenate([lhs[: 2 * WINDOWS], lhs[WINDOWS:]], axis=1)
            right = jnp.concatenate([ring * upper, ring * lower], axis=0)
            res = jnp.dot(left, right, preferred_element_type=jnp.float32)
            passed[r + HL] = res.astype(jnp.bfloat16).astype(jnp.float32)

    w0, w1, w2 = lat_taps()[:3]
    laneb = lax.broadcasted_iota(jnp.int32, (WINDOWS, LANES), 1)

    def lat_band(b):
        def smoothed(rr, lo, hi):
            r = b * LAT_DEV + rr
            outer = passed[r, lo:hi] + passed[r + 4, lo:hi]
            inner = passed[r + 1, lo:hi] + passed[r + 3, lo:hi]
            return w0 * outer + w1 * inner + w2 * passed[r + 2, lo:hi]

        def put(g, value):
            for m in range(MON_DEV):
                staged[pl.ds(m * GROUPS + g, N_LON, stride=VSTRIDE), :] = value[8 * m : 8 * m + 8]

        for rr in range(LAT_DEV):
            put(rr, smoothed(rr, 0, WINDOWS))
        last = smoothed(LAT_DEV - 1, WINDOWS, 2 * WINDOWS)
        for q in range(7):
            even = smoothed(2 * q, WINDOWS, 2 * WINDOWS)
            odd = smoothed(2 * q + 1, WINDOWS, 2 * WINDOWS)
            value = jnp.where(laneb < SECOND, even, pltpu.roll(odd, SECOND, 1))
            if q < 4:
                tail = pltpu.roll(last, TAIL - 16 * q, 1)
                value = jnp.where(laneb < TAIL, value, tail)
            put(LAT_DEV + q, value)
        for l in range(N_LON):
            out[l, b] = staged[l * VSTRIDE : l * VSTRIDE + CHUNK, :].astype(jnp.bfloat16)

    fetch(0).wait()
    lon_band(0)

    def band(b, carry):
        fetch(b).wait()
        lon_band(b)
        lat_band(b - 1)
        store(b - 1).start()
        return carry

    lax.fori_loop(1, N_LAT - 1, band, 0)
    lon_band(N_LAT - 1)
    for b in (N_LAT - 2, N_LAT - 1):
        lat_band(b)
        store(b).start()
    for b in range(N_LAT):
        store(b).wait()


def smooth(widths, windows):
    out = pl.pallas_call(
        smooth_kernel,
        out_shape=jax.ShapeDtypeStruct((N_LON, N_LAT, CHUNK, LANES), jnp.bfloat16),
        in_specs=[pl.BlockSpec(memory_space=pltpu.SMEM), pl.BlockSpec(memory_space=pl.ANY)],
        out_specs=pl.BlockSpec(memory_space=pl.ANY),
        scratch_shapes=[
            pltpu.VMEM((NLAT, SROWS, LANES), jnp.bfloat16),
            pltpu.VMEM((N_LON, N_LAT, CHUNK, LANES), jnp.bfloat16),
            pltpu.VMEM((NLAT, LANES), jnp.float32),
            pltpu.VMEM((NLAT + 2 * HL, 2 * WINDOWS, LANES), jnp.float32),
            pltpu.VMEM((N_LON * VSTRIDE + 8, LANES), jnp.float32),
            pltpu.SemaphoreType.DMA((NLAT // 16,)),
            pltpu.SemaphoreType.DMA((N_LAT,)),
        ],
        compiler_params=pltpu.CompilerParams(vmem_limit_bytes=VMEM_LIMIT),
        name="smooth",
    )(widths, windows)
    return out.reshape(N_LON * N_LAT, CHUNK, LANES)


def gram_kernel(core, landed, weight, mine, theirs, anomaly, wide, square):
    def widen(s, carry):
        wide[pl.ds(pl.multiple_of(s * CHUNK, 8), CHUNK), :] = landed[s].astype(jnp.float32)
        return carry

    lax.fori_loop(0, N_LON * N_LAT, widen, 0, unroll=4)
    lane = lax.broadcasted_iota(jnp.int32, (1, LANES), 1)
    for g in range(GROUPS):
        if g < LAT_DEV:
            scale = weight[g : g + 1, :LANES]
        else:
            q = g - LAT_DEV
            scale = weight[2 * q : 2 * q + 1, LANES:]
            scale = scale + pltpu.roll(weight[2 * q + 1 : 2 * q + 2, LANES:], SECOND, 1)
            if q < 4:
                last = weight[LAT_DEV - 1 : LAT_DEV, LANES:]
                last = jnp.where((lane >= 16 * q) & (lane < 16 * q + 16), last, 0.0)
                scale = scale + pltpu.roll(last, TAIL - 16 * q, 1)
        cells = wide[pl.ds(g, MONTHS, stride=GROUPS), :]
        mean = jnp.sum(cells, axis=0, keepdims=True) * (1.0 / MONTHS)
        anomaly[:, g * LANES : (g + 1) * LANES] = ((cells - mean) * scale).astype(jnp.bfloat16)
    for i, j in ((0, 0), (0, 1), (1, 1)):
        block = lax.dot_general(
            anomaly[i * ROWB : (i + 1) * ROWB, :],
            anomaly[j * ROWB : (j + 1) * ROWB, :],
            (((1,), (1,)), ((), ())),
            preferred_element_type=jnp.float32,
        )
        for n, (bi, bj) in enumerate(BLOCKS):
            if bi // 2 == i and bj // 2 == j:
                a, c = (bi % 2) * LANES, (bj % 2) * LANES
                square[...] = block[a : a + LANES, c : c + LANES]
                for ref, half in ((mine, core[0]), (theirs, 1 - core[0])):
                    rows = pl.ds(pl.multiple_of(half * HALF, HALF), HALF)
                    ref[pl.ds(n, HALF, stride=PACK), :] = square[rows, :]


def gram_terms(core, landed, weight):
    part = jax.ShapeDtypeStruct((HALF * PACK, LANES), jnp.float32)
    return pl.pallas_call(
        gram_kernel,
        out_shape=(part, part, jax.ShapeDtypeStruct((MONTHS, GROUPS * LANES), jnp.bfloat16)),
        in_specs=[
            pl.BlockSpec(memory_space=pltpu.SMEM),
            pl.BlockSpec(memory_space=pltpu.VMEM),
            pl.BlockSpec(memory_space=pltpu.VMEM),
        ],
        out_specs=(pl.BlockSpec(memory_space=pltpu.VMEM),) * 3,
        scratch_shapes=[
            pltpu.VMEM((N_LON * N_LAT * CHUNK, LANES), jnp.float32),
            pltpu.VMEM((LANES, LANES), jnp.float32),
        ],
        compiler_params=pltpu.CompilerParams(vmem_limit_bytes=32 * 1024 * 1024),
        name="gram_terms",
    )(core, landed, weight)


def turn_kernel(anomaly, turned):
    for g in range(GROUPS):
        turned[g * LANES : (g + 1) * LANES, :] = anomaly[:, g * LANES : (g + 1) * LANES].T


def turn(anomaly):
    return pl.pallas_call(
        turn_kernel,
        out_shape=jax.ShapeDtypeStruct((GROUPS * LANES, MONTHS), jnp.bfloat16),
        in_specs=[pl.BlockSpec(memory_space=pltpu.VMEM)],
        out_specs=pl.BlockSpec(memory_space=pltpu.VMEM),
        compiler_params=pltpu.CompilerParams(vmem_limit_bytes=16 * 1024 * 1024),
        cost_estimate=pl.CostEstimate(flops=2000000000, bytes_accessed=6000000, transcendentals=0),
        name="turn",
    )(anomaly)


def add_kernel(terms, out):
    step = 4 * PACK
    total = terms[0:step, :]
    for s in range(1, HALF // 4):
        total = total + terms[s * step : (s + 1) * step, :]
    row = total[0:PACK] + total[PACK : 2 * PACK] + total[2 * PACK : 3 * PACK] + total[3 * PACK :]
    total = jnp.concatenate([row] * 4, axis=0)
    for s in range(HALF // 4):
        out[s * step : (s + 1) * step, :] = total


def add_terms(terms):
    return pl.pallas_call(
        add_kernel,
        out_shape=jax.ShapeDtypeStruct(terms.shape, jnp.float32),
        in_specs=[pl.BlockSpec(memory_space=pltpu.VMEM)],
        out_specs=pl.BlockSpec(memory_space=pltpu.VMEM),
        compiler_params=pltpu.CompilerParams(vmem_limit_bytes=8 * 1024 * 1024),
        name="add_terms",
    )(terms)


STEP = (2.25, -2.4375, 1.6875, -0.5625, 0.0625)
ROWB = 256
MIRROR = True


def root_kernel(core, mine, theirs, anomaly, patterns_hbm, whitener_hbm, patterns, whitener, ws, hs, ps, ss, zs, wb, out_sems):
    for n, (bi, bj) in enumerate(BLOCKS):
        for ref, half in ((mine, core[0]), (theirs, 1 - core[0])):
            rows = pl.ds(pl.multiple_of(bi * LANES + half * HALF, HALF), HALF)
            whitener[rows, bj * LANES : (bj + 1) * LANES] = ref[pl.ds(n, HALF, stride=PACK), :]
        if bi != bj:
            block = whitener[bi * LANES : (bi + 1) * LANES, bj * LANES : (bj + 1) * LANES]
            whitener[bj * LANES : (bj + 1) * LANES, bi * LANES : (bi + 1) * LANES] = block.T
    gram = whitener[...]
    squares = jnp.sum(gram * gram, axis=0, keepdims=True)
    frobenius = jnp.sqrt(jnp.sum(squares, axis=1, keepdims=True) + 1e-06)
    final_scale = jnp.sqrt(float(NLAT * NLON) / frobenius)

    def split(ref, start, value):
        size = value.shape[0]
        high = value.astype(jnp.bfloat16)
        ref[start : start + size, :] = high
        ref[MONTHS + start : MONTHS + start + size, :] = (value - high.astype(jnp.float32)).astype(jnp.bfloat16)
        if ref.shape[0] == 3 * MONTHS:
            ref[2 * MONTHS + start : 2 * MONTHS + start + size, :] = high

    def join(ref, start):
        high = ref[start : start + ROWB, :].astype(jnp.float32)
        return high + ref[MONTHS + start : MONTHS + start + ROWB, :].astype(jnp.float32)

    def product(left, right):
        def rows(start):
            high = left[start : start + ROWB, :]
            low = left[MONTHS + start : MONTHS + start + ROWB, :]
            return jnp.concatenate([high, high, low], axis=1)

        upper = jnp.dot(rows(0), right[...], preferred_element_type=jnp.float32)
        if not MIRROR:
            return upper, jnp.dot(rows(ROWB), right[...], preferred_element_type=jnp.float32)
        corner = jnp.dot(rows(ROWB), right[:, ROWB:], preferred_element_type=jnp.float32)
        return upper, jnp.concatenate([upper[:, ROWB:].T, corner], axis=1)

    def plus_eye(value, start, scale):
        row = lax.broadcasted_iota(jnp.int32, value.shape, 0) + start
        column = lax.broadcasted_iota(jnp.int32, value.shape, 1)
        return jnp.where(row == column, value + scale, value)

    split(ws, 0, gram / frobenius)
    c0, c1, c2, c3, c4 = STEP
    last = ITERS // 2 - 1

    def double_step(k):
        for n, square in enumerate(product(ws, ws)):
            start = n * ROWB
            split(ss, start, square)
            split(hs, start, plus_eye(c3 * join(ws, start) + c4 * square, start, c2))
        for n, value in enumerate(product(ss, hs)):
            start = n * ROWB
            split(ps, start, plus_eye(value + c1 * join(ws, start), start, c0))

        if k == 0:
            zs[...] = ps[0 : 2 * MONTHS, :]

        if k > 0:
            for n, value in enumerate(product(zs, ps)):
                split(zs, n * ROWB, value)
                whitener[n * ROWB : (n + 1) * ROWB, :] = value * final_scale

        if k < last:
            for n, value in enumerate(product(ws, ps)):
                split(ss, n * ROWB, value)
            for n, value in enumerate(product(ss, ps)):
                split(ws, n * ROWB, value)

    for k in range(last + 1):
        double_step(k)
    copies = [pltpu.make_async_copy(whitener, whitener_hbm, out_sems.at[LAT_DEV])]
    copies[0].start()
    wb[...] = whitener[...].astype(jnp.bfloat16)

    def group(g):
        return lax.dot_general(
            anomaly[g * LANES : (g + 1) * LANES, :],
            wb[...],
            (((1,), (0,)), ((), ())),
            preferred_element_type=jnp.float32,
        ).astype(jnp.bfloat16)

    def finish(r):
        copy = pltpu.make_async_copy(patterns.at[r], patterns_hbm.at[r], out_sems.at[r])
        copy.start()
        copies.append(copy)

    for q in range(7):
        value = group(LAT_DEV + q)
        patterns[2 * q, LANES:, :] = value[0 : LON_DEV - LANES]
        patterns[2 * q + 1, LANES:, :] = value[SECOND : SECOND + LON_DEV - LANES]
        if q < 4:
            first = LANES + 16 * q
            size = min(16, LON_DEV - first)
            patterns[LAT_DEV - 1, first : first + size, :] = value[TAIL : TAIL + size]
        for r in (2 * q, 2 * q + 1):
            patterns[r, 0:LANES, :] = group(r)
            finish(r)
    patterns[LAT_DEV - 1, 0:LANES, :] = group(LAT_DEV - 1)
    finish(LAT_DEV - 1)
    for copy in copies:
        copy.wait()


def root_and_patterns(core, mine, theirs, turned):
    return pl.pallas_call(
        root_kernel,
        out_shape=(
            jax.ShapeDtypeStruct((LAT_DEV, LON_DEV, MONTHS), jnp.bfloat16),
            jax.ShapeDtypeStruct((MONTHS, MONTHS), jnp.float32),
        ),
        in_specs=[
            pl.BlockSpec(memory_space=pltpu.SMEM),
            pl.BlockSpec(memory_space=pltpu.VMEM),
            pl.BlockSpec(memory_space=pltpu.VMEM),
            pl.BlockSpec(memory_space=pltpu.VMEM),
        ],
        out_specs=(pl.BlockSpec(memory_space=pl.ANY),) * 2,
        scratch_shapes=[
            pltpu.VMEM((LAT_DEV, LON_DEV, MONTHS), jnp.bfloat16),
            pltpu.VMEM((MONTHS, MONTHS), jnp.float32),
            pltpu.VMEM((3 * MONTHS, MONTHS), jnp.bfloat16),
            pltpu.VMEM((3 * MONTHS, MONTHS), jnp.bfloat16),
            pltpu.VMEM((3 * MONTHS, MONTHS), jnp.bfloat16),
            pltpu.VMEM((2 * MONTHS, MONTHS), jnp.bfloat16),
            pltpu.VMEM((2 * MONTHS, MONTHS), jnp.bfloat16),
            pltpu.VMEM((MONTHS, MONTHS), jnp.bfloat16),
            pltpu.SemaphoreType.DMA((LAT_DEV + 1,)),
        ],
        compiler_params=pltpu.CompilerParams(vmem_limit_bytes=32 * 1024 * 1024),
        name="root_and_patterns",
    )(core, mine, theirs, turned)


def exchange(pieces, axes):
    return lax.all_to_all(pieces, axes, split_axis=0, concat_axis=0, tiled=True)


def exchange_packed(packed):
    pieces = packed.reshape(HALF, PACK // 2, 2, LANES)
    return exchange(pieces, SAME_CORE).reshape(packed.shape)


def swap_cores(x):
    return lax.ppermute(x, "core", [(0, 1), (1, 0)])


def local(monthly_field, half_width, land_mask):
    widths = jnp.broadcast_to(jnp.pad(half_width, (0, LANES - LAT_DEV)), (N_LAT, 1, LANES))
    widths = exchange(widths, LAT).reshape(N_LAT, LANES)
    windows = cut_windows(monthly_field)
    landed = exchange(smooth(widths, windows), BOTH)
    row_index = lax.axis_index(LAT) * LAT_DEV + jnp.arange(LAT_DEV)
    latitude = math.pi * ((row_index.astype(jnp.float32) + 0.5) / NLAT - 0.5)
    weight = jnp.sqrt(jnp.cos(latitude))[:, None] * land_mask.astype(jnp.float32)
    weight = jnp.pad(weight, ((0, 0), (0, 2 * LANES - LON_DEV)))
    core = lax.axis_index("core").reshape(1)
    mine, theirs, anomaly = gram_terms(core, landed, weight)
    terms = exchange_packed(mine + swap_cores(theirs))
    turned = turn(anomaly)
    mine = exchange_packed(add_terms(terms))
    patterns, whitener = root_and_patterns(core, mine, swap_cores(mine), turned)
    return (jnp.transpose(patterns, (2, 0, 1)), whitener)


def solution(mesh):
    fine = Mesh(mesh.devices.reshape(N_LON, N_LAT // 2, 2), BOTH)
    placed = (P(BOTH, None, None), P(LAT), P(LAT, "lon"))
    return jax.shard_map(
        local, mesh=fine, in_specs=placed, out_specs=(P(None, LAT, "lon"), P()), check_vma=False
    )
```

```python
import functools
import math

import jax
import jax.numpy as jnp
import numpy as np
from jax import lax
from jax.experimental import pallas as pl
from jax.experimental.pallas import tpu as pltpu
from jax.sharding import Mesh
from jax.sharding import PartitionSpec as P

HMAX = 64
HL = 2
ITERS = 8
LAT = ("chip", "core")
BOTH = ("lon", "chip", "core")
SAME_CORE = ("lon", "chip")
HALF = 64
N_LON = 8
N_LAT = 16
NLAT = 240
NLON = 1440
MONTHS = 512
MON_DEV = 4
LAT_DEV = 15
LON_DEV = 180
LANES = 128
GROUPS = 22
SECOND = 56
TAIL = 112
EARLY = 12
LATE = GROUPS - EARLY
WINDOWS = MON_DEV * N_LON
BLOCKS = [(i, j) for i in range(4) for j in range(i, 4)]
PACK = len(BLOCKS)
VMEM_LIMIT = 60 * 1024 * 1024


def lat_taps():
    offsets = np.arange(-HL, HL + 1).astype(np.float32)
    taps = np.exp(-(offsets * offsets) / np.float32(2.0)).astype(np.float32)
    taps = taps / taps.sum(dtype=np.float32)
    return [float(t) for t in taps.astype(jnp.bfloat16).astype(np.float32)]


def windows_kernel(tiles, field_hbm, out_hbm, field, windows, staged, in_sems, out_sems):
    steps = NLAT // 16
    count = len(tiles) * WINDOWS
    stride = count + 1
    lane16 = lax.broadcasted_iota(jnp.int32, (16, LANES), 1)

    def fetch(i):
        rows = pl.ds(pl.multiple_of(i * 16, 16), 16)
        return pltpu.make_async_copy(field_hbm.at[:, rows, :], field.at[:, rows, :], in_sems.at[i])

    def store(i):
        rows = pl.ds(pl.multiple_of(i * 16, 16), 16)
        return pltpu.make_async_copy(windows.at[rows], out_hbm.at[rows], out_sems.at[i])

    for i in range(steps):
        fetch(i).start()

    def step(i, carry):
        fetch(i).wait()
        for m in range(MON_DEV):
            rows = field[m, pl.ds(pl.multiple_of(i * 16, 16), 16), :]
            ring = jnp.concatenate([rows, rows[:, :352]], axis=1)
            for l in range(N_LON):
                start = (LON_DEV * l - HMAX) % NLON
                first_tile, shift = start // LANES, start % LANES
                near = range(tiles[0], tiles[-1] + 2)
                rolled = {t: ring[:, (first_tile + t) * LANES : (first_tile + t + 1) * LANES] for t in near}
                if shift:
                    rolled = {t: pltpu.roll(v, LANES - shift, 1) for t, v in rolled.items()}
                for n, j in enumerate(tiles):
                    piece = jnp.where(lane16 < LANES - shift, rolled[j], rolled[j + 1]) if shift else rolled[j]
                    piece = piece.astype(jnp.float32)
                    for half in range(2):
                        first = half * 8 * stride + n * WINDOWS + m * N_LON + l
                        staged[pl.ds(first, 8, stride=stride), :] = piece[half * 8 : half * 8 + 8]
        for r in range(16):
            windows[i * 16 + r] = staged[r * stride : r * stride + count, :].astype(jnp.bfloat16)
        store(i).start()
        return carry

    lax.fori_loop(0, steps, step, 0)
    for i in range(steps):
        store(i).wait()


def cut_windows(field, tiles):
    steps = NLAT // 16
    count = len(tiles) * WINDOWS
    return pl.pallas_call(
        functools.partial(windows_kernel, tiles),
        out_shape=jax.ShapeDtypeStruct((NLAT, count, LANES), jnp.bfloat16),
        in_specs=[pl.BlockSpec(memory_space=pl.ANY)],
        out_specs=pl.BlockSpec(memory_space=pl.ANY),
        scratch_shapes=[
            pltpu.VMEM((MON_DEV, NLAT, NLON), jnp.bfloat16),
            pltpu.VMEM((NLAT, count, LANES), jnp.bfloat16),
            pltpu.VMEM((16 * (count + 1) + 8, LANES), jnp.float32),
            pltpu.SemaphoreType.DMA((steps,)),
            pltpu.SemaphoreType.DMA((steps,)),
        ],
        compiler_params=pltpu.CompilerParams(vmem_limit_bytes=VMEM_LIMIT),
        cost_estimate=pl.CostEstimate(flops=3000000000, bytes_accessed=9000000, transcendentals=0),
        name="cut_windows",
    )(field)


def build_taps(widths, taps):
    lane8 = lax.broadcasted_iota(jnp.int32, (8, LANES), 1)
    sub8 = lax.broadcasted_iota(jnp.int32, (8, LANES), 0)
    offset = (lane8 - HMAX).astype(jnp.float32)

    def band(b, carry):
        for half in range(2):
            reach = jnp.ones((8, LANES), jnp.int32)
            for s in range(min(8, LAT_DEV - 8 * half)):
                reach = jnp.where(sub8 == s, widths[b, 8 * half + s], reach)
            reach = reach.astype(jnp.float32)
            spread = 0.5 * reach
            value = jnp.exp(-(offset * offset) / (2.0 * spread * spread))
            value = jnp.where(jnp.abs(offset) <= reach, value, 0.0)
            total = jnp.sum(value, axis=1, keepdims=True) + value[:, 0:1]
            value = (value / total).astype(jnp.bfloat16).astype(jnp.float32)
            taps[pl.ds(pl.multiple_of(b * 16 + 8 * half, 8), 8), :] = value
        return carry

    lax.fori_loop(0, N_LAT, band, 0, unroll=4)


def filter_rows(taps, passed, lhs_of, emit, fetch):
    edge = jnp.zeros((HL, WINDOWS, LANES), jnp.float32)
    passed[0:HL] = edge
    passed[NLAT + HL : NLAT + 2 * HL] = edge
    sub = lax.broadcasted_iota(jnp.int32, (LANES, LANES), 0)
    lane = lax.broadcasted_iota(jnp.int32, (LANES, LANES), 1)
    upper = jnp.where(sub >= lane, 1.0, 0.0).astype(jnp.bfloat16)
    lower = jnp.where(sub <= lane, 1.0, 0.0).astype(jnp.bfloat16)
    w0, w1, w2 = lat_taps()[:3]

    def lon_band(b):
        for rr in range(LAT_DEV):
            r = b * LAT_DEV + rr
            spread_taps = jnp.broadcast_to(taps[pl.ds(b * 16 + rr, 1), :], (LANES, LANES))
            ring = pltpu.roll(spread_taps, 0, 1, stride=1, stride_axis=0).astype(jnp.bfloat16)
            right = jnp.concatenate([ring * upper, ring * lower], axis=0)
            res = jnp.dot(lhs_of(r), right, preferred_element_type=jnp.float32)
            passed[r + HL] = res.astype(jnp.bfloat16).astype(jnp.float32)

    def lat_band(b):
        def smoothed(rr):
            r = b * LAT_DEV + rr
            outer = passed[r] + passed[r + 4]
            inner = passed[r + 1] + passed[r + 3]
            return w0 * outer + w1 * inner + w2 * passed[r + 2]

        emit(b, smoothed)

    fetch(0)
    lon_band(0)

    def band(b, carry):
        fetch(b)
        lon_band(b)
        lat_band(b - 1)
        return carry

    lax.fori_loop(1, N_LAT - 1, band, 0)
    lon_band(N_LAT - 1)
    lat_band(N_LAT - 2)
    lat_band(N_LAT - 1)


def chunk_copy(out, out_hbm, sems, b):
    return pltpu.make_async_copy(out.at[:, b], out_hbm.at[:, b], sems.at[b])


def put(staged, groups, g, value):
    for m in range(MON_DEV):
        rows = pl.ds(m * groups + g, N_LON, stride=MON_DEV * groups + 1)
        staged[rows, :] = value[8 * m : 8 * m + 8]


def pack(staged, groups, out, b):
    size = MON_DEV * groups
    for l in range(N_LON):
        out[l, b] = staged[l * (size + 1) : l * (size + 1) + size, :].astype(jnp.bfloat16)


def early_kernel(widths, windows_hbm, out_hbm, extra, taps, windows, out, passed, staged, in_sems, out_sems):
    def fetch(i):
        rows = pl.ds(pl.multiple_of(i * 16, 16), 16)
        return pltpu.make_async_copy(windows_hbm.at[rows], windows.at[rows], in_sems.at[i])

    for i in range(NLAT // 16):
        fetch(i).start()
    build_taps(widths, taps)

    def lhs_of(r):
        both = windows[r]
        return jnp.concatenate([both[:WINDOWS], both[WINDOWS:]], axis=1)

    def emit(b, smoothed):
        for rr in range(EARLY):
            put(staged, EARLY, rr, smoothed(rr))
        for rr in range(EARLY, LAT_DEV):
            extra[b, rr - EARLY] = smoothed(rr).astype(jnp.bfloat16)
        pack(staged, EARLY, out, b)
        chunk_copy(out, out_hbm, out_sems, b).start()

    filter_rows(taps, passed, lhs_of, emit, lambda i: fetch(i).wait())
    for b in range(N_LAT):
        chunk_copy(out, out_hbm, out_sems, b).wait()


def late_kernel(taps, extra, windows_hbm, third_hbm, out_hbm, second, third, out, passed, staged, in_sems, out_sems):
    def fetch(i):
        rows = pl.ds(pl.multiple_of(i * 16, 16), 16)
        middle = windows_hbm.at[rows, WINDOWS : 2 * WINDOWS]
        return (
            pltpu.make_async_copy(middle, second.at[rows], in_sems.at[i, 0]),
            pltpu.make_async_copy(third_hbm.at[rows], third.at[rows], in_sems.at[i, 1]),
        )

    def arrived(i):
        for copy in fetch(i):
            copy.wait()

    for i in range(NLAT // 16):
        for copy in fetch(i):
            copy.start()
    lane = lax.broadcasted_iota(jnp.int32, (WINDOWS, LANES), 1)

    def lhs_of(r):
        return jnp.concatenate([second[r], third[r]], axis=1)

    def emit(b, smoothed):
        for rr in range(EARLY, LAT_DEV):
            put(staged, LATE, rr - EARLY, extra[b, rr - EARLY].astype(jnp.float32))
        last = smoothed(LAT_DEV - 1)
        for q in range(7):
            value = jnp.where(lane < SECOND, smoothed(2 * q), pltpu.roll(smoothed(2 * q + 1), SECOND, 1))
            if q < 4:
                value = jnp.where(lane < TAIL, value, pltpu.roll(last, TAIL - 16 * q, 1))
            put(staged, LATE, LAT_DEV - EARLY + q, value)
        pack(staged, LATE, out, b)
        chunk_copy(out, out_hbm, out_sems, b).start()

    filter_rows(taps, passed, lhs_of, emit, arrived)
    for b in range(N_LAT):
        chunk_copy(out, out_hbm, out_sems, b).wait()


def filter_scratch(groups):
    size = MON_DEV * groups
    return [
        pltpu.VMEM((N_LON, N_LAT, size, LANES), jnp.bfloat16),
        pltpu.VMEM((NLAT + 2 * HL, WINDOWS, LANES), jnp.float32),
        pltpu.VMEM((N_LON * (size + 1) + 8, LANES), jnp.float32),
    ]


def smooth_early(widths, windows):
    pieces, extra, taps = pl.pallas_call(
        early_kernel,
        out_shape=(
            jax.ShapeDtypeStruct((N_LON, N_LAT, MON_DEV * EARLY, LANES), jnp.bfloat16),
            jax.ShapeDtypeStruct((N_LAT, LAT_DEV - EARLY, WINDOWS, LANES), jnp.bfloat16),
            jax.ShapeDtypeStruct((N_LAT * 16, LANES), jnp.float32),
        ),
        in_specs=[pl.BlockSpec(memory_space=pltpu.SMEM), pl.BlockSpec(memory_space=pl.ANY)],
        out_specs=(pl.BlockSpec(memory_space=pl.ANY),) + (pl.BlockSpec(memory_space=pltpu.VMEM),) * 2,
        scratch_shapes=[pltpu.VMEM((NLAT, 2 * WINDOWS, LANES), jnp.bfloat16)]
        + filter_scratch(EARLY)
        + [pltpu.SemaphoreType.DMA((NLAT // 16,)), pltpu.SemaphoreType.DMA((N_LAT,))],
        compiler_params=pltpu.CompilerParams(vmem_limit_bytes=VMEM_LIMIT),
        name="smooth_early",
    )(widths, windows)
    return pieces.reshape(N_LON * N_LAT, MON_DEV * EARLY, LANES), extra, taps


def smooth_late(taps, extra, windows, third):
    pieces = pl.pallas_call(
        late_kernel,
        out_shape=jax.ShapeDtypeStruct((N_LON, N_LAT, MON_DEV * LATE, LANES), jnp.bfloat16),
        in_specs=[pl.BlockSpec(memory_space=pltpu.VMEM)] * 2 + [pl.BlockSpec(memory_space=pl.ANY)] * 2,
        out_specs=pl.BlockSpec(memory_space=pl.ANY),
        scratch_shapes=[pltpu.VMEM((NLAT, WINDOWS, LANES), jnp.bfloat16)] * 2
        + filter_scratch(LATE)
        + [pltpu.SemaphoreType.DMA((NLAT // 16, 2)), pltpu.SemaphoreType.DMA((N_LAT,))],
        compiler_params=pltpu.CompilerParams(vmem_limit_bytes=VMEM_LIMIT),
        cost_estimate=pl.CostEstimate(flops=8000000000, bytes_accessed=9000000, transcendentals=0),
        name="smooth_late",
    )(taps, extra, windows, third)
    return pieces.reshape(N_LON * N_LAT, MON_DEV * LATE, LANES)


def gram_kernel(core, early, late, weight, mine, theirs, anomaly, wide_early, wide_late, square):
    for landed, wide, groups in ((early, wide_early, EARLY), (late, wide_late, LATE)):
        size = MON_DEV * groups

        def widen(s, carry):
            wide[pl.ds(pl.multiple_of(s * size, 8), size), :] = landed[s].astype(jnp.float32)
            return carry

        lax.fori_loop(0, N_LON * N_LAT, widen, 0, unroll=4)
    lane = lax.broadcasted_iota(jnp.int32, (1, LANES), 1)
    for g in range(GROUPS):
        if g < LAT_DEV:
            scale = weight[g : g + 1, :LANES]
        else:
            q = g - LAT_DEV
            scale = weight[2 * q : 2 * q + 1, LANES:]
            scale = scale + pltpu.roll(weight[2 * q + 1 : 2 * q + 2, LANES:], SECOND, 1)
            if q < 4:
                last = weight[LAT_DEV - 1 : LAT_DEV, LANES:]
                last = jnp.where((lane >= 16 * q) & (lane < 16 * q + 16), last, 0.0)
                scale = scale + pltpu.roll(last, TAIL - 16 * q, 1)
        if g < EARLY:
            cells = wide_early[pl.ds(g, MONTHS, stride=EARLY), :]
        else:
            cells = wide_late[pl.ds(g - EARLY, MONTHS, stride=LATE), :]
        mean = jnp.sum(cells, axis=0, keepdims=True) * (1.0 / MONTHS)
        anomaly[:, g * LANES : (g + 1) * LANES] = ((cells - mean) * scale).astype(jnp.bfloat16)
    for i, j in ((0, 0), (0, 1), (1, 1)):
        block = lax.dot_general(
            anomaly[i * ROWB : (i + 1) * ROWB, :],
            anomaly[j * ROWB : (j + 1) * ROWB, :],
            (((1,), (1,)), ((), ())),
            preferred_element_type=jnp.float32,
        )
        for n, (bi, bj) in enumerate(BLOCKS):
            if bi // 2 == i and bj // 2 == j:
                a, c = (bi % 2) * LANES, (bj % 2) * LANES
                square[...] = block[a : a + LANES, c : c + LANES]
                for ref, half in ((mine, core[0]), (theirs, 1 - core[0])):
                    rows = pl.ds(pl.multiple_of(half * HALF, HALF), HALF)
                    ref[pl.ds(n, HALF, stride=PACK), :] = square[rows, :]


def gram_terms(core, early, late, weight):
    part = jax.ShapeDtypeStruct((HALF * PACK, LANES), jnp.float32)
    return pl.pallas_call(
        gram_kernel,
        out_shape=(part, part, jax.ShapeDtypeStruct((MONTHS, GROUPS * LANES), jnp.bfloat16)),
        in_specs=[
            pl.BlockSpec(memory_space=pltpu.SMEM),
            pl.BlockSpec(memory_space=pltpu.VMEM),
            pl.BlockSpec(memory_space=pltpu.VMEM),
            pl.BlockSpec(memory_space=pltpu.VMEM),
        ],
        out_specs=(pl.BlockSpec(memory_space=pltpu.VMEM),) * 3,
        scratch_shapes=[
            pltpu.VMEM((MONTHS * EARLY, LANES), jnp.float32),
            pltpu.VMEM((MONTHS * LATE, LANES), jnp.float32),
            pltpu.VMEM((LANES, LANES), jnp.float32),
        ],
        compiler_params=pltpu.CompilerParams(vmem_limit_bytes=32 * 1024 * 1024),
        name="gram_terms",
    )(core, early, late, weight)


def turn_kernel(anomaly, turned):
    for g in range(GROUPS):
        turned[g * LANES : (g + 1) * LANES, :] = anomaly[:, g * LANES : (g + 1) * LANES].T


def turn(anomaly):
    return pl.pallas_call(
        turn_kernel,
        out_shape=jax.ShapeDtypeStruct((GROUPS * LANES, MONTHS), jnp.bfloat16),
        in_specs=[pl.BlockSpec(memory_space=pltpu.VMEM)],
        out_specs=pl.BlockSpec(memory_space=pltpu.VMEM),
        compiler_params=pltpu.CompilerParams(vmem_limit_bytes=16 * 1024 * 1024),
        cost_estimate=pl.CostEstimate(flops=2000000000, bytes_accessed=6000000, transcendentals=0),
        name="turn",
    )(anomaly)


def add_kernel(terms, out):
    step = 4 * PACK
    total = terms[0:step, :]
    for s in range(1, HALF // 4):
        total = total + terms[s * step : (s + 1) * step, :]
    row = total[0:PACK] + total[PACK : 2 * PACK] + total[2 * PACK : 3 * PACK] + total[3 * PACK :]
    total = jnp.concatenate([row] * 4, axis=0)
    for s in range(HALF // 4):
        out[s * step : (s + 1) * step, :] = total


def add_terms(terms):
    return pl.pallas_call(
        add_kernel,
        out_shape=jax.ShapeDtypeStruct(terms.shape, jnp.float32),
        in_specs=[pl.BlockSpec(memory_space=pltpu.VMEM)],
        out_specs=pl.BlockSpec(memory_space=pltpu.VMEM),
        compiler_params=pltpu.CompilerParams(vmem_limit_bytes=8 * 1024 * 1024),
        name="add_terms",
    )(terms)


STEP = (2.25, -2.4375, 1.6875, -0.5625, 0.0625)
ROWB = 256
MIRROR = True


def root_kernel(core, mine, theirs, anomaly, patterns_hbm, whitener_hbm, patterns, whitener, ws, hs, ps, ss, zs, wb, out_sems):
    for n, (bi, bj) in enumerate(BLOCKS):
        for ref, half in ((mine, core[0]), (theirs, 1 - core[0])):
            rows = pl.ds(pl.multiple_of(bi * LANES + half * HALF, HALF), HALF)
            whitener[rows, bj * LANES : (bj + 1) * LANES] = ref[pl.ds(n, HALF, stride=PACK), :]
        if bi != bj:
            block = whitener[bi * LANES : (bi + 1) * LANES, bj * LANES : (bj + 1) * LANES]
            whitener[bj * LANES : (bj + 1) * LANES, bi * LANES : (bi + 1) * LANES] = block.T
    gram = whitener[...]
    squares = jnp.sum(gram * gram, axis=0, keepdims=True)
    frobenius = jnp.sqrt(jnp.sum(squares, axis=1, keepdims=True) + 1e-06)
    final_scale = jnp.sqrt(float(NLAT * NLON) / frobenius)

    def split(ref, start, value):
        size = value.shape[0]
        high = value.astype(jnp.bfloat16)
        ref[start : start + size, :] = high
        ref[MONTHS + start : MONTHS + start + size, :] = (value - high.astype(jnp.float32)).astype(jnp.bfloat16)
        if ref.shape[0] == 3 * MONTHS:
            ref[2 * MONTHS + start : 2 * MONTHS + start + size, :] = high

    def join(ref, start):
        high = ref[start : start + ROWB, :].astype(jnp.float32)
        return high + ref[MONTHS + start : MONTHS + start + ROWB, :].astype(jnp.float32)

    def product(left, right):
        def rows(start):
            high = left[start : start + ROWB, :]
            low = left[MONTHS + start : MONTHS + start + ROWB, :]
            return jnp.concatenate([high, high, low], axis=1)

        upper = jnp.dot(rows(0), right[...], preferred_element_type=jnp.float32)
        if not MIRROR:
            return upper, jnp.dot(rows(ROWB), right[...], preferred_element_type=jnp.float32)
        corner = jnp.dot(rows(ROWB), right[:, ROWB:], preferred_element_type=jnp.float32)
        return upper, jnp.concatenate([upper[:, ROWB:].T, corner], axis=1)

    def plus_eye(value, start, scale):
        row = lax.broadcasted_iota(jnp.int32, value.shape, 0) + start
        column = lax.broadcasted_iota(jnp.int32, value.shape, 1)
        return jnp.where(row == column, value + scale, value)

    split(ws, 0, gram / frobenius)
    c0, c1, c2, c3, c4 = STEP
    last = ITERS // 2 - 1

    def double_step(k):
        for n, square in enumerate(product(ws, ws)):
            start = n * ROWB
            split(ss, start, square)
            split(hs, start, plus_eye(c3 * join(ws, start) + c4 * square, start, c2))
        for n, value in enumerate(product(ss, hs)):
            start = n * ROWB
            split(ps, start, plus_eye(value + c1 * join(ws, start), start, c0))

        if k == 0:
            zs[...] = ps[0 : 2 * MONTHS, :]

        if k > 0:
            for n, value in enumerate(product(zs, ps)):
                split(zs, n * ROWB, value)
                whitener[n * ROWB : (n + 1) * ROWB, :] = value * final_scale

        if k < last:
            for n, value in enumerate(product(ws, ps)):
                split(ss, n * ROWB, value)
            for n, value in enumerate(product(ss, ps)):
                split(ws, n * ROWB, value)

    for k in range(last + 1):
        double_step(k)
    copies = [pltpu.make_async_copy(whitener, whitener_hbm, out_sems.at[LAT_DEV])]
    copies[0].start()
    wb[...] = whitener[...].astype(jnp.bfloat16)

    def group(g):
        return lax.dot_general(
            anomaly[g * LANES : (g + 1) * LANES, :],
            wb[...],
            (((1,), (0,)), ((), ())),
            preferred_element_type=jnp.float32,
        ).astype(jnp.bfloat16)

    def finish(r):
        copy = pltpu.make_async_copy(patterns.at[r], patterns_hbm.at[r], out_sems.at[r])
        copy.start()
        copies.append(copy)

    for q in range(7):
        value = group(LAT_DEV + q)
        patterns[2 * q, LANES:, :] = value[0 : LON_DEV - LANES]
        patterns[2 * q + 1, LANES:, :] = value[SECOND : SECOND + LON_DEV - LANES]
        if q < 4:
            first = LANES + 16 * q
            size = min(16, LON_DEV - first)
            patterns[LAT_DEV - 1, first : first + size, :] = value[TAIL : TAIL + size]
        for r in (2 * q, 2 * q + 1):
            patterns[r, 0:LANES, :] = group(r)
            finish(r)
    patterns[LAT_DEV - 1, 0:LANES, :] = group(LAT_DEV - 1)
    finish(LAT_DEV - 1)
    for copy in copies:
        copy.wait()


def root_and_patterns(core, mine, theirs, turned):
    return pl.pallas_call(
        root_kernel,
        out_shape=(
            jax.ShapeDtypeStruct((LAT_DEV, LON_DEV, MONTHS), jnp.bfloat16),
            jax.ShapeDtypeStruct((MONTHS, MONTHS), jnp.float32),
        ),
        in_specs=[
            pl.BlockSpec(memory_space=pltpu.SMEM),
            pl.BlockSpec(memory_space=pltpu.VMEM),
            pl.BlockSpec(memory_space=pltpu.VMEM),
            pl.BlockSpec(memory_space=pltpu.VMEM),
        ],
        out_specs=(pl.BlockSpec(memory_space=pl.ANY),) * 2,
        scratch_shapes=[
            pltpu.VMEM((LAT_DEV, LON_DEV, MONTHS), jnp.bfloat16),
            pltpu.VMEM((MONTHS, MONTHS), jnp.float32),
            pltpu.VMEM((3 * MONTHS, MONTHS), jnp.bfloat16),
            pltpu.VMEM((3 * MONTHS, MONTHS), jnp.bfloat16),
            pltpu.VMEM((3 * MONTHS, MONTHS), jnp.bfloat16),
            pltpu.VMEM((2 * MONTHS, MONTHS), jnp.bfloat16),
            pltpu.VMEM((2 * MONTHS, MONTHS), jnp.bfloat16),
            pltpu.VMEM((MONTHS, MONTHS), jnp.bfloat16),
            pltpu.SemaphoreType.DMA((LAT_DEV + 1,)),
        ],
        compiler_params=pltpu.CompilerParams(vmem_limit_bytes=32 * 1024 * 1024),
        name="root_and_patterns",
    )(core, mine, theirs, turned)


def exchange(pieces, axes):
    return lax.all_to_all(pieces, axes, split_axis=0, concat_axis=0, tiled=True)


def exchange_packed(packed):
    pieces = packed.reshape(HALF, PACK // 2, 2, LANES)
    return exchange(pieces, SAME_CORE).reshape(packed.shape)


def swap_cores(x):
    return lax.ppermute(x, "core", [(0, 1), (1, 0)])


def local(monthly_field, half_width, land_mask):
    widths = exchange(jnp.broadcast_to(half_width, (N_LAT, 1, LAT_DEV)), LAT).reshape(N_LAT, LAT_DEV)
    windows = cut_windows(monthly_field, (0, 1))
    pieces, extra, taps = smooth_early(widths, windows)
    early = exchange(pieces, BOTH)
    field, extra = lax.optimization_barrier((monthly_field, extra))
    third = cut_windows(field, (2,))
    pieces = smooth_late(taps, extra, windows, third)
    early, pieces = lax.optimization_barrier((early, pieces))
    late = exchange(pieces, BOTH)
    row_index = lax.axis_index(LAT) * LAT_DEV + jnp.arange(LAT_DEV)
    latitude = math.pi * ((row_index.astype(jnp.float32) + 0.5) / NLAT - 0.5)
    weight = jnp.sqrt(jnp.cos(latitude))[:, None] * land_mask.astype(jnp.float32)
    weight = jnp.pad(weight, ((0, 0), (0, 2 * LANES - LON_DEV)))
    core = lax.axis_index("core").reshape(1)
    mine, theirs, anomaly = gram_terms(core, early, late, weight)
    terms = exchange_packed(mine + swap_cores(theirs))
    turned = turn(anomaly)
    mine = exchange_packed(add_terms(terms))
    patterns, whitener = root_and_patterns(core, mine, swap_cores(mine), turned)
    return (jnp.transpose(patterns, (2, 0, 1)), whitener)


def solution(mesh):
    fine = Mesh(mesh.devices.reshape(N_LON, N_LAT // 2, 2), BOTH)
    placed = (P(BOTH, None, None), P(LAT), P(LAT, "lon"))
    return jax.shard_map(
        local, mesh=fine, in_specs=placed, out_specs=(P(None, LAT, "lon"), P()), check_vma=False
    )
```

```python
import math

import jax
import jax.numpy as jnp
import numpy as np
from jax import lax
from jax.experimental import pallas as pl
from jax.experimental.pallas import tpu as pltpu
from jax.sharding import Mesh
from jax.sharding import PartitionSpec as P

HMAX = 64
HL = 2
ITERS = 8
LAT = ("chip", "core")
BOTH = ("lon", "chip", "core")
SAME_CORE = ("lon", "chip")
HALF = 64
N_LON = 8
N_LAT = 16
NLAT = 240
NLON = 1440
MONTHS = 512
MON_DEV = 4
LAT_DEV = 15
LON_DEV = 180
LANES = 128
GROUPS = 22
SECOND = 56
TAIL = 112
CHUNK = MON_DEV * GROUPS
WINDOWS = MON_DEV * N_LON
SROWS = 3 * WINDOWS
SSTRIDE = 97
VSTRIDE = 89
BLOCKS = [(i, j) for i in range(4) for j in range(i, 4)]
PACK = len(BLOCKS)
VMEM_LIMIT = 60 * 1024 * 1024


def lat_taps():
    offsets = np.arange(-HL, HL + 1).astype(np.float32)
    taps = np.exp(-(offsets * offsets) / np.float32(2.0)).astype(np.float32)
    taps = taps / taps.sum(dtype=np.float32)
    return [float(t) for t in taps.astype(jnp.bfloat16).astype(np.float32)]


def windows_kernel(field_hbm, out_hbm, field, windows, staged, in_sems, out_sems):
    steps = windows.shape[0] // 16
    lane16 = lax.broadcasted_iota(jnp.int32, (16, LANES), 1)

    def fetch(i):
        rows = pl.ds(pl.multiple_of(i * 16, 16), 16)
        return pltpu.make_async_copy(field_hbm.at[:, rows, :], field.at[:, rows, :], in_sems.at[i])

    def store(i):
        rows = pl.ds(pl.multiple_of(i * 16, 16), 16)
        return pltpu.make_async_copy(windows.at[rows], out_hbm.at[rows], out_sems.at[i])

    for i in range(steps):
        fetch(i).start()

    def step(i, carry):
        fetch(i).wait()
        for m in range(MON_DEV):
            rows = field[m, pl.ds(pl.multiple_of(i * 16, 16), 16), :]
            ring = jnp.concatenate([rows, rows[:, :352]], axis=1)
            for l in range(N_LON):
                start = (LON_DEV * l - HMAX) % NLON
                first_tile, shift = start // LANES, start % LANES
                tiles = [ring[:, t * LANES : (t + 1) * LANES] for t in range(first_tile, first_tile + 4)]
                if shift:
                    tiles = [pltpu.roll(t, LANES - shift, 1) for t in tiles]
                for j in range(3):
                    piece = jnp.where(lane16 < LANES - shift, tiles[j], tiles[j + 1]) if shift else tiles[j]
                    piece = piece.astype(jnp.float32)
                    for half in range(2):
                        first = half * 8 * SSTRIDE + j * WINDOWS + m * N_LON + l
                        staged[pl.ds(first, 8, stride=SSTRIDE), :] = piece[half * 8 : half * 8 + 8]
        for r in range(16):
            windows[i * 16 + r] = staged[r * SSTRIDE : r * SSTRIDE + SROWS, :].astype(jnp.bfloat16)
        store(i).start()
        return carry

    lax.fori_loop(0, steps, step, 0)
    for i in range(steps):
        store(i).wait()


def cut_windows(field):
    steps = NLAT // 16
    return pl.pallas_call(
        windows_kernel,
        out_shape=jax.ShapeDtypeStruct((steps * 16, SROWS, LANES), jnp.bfloat16),
        in_specs=[pl.BlockSpec(memory_space=pl.ANY)],
        out_specs=pl.BlockSpec(memory_space=pl.ANY),
        scratch_shapes=[
            pltpu.VMEM((MON_DEV, steps * 16, NLON), jnp.bfloat16),
            pltpu.VMEM((steps * 16, SROWS, LANES), jnp.bfloat16),
            pltpu.VMEM((16 * SSTRIDE + 8, LANES), jnp.float32),
            pltpu.SemaphoreType.DMA((steps,)),
            pltpu.SemaphoreType.DMA((steps,)),
        ],
        compiler_params=pltpu.CompilerParams(vmem_limit_bytes=VMEM_LIMIT),
        cost_estimate=pl.CostEstimate(flops=3000000000, bytes_accessed=9000000, transcendentals=0),
        name="cut_windows",
    )(field)


def smooth_kernel(widths, windows_hbm, out_hbm, windows, out, taps, table, passed, staged, in_sems, out_sems):

    def fetch(i):
        rows = pl.ds(pl.multiple_of(i * 16, 16), 16)
        return pltpu.make_async_copy(windows_hbm.at[rows], windows.at[rows], in_sems.at[i])

    def store(b):
        return pltpu.make_async_copy(out.at[:, b], out_hbm.at[:, b], out_sems.at[b])

    for i in range(NLAT // 16):
        fetch(i).start()
    reach = (lax.broadcasted_iota(jnp.int32, (HMAX, LANES), 0) + 1).astype(jnp.float32)
    offset = (lax.broadcasted_iota(jnp.int32, (HMAX, LANES), 1) - HMAX).astype(jnp.float32)
    spread = 0.5 * reach
    value = jnp.exp(-(offset * offset) / (2.0 * spread * spread))
    value = jnp.where(jnp.abs(offset) <= reach, value, 0.0)
    total = jnp.sum(value, axis=1, keepdims=True) + value[:, 0:1]
    taps[...] = (value / total).astype(jnp.bfloat16).astype(jnp.float32)
    sub = lax.broadcasted_iota(jnp.int32, (LANES, LANES), 0)
    lane = lax.broadcasted_iota(jnp.int32, (LANES, LANES), 1)
    upper = jnp.where(sub >= lane, 1.0, 0.0).astype(jnp.bfloat16)
    lower = jnp.where(sub <= lane, 1.0, 0.0).astype(jnp.bfloat16)

    def build_matrix(h, carry):
        spread_taps = jnp.broadcast_to(taps[pl.ds(h, 1), :], (LANES, LANES))
        ring = pltpu.roll(spread_taps, 0, 1, stride=1, stride_axis=0).astype(jnp.bfloat16)
        table[h, 0:LANES, :] = ring * upper
        table[h, LANES:, :] = ring * lower
        return carry

    lax.fori_loop(0, HMAX, build_matrix, 0, unroll=8)
    edge = jnp.zeros((HL, 2 * WINDOWS, LANES), jnp.float32)
    passed[0:HL] = edge
    passed[NLAT + HL : NLAT + 2 * HL] = edge

    def lon_band(b):
        for rr in range(LAT_DEV):
            r = b * LAT_DEV + rr
            lhs = windows[r]
            left = jnp.concatenate([lhs[: 2 * WINDOWS], lhs[WINDOWS:]], axis=1)
            right = table[widths[b, rr] - 1]
            res = jnp.dot(left, right, preferred_element_type=jnp.float32)
            passed[r + HL] = res.astype(jnp.bfloat16).astype(jnp.float32)

    w0, w1, w2 = lat_taps()[:3]
    laneb = lax.broadcasted_iota(jnp.int32, (WINDOWS, LANES), 1)

    def lat_band(b):
        def smoothed(rr, lo, hi):
            r = b * LAT_DEV + rr
            outer = passed[r, lo:hi] + passed[r + 4, lo:hi]
            inner = passed[r + 1, lo:hi] + passed[r + 3, lo:hi]
            return w0 * outer + w1 * inner + w2 * passed[r + 2, lo:hi]

        def put(g, value):
            for m in range(MON_DEV):
                staged[pl.ds(m * GROUPS + g, N_LON, stride=VSTRIDE), :] = value[8 * m : 8 * m + 8]

        for rr in range(LAT_DEV):
            put(rr, smoothed(rr, 0, WINDOWS))
        last = smoothed(LAT_DEV - 1, WINDOWS, 2 * WINDOWS)
        for q in range(7):
            even = smoothed(2 * q, WINDOWS, 2 * WINDOWS)
            odd = smoothed(2 * q + 1, WINDOWS, 2 * WINDOWS)
            value = jnp.where(laneb < SECOND, even, pltpu.roll(odd, SECOND, 1))
            if q < 4:
                tail = pltpu.roll(last, TAIL - 16 * q, 1)
                value = jnp.where(laneb < TAIL, value, tail)
            put(LAT_DEV + q, value)
        for l in range(N_LON):
            out[l, b] = staged[l * VSTRIDE : l * VSTRIDE + CHUNK, :].astype(jnp.bfloat16)

    fetch(0).wait()
    lon_band(0)

    def band(b, carry):
        fetch(b).wait()
        lon_band(b)
        lat_band(b - 1)
        store(b - 1).start()
        return carry

    lax.fori_loop(1, N_LAT - 1, band, 0)
    lon_band(N_LAT - 1)
    for b in (N_LAT - 2, N_LAT - 1):
        lat_band(b)
        store(b).start()
    for b in range(N_LAT):
        store(b).wait()


def smooth(widths, windows):
    out = pl.pallas_call(
        smooth_kernel,
        out_shape=jax.ShapeDtypeStruct((N_LON, N_LAT, CHUNK, LANES), jnp.bfloat16),
        in_specs=[pl.BlockSpec(memory_space=pltpu.SMEM), pl.BlockSpec(memory_space=pl.ANY)],
        out_specs=pl.BlockSpec(memory_space=pl.ANY),
        scratch_shapes=[
            pltpu.VMEM((NLAT, SROWS, LANES), jnp.bfloat16),
            pltpu.VMEM((N_LON, N_LAT, CHUNK, LANES), jnp.bfloat16),
            pltpu.VMEM((HMAX, LANES), jnp.float32),
            pltpu.VMEM((HMAX, 2 * LANES, LANES), jnp.bfloat16),
            pltpu.VMEM((NLAT + 2 * HL, 2 * WINDOWS, LANES), jnp.float32),
            pltpu.VMEM((N_LON * VSTRIDE + 8, LANES), jnp.float32),
            pltpu.SemaphoreType.DMA((NLAT // 16,)),
            pltpu.SemaphoreType.DMA((N_LAT,)),
        ],
        compiler_params=pltpu.CompilerParams(vmem_limit_bytes=VMEM_LIMIT),
        name="smooth",
    )(widths, windows)
    return out.reshape(N_LON * N_LAT, CHUNK, LANES)


def gram_kernel(core, landed, weight, mine, theirs, anomaly, wide, square):
    def widen(s, carry):
        wide[pl.ds(pl.multiple_of(s * CHUNK, 8), CHUNK), :] = landed[s].astype(jnp.float32)
        return carry

    lax.fori_loop(0, N_LON * N_LAT, widen, 0, unroll=4)
    lane = lax.broadcasted_iota(jnp.int32, (1, LANES), 1)
    for g in range(GROUPS):
        if g < LAT_DEV:
            scale = weight[g : g + 1, :LANES]
        else:
            q = g - LAT_DEV
            scale = weight[2 * q : 2 * q + 1, LANES:]
            scale = scale + pltpu.roll(weight[2 * q + 1 : 2 * q + 2, LANES:], SECOND, 1)
            if q < 4:
                last = weight[LAT_DEV - 1 : LAT_DEV, LANES:]
                last = jnp.where((lane >= 16 * q) & (lane < 16 * q + 16), last, 0.0)
                scale = scale + pltpu.roll(last, TAIL - 16 * q, 1)
        cells = wide[pl.ds(g, MONTHS, stride=GROUPS), :]
        mean = jnp.sum(cells, axis=0, keepdims=True) * (1.0 / MONTHS)
        anomaly[:, g * LANES : (g + 1) * LANES] = ((cells - mean) * scale).astype(jnp.bfloat16)
    for i, j in ((0, 0), (0, 1), (1, 1)):
        block = lax.dot_general(
            anomaly[i * ROWB : (i + 1) * ROWB, :],
            anomaly[j * ROWB : (j + 1) * ROWB, :],
            (((1,), (1,)), ((), ())),
            preferred_element_type=jnp.float32,
        )
        for n, (bi, bj) in enumerate(BLOCKS):
            if bi // 2 == i and bj // 2 == j:
                a, c = (bi % 2) * LANES, (bj % 2) * LANES
                square[...] = block[a : a + LANES, c : c + LANES]
                for ref, half in ((mine, core[0]), (theirs, 1 - core[0])):
                    rows = pl.ds(pl.multiple_of(half * HALF, HALF), HALF)
                    ref[pl.ds(n, HALF, stride=PACK), :] = square[rows, :]


def gram_terms(core, landed, weight):
    part = jax.ShapeDtypeStruct((HALF * PACK, LANES), jnp.float32)
    return pl.pallas_call(
        gram_kernel,
        out_shape=(part, part, jax.ShapeDtypeStruct((MONTHS, GROUPS * LANES), jnp.bfloat16)),
        in_specs=[
            pl.BlockSpec(memory_space=pltpu.SMEM),
            pl.BlockSpec(memory_space=pltpu.VMEM),
            pl.BlockSpec(memory_space=pltpu.VMEM),
        ],
        out_specs=(pl.BlockSpec(memory_space=pltpu.VMEM),) * 3,
        scratch_shapes=[
            pltpu.VMEM((N_LON * N_LAT * CHUNK, LANES), jnp.float32),
            pltpu.VMEM((LANES, LANES), jnp.float32),
        ],
        compiler_params=pltpu.CompilerParams(vmem_limit_bytes=32 * 1024 * 1024),
        name="gram_terms",
    )(core, landed, weight)


def turn_kernel(anomaly, turned):
    for g in range(GROUPS):
        turned[g * LANES : (g + 1) * LANES, :] = anomaly[:, g * LANES : (g + 1) * LANES].T


def turn(anomaly):
    return pl.pallas_call(
        turn_kernel,
        out_shape=jax.ShapeDtypeStruct((GROUPS * LANES, MONTHS), jnp.bfloat16),
        in_specs=[pl.BlockSpec(memory_space=pltpu.VMEM)],
        out_specs=pl.BlockSpec(memory_space=pltpu.VMEM),
        compiler_params=pltpu.CompilerParams(vmem_limit_bytes=16 * 1024 * 1024),
        cost_estimate=pl.CostEstimate(flops=2000000000, bytes_accessed=6000000, transcendentals=0),
        name="turn",
    )(anomaly)


def add_kernel(terms, out):
    step = 4 * PACK
    total = terms[0:step, :]
    for s in range(1, HALF // 4):
        total = total + terms[s * step : (s + 1) * step, :]
    row = total[0:PACK] + total[PACK : 2 * PACK] + total[2 * PACK : 3 * PACK] + total[3 * PACK :]
    total = jnp.concatenate([row] * 4, axis=0)
    for s in range(HALF // 4):
        out[s * step : (s + 1) * step, :] = total


def add_terms(terms):
    return pl.pallas_call(
        add_kernel,
        out_shape=jax.ShapeDtypeStruct(terms.shape, jnp.float32),
        in_specs=[pl.BlockSpec(memory_space=pltpu.VMEM)],
        out_specs=pl.BlockSpec(memory_space=pltpu.VMEM),
        compiler_params=pltpu.CompilerParams(vmem_limit_bytes=8 * 1024 * 1024),
        name="add_terms",
    )(terms)


STEP = (2.25, -2.4375, 1.6875, -0.5625, 0.0625)
ROWB = 256
MIRROR = True


def root_kernel(core, mine, theirs, anomaly, patterns_hbm, whitener_hbm, patterns, whitener, ws, hs, ps, ss, zs, wb, out_sems):
    for n, (bi, bj) in enumerate(BLOCKS):
        for ref, half in ((mine, core[0]), (theirs, 1 - core[0])):
            rows = pl.ds(pl.multiple_of(bi * LANES + half * HALF, HALF), HALF)
            whitener[rows, bj * LANES : (bj + 1) * LANES] = ref[pl.ds(n, HALF, stride=PACK), :]
        if bi != bj:
            block = whitener[bi * LANES : (bi + 1) * LANES, bj * LANES : (bj + 1) * LANES]
            whitener[bj * LANES : (bj + 1) * LANES, bi * LANES : (bi + 1) * LANES] = block.T
    gram = whitener[...]
    squares = jnp.sum(gram * gram, axis=0, keepdims=True)
    frobenius = jnp.sqrt(jnp.sum(squares, axis=1, keepdims=True) + 1e-06)
    final_scale = jnp.sqrt(float(NLAT * NLON) / frobenius)

    def split(ref, start, value):
        size = value.shape[0]
        high = value.astype(jnp.bfloat16)
        ref[start : start + size, :] = high
        ref[MONTHS + start : MONTHS + start + size, :] = (value - high.astype(jnp.float32)).astype(jnp.bfloat16)
        if ref.shape[0] == 3 * MONTHS:
            ref[2 * MONTHS + start : 2 * MONTHS + start + size, :] = high

    def join(ref, start):
        high = ref[start : start + ROWB, :].astype(jnp.float32)
        return high + ref[MONTHS + start : MONTHS + start + ROWB, :].astype(jnp.float32)

    def product(left, right):
        def rows(start):
            high = left[start : start + ROWB, :]
            low = left[MONTHS + start : MONTHS + start + ROWB, :]
            return jnp.concatenate([high, high, low], axis=1)

        upper = jnp.dot(rows(0), right[...], preferred_element_type=jnp.float32)
        if not MIRROR:
            return upper, jnp.dot(rows(ROWB), right[...], preferred_element_type=jnp.float32)
        corner = jnp.dot(rows(ROWB), right[:, ROWB:], preferred_element_type=jnp.float32)
        return upper, jnp.concatenate([upper[:, ROWB:].T, corner], axis=1)

    def plus_eye(value, start, scale):
        row = lax.broadcasted_iota(jnp.int32, value.shape, 0) + start
        column = lax.broadcasted_iota(jnp.int32, value.shape, 1)
        return jnp.where(row == column, value + scale, value)

    split(ws, 0, gram / frobenius)
    c0, c1, c2, c3, c4 = STEP
    last = ITERS // 2 - 1

    def double_step(k):
        for n, square in enumerate(product(ws, ws)):
            start = n * ROWB
            split(ss, start, square)
            split(hs, start, plus_eye(c3 * join(ws, start) + c4 * square, start, c2))
        for n, value in enumerate(product(ss, hs)):
            start = n * ROWB
            split(ps, start, plus_eye(value + c1 * join(ws, start), start, c0))

        if k == 0:
            zs[...] = ps[0 : 2 * MONTHS, :]

        if k > 0:
            for n, value in enumerate(product(zs, ps)):
                split(zs, n * ROWB, value)
                whitener[n * ROWB : (n + 1) * ROWB, :] = value * final_scale

        if k < last:
            for n, value in enumerate(product(ws, ps)):
                split(ss, n * ROWB, value)
            for n, value in enumerate(product(ss, ps)):
                split(ws, n * ROWB, value)

    for k in range(last + 1):
        double_step(k)
    copies = [pltpu.make_async_copy(whitener, whitener_hbm, out_sems.at[LAT_DEV])]
    copies[0].start()
    wb[...] = whitener[...].astype(jnp.bfloat16)

    def group(g):
        return lax.dot_general(
            anomaly[g * LANES : (g + 1) * LANES, :],
            wb[...],
            (((1,), (0,)), ((), ())),
            preferred_element_type=jnp.float32,
        ).astype(jnp.bfloat16)

    def finish(r):
        copy = pltpu.make_async_copy(patterns.at[r], patterns_hbm.at[r], out_sems.at[r])
        copy.start()
        copies.append(copy)

    for q in range(7):
        value = group(LAT_DEV + q)
        patterns[2 * q, LANES:, :] = value[0 : LON_DEV - LANES]
        patterns[2 * q + 1, LANES:, :] = value[SECOND : SECOND + LON_DEV - LANES]
        if q < 4:
            first = LANES + 16 * q
            size = min(16, LON_DEV - first)
            patterns[LAT_DEV - 1, first : first + size, :] = value[TAIL : TAIL + size]
        for r in (2 * q, 2 * q + 1):
            patterns[r, 0:LANES, :] = group(r)
            finish(r)
    patterns[LAT_DEV - 1, 0:LANES, :] = group(LAT_DEV - 1)
    finish(LAT_DEV - 1)
    for copy in copies:
        copy.wait()


def root_and_patterns(core, mine, theirs, turned):
    return pl.pallas_call(
        root_kernel,
        out_shape=(
            jax.ShapeDtypeStruct((LAT_DEV, LON_DEV, MONTHS), jnp.bfloat16),
            jax.ShapeDtypeStruct((MONTHS, MONTHS), jnp.float32),
        ),
        in_specs=[
            pl.BlockSpec(memory_space=pltpu.SMEM),
            pl.BlockSpec(memory_space=pltpu.VMEM),
            pl.BlockSpec(memory_space=pltpu.VMEM),
            pl.BlockSpec(memory_space=pltpu.VMEM),
        ],
        out_specs=(pl.BlockSpec(memory_space=pl.ANY),) * 2,
        scratch_shapes=[
            pltpu.VMEM((LAT_DEV, LON_DEV, MONTHS), jnp.bfloat16),
            pltpu.VMEM((MONTHS, MONTHS), jnp.float32),
            pltpu.VMEM((3 * MONTHS, MONTHS), jnp.bfloat16),
            pltpu.VMEM((3 * MONTHS, MONTHS), jnp.bfloat16),
            pltpu.VMEM((3 * MONTHS, MONTHS), jnp.bfloat16),
            pltpu.VMEM((2 * MONTHS, MONTHS), jnp.bfloat16),
            pltpu.VMEM((2 * MONTHS, MONTHS), jnp.bfloat16),
            pltpu.VMEM((MONTHS, MONTHS), jnp.bfloat16),
            pltpu.SemaphoreType.DMA((LAT_DEV + 1,)),
        ],
        compiler_params=pltpu.CompilerParams(vmem_limit_bytes=32 * 1024 * 1024),
        name="root_and_patterns",
    )(core, mine, theirs, turned)


def exchange(pieces, axes):
    return lax.all_to_all(pieces, axes, split_axis=0, concat_axis=0, tiled=True)


def exchange_packed(packed):
    pieces = packed.reshape(HALF, PACK // 2, 2, LANES)
    return exchange(pieces, SAME_CORE).reshape(packed.shape)


def swap_cores(x):
    return lax.ppermute(x, "core", [(0, 1), (1, 0)])


def local(monthly_field, half_width, land_mask):
    widths = exchange(jnp.broadcast_to(half_width, (N_LAT, 1, LAT_DEV)), LAT).reshape(N_LAT, LAT_DEV)
    windows = cut_windows(monthly_field)
    landed = exchange(smooth(widths, windows), BOTH)
    row_index = lax.axis_index(LAT) * LAT_DEV + jnp.arange(LAT_DEV)
    latitude = math.pi * ((row_index.astype(jnp.float32) + 0.5) / NLAT - 0.5)
    weight = jnp.sqrt(jnp.cos(latitude))[:, None] * land_mask.astype(jnp.float32)
    weight = jnp.pad(weight, ((0, 0), (0, 2 * LANES - LON_DEV)))
    core = lax.axis_index("core").reshape(1)
    mine, theirs, anomaly = gram_terms(core, landed, weight)
    terms = exchange_packed(mine + swap_cores(theirs))
    turned = turn(anomaly)
    mine = exchange_packed(add_terms(terms))
    patterns, whitener = root_and_patterns(core, mine, swap_cores(mine), turned)
    return (jnp.transpose(patterns, (2, 0, 1)), whitener)


def solution(mesh):
    fine = Mesh(mesh.devices.reshape(N_LON, N_LAT // 2, 2), BOTH)
    placed = (P(BOTH, None, None), P(LAT), P(LAT, "lon"))
    return jax.shard_map(
        local, mesh=fine, in_specs=placed, out_specs=(P(None, LAT, "lon"), P()), check_vma=False
    )
```

```python
import math

import jax
import jax.numpy as jnp
import numpy as np
from jax import lax
from jax.experimental import pallas as pl
from jax.experimental.pallas import tpu as pltpu
from jax.sharding import Mesh
from jax.sharding import PartitionSpec as P

HMAX = 64
HL = 2
ITERS = 8
LAT = ("chip", "core")
BOTH = ("lon", "chip", "core")
SAME_CORE = ("lon", "chip")
HALF = 64
N_LON = 8
N_LAT = 16
NLAT = 240
NLON = 1440
MONTHS = 512
MON_DEV = 4
LAT_DEV = 15
LON_DEV = 180
LANES = 128
GROUPS = 22
SECOND = 56
TAIL = 112
CHUNK = MON_DEV * GROUPS
WINDOWS = MON_DEV * N_LON
SROWS = 3 * WINDOWS
SSTRIDE = 97
VSTRIDE = 89
BLOCKS = [(i, j) for i in range(4) for j in range(i, 4)]
PACK = len(BLOCKS)
VMEM_LIMIT = 60 * 1024 * 1024


def lat_taps():
    offsets = np.arange(-HL, HL + 1).astype(np.float32)
    taps = np.exp(-(offsets * offsets) / np.float32(2.0)).astype(np.float32)
    taps = taps / taps.sum(dtype=np.float32)
    return [float(t) for t in taps.astype(jnp.bfloat16).astype(np.float32)]


def windows_kernel(field_hbm, out_hbm, field, windows, staged, in_sems, out_sems):
    steps = windows.shape[0] // 16
    lane16 = lax.broadcasted_iota(jnp.int32, (16, LANES), 1)

    def fetch(i):
        rows = pl.ds(pl.multiple_of(i * 16, 16), 16)
        return pltpu.make_async_copy(field_hbm.at[:, rows, :], field.at[:, rows, :], in_sems.at[i])

    def store(i):
        rows = pl.ds(pl.multiple_of(i * 16, 16), 16)
        return pltpu.make_async_copy(windows.at[rows], out_hbm.at[rows], out_sems.at[i])

    for i in range(steps):
        fetch(i).start()

    def step(i, carry):
        fetch(i).wait()
        for m in range(MON_DEV):
            rows = field[m, pl.ds(pl.multiple_of(i * 16, 16), 16), :]
            ring = jnp.concatenate([rows, rows[:, :352]], axis=1)
            for l in range(N_LON):
                start = (LON_DEV * l - HMAX) % NLON
                first_tile, shift = start // LANES, start % LANES
                tiles = [ring[:, t * LANES : (t + 1) * LANES] for t in range(first_tile, first_tile + 4)]
                if shift:
                    tiles = [pltpu.roll(t, LANES - shift, 1) for t in tiles]
                for j in range(3):
                    piece = jnp.where(lane16 < LANES - shift, tiles[j], tiles[j + 1]) if shift else tiles[j]
                    piece = piece.astype(jnp.float32)
                    for half in range(2):
                        first = half * 8 * SSTRIDE + j * WINDOWS + m * N_LON + l
                        staged[pl.ds(first, 8, stride=SSTRIDE), :] = piece[half * 8 : half * 8 + 8]
        for r in range(16):
            windows[i * 16 + r] = staged[r * SSTRIDE : r * SSTRIDE + SROWS, :].astype(jnp.bfloat16)
        store(i).start()
        return carry

    lax.fori_loop(0, steps, step, 0)
    for i in range(steps):
        store(i).wait()


def cut_windows(field):
    steps = NLAT // 16
    return pl.pallas_call(
        windows_kernel,
        out_shape=jax.ShapeDtypeStruct((steps * 16, SROWS, LANES), jnp.bfloat16),
        in_specs=[pl.BlockSpec(memory_space=pl.ANY)],
        out_specs=pl.BlockSpec(memory_space=pl.ANY),
        scratch_shapes=[
            pltpu.VMEM((MON_DEV, steps * 16, NLON), jnp.bfloat16),
            pltpu.VMEM((steps * 16, SROWS, LANES), jnp.bfloat16),
            pltpu.VMEM((16 * SSTRIDE + 8, LANES), jnp.float32),
            pltpu.SemaphoreType.DMA((steps,)),
            pltpu.SemaphoreType.DMA((steps,)),
        ],
        compiler_params=pltpu.CompilerParams(vmem_limit_bytes=VMEM_LIMIT),
        cost_estimate=pl.CostEstimate(flops=3000000000, bytes_accessed=9000000, transcendentals=0),
        name="cut_windows",
    )(field)


def smooth_kernel(widths_in, windows_hbm, out_hbm, widths, windows, out, taps, table, passed, staged, in_sems, out_sems, sem):
    bring = pltpu.make_async_copy(widths_in, widths, sem)
    bring.start()


    def fetch(i):
        rows = pl.ds(pl.multiple_of(i * 16, 16), 16)
        return pltpu.make_async_copy(windows_hbm.at[rows], windows.at[rows], in_sems.at[i])

    def store(b):
        return pltpu.make_async_copy(out.at[:, b], out_hbm.at[:, b], out_sems.at[b])

    for i in range(NLAT // 16):
        fetch(i).start()
    reach = (lax.broadcasted_iota(jnp.int32, (HMAX, LANES), 0) + 1).astype(jnp.float32)
    offset = (lax.broadcasted_iota(jnp.int32, (HMAX, LANES), 1) - HMAX).astype(jnp.float32)
    spread = 0.5 * reach
    value = jnp.exp(-(offset * offset) / (2.0 * spread * spread))
    value = jnp.where(jnp.abs(offset) <= reach, value, 0.0)
    total = jnp.sum(value, axis=1, keepdims=True) + value[:, 0:1]
    taps[...] = (value / total).astype(jnp.bfloat16).astype(jnp.float32)
    sub = lax.broadcasted_iota(jnp.int32, (LANES, LANES), 0)
    lane = lax.broadcasted_iota(jnp.int32, (LANES, LANES), 1)
    upper = jnp.where(sub >= lane, 1.0, 0.0).astype(jnp.bfloat16)
    lower = jnp.where(sub <= lane, 1.0, 0.0).astype(jnp.bfloat16)

    def build_matrix(h, carry):
        spread_taps = jnp.broadcast_to(taps[pl.ds(h, 1), :], (LANES, LANES))
        ring = pltpu.roll(spread_taps, 0, 1, stride=1, stride_axis=0).astype(jnp.bfloat16)
        table[h, 0:LANES, :] = ring * upper
        table[h, LANES:, :] = ring * lower
        return carry

    lax.fori_loop(0, HMAX, build_matrix, 0, unroll=8)
    edge = jnp.zeros((HL, 2 * WINDOWS, LANES), jnp.float32)
    passed[0:HL] = edge
    passed[NLAT + HL : NLAT + 2 * HL] = edge

    def lon_band(b):
        for rr in range(LAT_DEV):
            r = b * LAT_DEV + rr
            lhs = windows[r]
            left = jnp.concatenate([lhs[: 2 * WINDOWS], lhs[WINDOWS:]], axis=1)
            right = table[widths[b, rr] - 1]
            res = jnp.dot(left, right, preferred_element_type=jnp.float32)
            passed[r + HL] = res.astype(jnp.bfloat16).astype(jnp.float32)

    w0, w1, w2 = lat_taps()[:3]
    laneb = lax.broadcasted_iota(jnp.int32, (WINDOWS, LANES), 1)

    def lat_band(b):
        def smoothed(rr, lo, hi):
            r = b * LAT_DEV + rr
            outer = passed[r, lo:hi] + passed[r + 4, lo:hi]
            inner = passed[r + 1, lo:hi] + passed[r + 3, lo:hi]
            return w0 * outer + w1 * inner + w2 * passed[r + 2, lo:hi]

        def put(g, value):
            for m in range(MON_DEV):
                staged[pl.ds(m * GROUPS + g, N_LON, stride=VSTRIDE), :] = value[8 * m : 8 * m + 8]

        for rr in range(LAT_DEV):
            put(rr, smoothed(rr, 0, WINDOWS))
        last = smoothed(LAT_DEV - 1, WINDOWS, 2 * WINDOWS)
        for q in range(7):
            even = smoothed(2 * q, WINDOWS, 2 * WINDOWS)
            odd = smoothed(2 * q + 1, WINDOWS, 2 * WINDOWS)
            value = jnp.where(laneb < SECOND, even, pltpu.roll(odd, SECOND, 1))
            if q < 4:
                tail = pltpu.roll(last, TAIL - 16 * q, 1)
                value = jnp.where(laneb < TAIL, value, tail)
            put(LAT_DEV + q, value)
        for l in range(N_LON):
            out[l, b] = staged[l * VSTRIDE : l * VSTRIDE + CHUNK, :].astype(jnp.bfloat16)

    bring.wait()
    for b in range(2):
        fetch(b).wait()
        lon_band(b)

    def band(b, carry):
        fetch(b).wait()
        lat_band(b - 2)
        lon_band(b)
        store(b - 2).start()
        return carry

    lax.fori_loop(2, N_LAT - 1, band, 0)
    lat_band(N_LAT - 3)
    lon_band(N_LAT - 1)
    store(N_LAT - 3).start()
    for b in (N_LAT - 2, N_LAT - 1):
        lat_band(b)
        store(b).start()
    for b in range(N_LAT):
        store(b).wait()


def smooth(widths, windows):
    out = pl.pallas_call(
        smooth_kernel,
        out_shape=jax.ShapeDtypeStruct((N_LON, N_LAT, CHUNK, LANES), jnp.bfloat16),
        in_specs=[pl.BlockSpec(memory_space=pltpu.VMEM), pl.BlockSpec(memory_space=pl.ANY)],
        out_specs=pl.BlockSpec(memory_space=pl.ANY),
        scratch_shapes=[
            pltpu.SMEM((N_LAT, LAT_DEV), jnp.int32),
            pltpu.VMEM((NLAT, SROWS, LANES), jnp.bfloat16),
            pltpu.VMEM((N_LON, N_LAT, CHUNK, LANES), jnp.bfloat16),
            pltpu.VMEM((HMAX, LANES), jnp.float32),
            pltpu.VMEM((HMAX, 2 * LANES, LANES), jnp.bfloat16),
            pltpu.VMEM((NLAT + 2 * HL, 2 * WINDOWS, LANES), jnp.float32),
            pltpu.VMEM((N_LON * VSTRIDE + 8, LANES), jnp.float32),
            pltpu.SemaphoreType.DMA((NLAT // 16,)),
            pltpu.SemaphoreType.DMA((N_LAT,)),
            pltpu.SemaphoreType.DMA,
        ],
        compiler_params=pltpu.CompilerParams(vmem_limit_bytes=VMEM_LIMIT),
        name="smooth",
    )(widths, windows)
    return out.reshape(N_LON * N_LAT, CHUNK, LANES)


def gram_kernel(core, landed, weight, mine, theirs, anomaly, wide, square):
    def widen(s, carry):
        wide[pl.ds(pl.multiple_of(s * CHUNK, 8), CHUNK), :] = landed[s].astype(jnp.float32)
        return carry

    lax.fori_loop(0, N_LON * N_LAT, widen, 0, unroll=4)
    lane = lax.broadcasted_iota(jnp.int32, (1, LANES), 1)
    for g in range(GROUPS):
        if g < LAT_DEV:
            scale = weight[g : g + 1, :LANES]
        else:
            q = g - LAT_DEV
            scale = weight[2 * q : 2 * q + 1, LANES:]
            scale = scale + pltpu.roll(weight[2 * q + 1 : 2 * q + 2, LANES:], SECOND, 1)
            if q < 4:
                last = weight[LAT_DEV - 1 : LAT_DEV, LANES:]
                last = jnp.where((lane >= 16 * q) & (lane < 16 * q + 16), last, 0.0)
                scale = scale + pltpu.roll(last, TAIL - 16 * q, 1)
        cells = wide[pl.ds(g, MONTHS, stride=GROUPS), :]
        mean = jnp.sum(cells, axis=0, keepdims=True) * (1.0 / MONTHS)
        anomaly[:, g * LANES : (g + 1) * LANES] = ((cells - mean) * scale).astype(jnp.bfloat16)
    for i, j in ((0, 0), (0, 1), (1, 1)):
        block = lax.dot_general(
            anomaly[i * ROWB : (i + 1) * ROWB, :],
            anomaly[j * ROWB : (j + 1) * ROWB, :],
            (((1,), (1,)), ((), ())),
            preferred_element_type=jnp.float32,
        )
        for n, (bi, bj) in enumerate(BLOCKS):
            if bi // 2 == i and bj // 2 == j:
                a, c = (bi % 2) * LANES, (bj % 2) * LANES
                square[...] = block[a : a + LANES, c : c + LANES]
                for ref, half in ((mine, core[0]), (theirs, 1 - core[0])):
                    rows = pl.ds(pl.multiple_of(half * HALF, HALF), HALF)
                    ref[pl.ds(n, HALF, stride=PACK), :] = square[rows, :]


def gram_terms(core, landed, weight):
    part = jax.ShapeDtypeStruct((HALF * PACK, LANES), jnp.float32)
    return pl.pallas_call(
        gram_kernel,
        out_shape=(part, part, jax.ShapeDtypeStruct((MONTHS, GROUPS * LANES), jnp.bfloat16)),
        in_specs=[
            pl.BlockSpec(memory_space=pltpu.SMEM),
            pl.BlockSpec(memory_space=pltpu.VMEM),
            pl.BlockSpec(memory_space=pltpu.VMEM),
        ],
        out_specs=(pl.BlockSpec(memory_space=pltpu.VMEM),) * 3,
        scratch_shapes=[
            pltpu.VMEM((N_LON * N_LAT * CHUNK, LANES), jnp.float32),
            pltpu.VMEM((LANES, LANES), jnp.float32),
        ],
        compiler_params=pltpu.CompilerParams(vmem_limit_bytes=32 * 1024 * 1024),
        name="gram_terms",
    )(core, landed, weight)


def turn_kernel(anomaly, turned):
    for g in range(GROUPS):
        turned[g * LANES : (g + 1) * LANES, :] = anomaly[:, g * LANES : (g + 1) * LANES].T


def turn(anomaly):
    return pl.pallas_call(
        turn_kernel,
        out_shape=jax.ShapeDtypeStruct((GROUPS * LANES, MONTHS), jnp.bfloat16),
        in_specs=[pl.BlockSpec(memory_space=pltpu.VMEM)],
        out_specs=pl.BlockSpec(memory_space=pltpu.VMEM),
        compiler_params=pltpu.CompilerParams(vmem_limit_bytes=16 * 1024 * 1024),
        cost_estimate=pl.CostEstimate(flops=2000000000, bytes_accessed=6000000, transcendentals=0),
        name="turn",
    )(anomaly)


def add_kernel(terms, out):
    step = 4 * PACK
    total = terms[0:step, :]
    for s in range(1, HALF // 4):
        total = total + terms[s * step : (s + 1) * step, :]
    row = total[0:PACK] + total[PACK : 2 * PACK] + total[2 * PACK : 3 * PACK] + total[3 * PACK :]
    total = jnp.concatenate([row] * 4, axis=0)
    for s in range(HALF // 4):
        out[s * step : (s + 1) * step, :] = total


def add_terms(terms):
    return pl.pallas_call(
        add_kernel,
        out_shape=jax.ShapeDtypeStruct(terms.shape, jnp.float32),
        in_specs=[pl.BlockSpec(memory_space=pltpu.VMEM)],
        out_specs=pl.BlockSpec(memory_space=pltpu.VMEM),
        compiler_params=pltpu.CompilerParams(vmem_limit_bytes=8 * 1024 * 1024),
        name="add_terms",
    )(terms)


STEP = (2.25, -2.4375, 1.6875, -0.5625, 0.0625)
ROWB = 256
MIRROR = True


def root_kernel(core, mine, theirs, anomaly, patterns_hbm, whitener_hbm, patterns, whitener, ws, hs, ps, ss, zs, wb, out_sems):
    for n, (bi, bj) in enumerate(BLOCKS):
        for ref, half in ((mine, core[0]), (theirs, 1 - core[0])):
            rows = pl.ds(pl.multiple_of(bi * LANES + half * HALF, HALF), HALF)
            whitener[rows, bj * LANES : (bj + 1) * LANES] = ref[pl.ds(n, HALF, stride=PACK), :]
        if bi != bj:
            block = whitener[bi * LANES : (bi + 1) * LANES, bj * LANES : (bj + 1) * LANES]
            whitener[bj * LANES : (bj + 1) * LANES, bi * LANES : (bi + 1) * LANES] = block.T
    gram = whitener[...]
    squares = jnp.sum(gram * gram, axis=0, keepdims=True)
    frobenius = jnp.sqrt(jnp.sum(squares, axis=1, keepdims=True) + 1e-06)
    final_scale = jnp.sqrt(float(NLAT * NLON) / frobenius)

    def split(ref, start, value):
        size = value.shape[0]
        high = value.astype(jnp.bfloat16)
        ref[start : start + size, :] = high
        ref[MONTHS + start : MONTHS + start + size, :] = (value - high.astype(jnp.float32)).astype(jnp.bfloat16)
        if ref.shape[0] == 3 * MONTHS:
            ref[2 * MONTHS + start : 2 * MONTHS + start + size, :] = high

    def join(ref, start):
        high = ref[start : start + ROWB, :].astype(jnp.float32)
        return high + ref[MONTHS + start : MONTHS + start + ROWB, :].astype(jnp.float32)

    def product(left, right):
        def rows(start):
            high = left[start : start + ROWB, :]
            low = left[MONTHS + start : MONTHS + start + ROWB, :]
            return jnp.concatenate([high, high, low], axis=1)

        upper = jnp.dot(rows(0), right[...], preferred_element_type=jnp.float32)
        if not MIRROR:
            return upper, jnp.dot(rows(ROWB), right[...], preferred_element_type=jnp.float32)
        corner = jnp.dot(rows(ROWB), right[:, ROWB:], preferred_element_type=jnp.float32)
        return upper, jnp.concatenate([upper[:, ROWB:].T, corner], axis=1)

    def plus_eye(value, start, scale):
        row = lax.broadcasted_iota(jnp.int32, value.shape, 0) + start
        column = lax.broadcasted_iota(jnp.int32, value.shape, 1)
        return jnp.where(row == column, value + scale, value)

    split(ws, 0, gram / frobenius)
    c0, c1, c2, c3, c4 = STEP
    last = ITERS // 2 - 1

    def double_step(k):
        for n, square in enumerate(product(ws, ws)):
            start = n * ROWB
            split(ss, start, square)
            split(hs, start, plus_eye(c3 * join(ws, start) + c4 * square, start, c2))
        for n, value in enumerate(product(ss, hs)):
            start = n * ROWB
            split(ps, start, plus_eye(value + c1 * join(ws, start), start, c0))

        if k == 0:
            zs[...] = ps[0 : 2 * MONTHS, :]

        if k > 0:
            for n, value in enumerate(product(zs, ps)):
                split(zs, n * ROWB, value)
                whitener[n * ROWB : (n + 1) * ROWB, :] = value * final_scale

        if k < last:
            for n, value in enumerate(product(ws, ps)):
                split(ss, n * ROWB, value)
            for n, value in enumerate(product(ss, ps)):
                split(ws, n * ROWB, value)

    for k in range(last + 1):
        double_step(k)
    copies = [pltpu.make_async_copy(whitener, whitener_hbm, out_sems.at[LAT_DEV])]
    copies[0].start()
    wb[...] = whitener[...].astype(jnp.bfloat16)

    def group(g):
        return lax.dot_general(
            anomaly[g * LANES : (g + 1) * LANES, :],
            wb[...],
            (((1,), (0,)), ((), ())),
            preferred_element_type=jnp.float32,
        ).astype(jnp.bfloat16)

    def finish(r):
        copy = pltpu.make_async_copy(patterns.at[r], patterns_hbm.at[r], out_sems.at[r])
        copy.start()
        copies.append(copy)

    for q in range(7):
        value = group(LAT_DEV + q)
        patterns[2 * q, LANES:, :] = value[0 : LON_DEV - LANES]
        patterns[2 * q + 1, LANES:, :] = value[SECOND : SECOND + LON_DEV - LANES]
        if q < 4:
            first = LANES + 16 * q
            size = min(16, LON_DEV - first)
            patterns[LAT_DEV - 1, first : first + size, :] = value[TAIL : TAIL + size]
        for r in (2 * q, 2 * q + 1):
            patterns[r, 0:LANES, :] = group(r)
            finish(r)
    patterns[LAT_DEV - 1, 0:LANES, :] = group(LAT_DEV - 1)
    finish(LAT_DEV - 1)
    for copy in copies:
        copy.wait()


def root_and_patterns(core, mine, theirs, turned):
    return pl.pallas_call(
        root_kernel,
        out_shape=(
            jax.ShapeDtypeStruct((LAT_DEV, LON_DEV, MONTHS), jnp.bfloat16),
            jax.ShapeDtypeStruct((MONTHS, MONTHS), jnp.float32),
        ),
        in_specs=[
            pl.BlockSpec(memory_space=pltpu.SMEM),
            pl.BlockSpec(memory_space=pltpu.VMEM),
            pl.BlockSpec(memory_space=pltpu.VMEM),
            pl.BlockSpec(memory_space=pltpu.VMEM),
        ],
        out_specs=(pl.BlockSpec(memory_space=pl.ANY),) * 2,
        scratch_shapes=[
            pltpu.VMEM((LAT_DEV, LON_DEV, MONTHS), jnp.bfloat16),
            pltpu.VMEM((MONTHS, MONTHS), jnp.float32),
            pltpu.VMEM((3 * MONTHS, MONTHS), jnp.bfloat16),
            pltpu.VMEM((3 * MONTHS, MONTHS), jnp.bfloat16),
            pltpu.VMEM((3 * MONTHS, MONTHS), jnp.bfloat16),
            pltpu.VMEM((2 * MONTHS, MONTHS), jnp.bfloat16),
            pltpu.VMEM((2 * MONTHS, MONTHS), jnp.bfloat16),
            pltpu.VMEM((MONTHS, MONTHS), jnp.bfloat16),
            pltpu.SemaphoreType.DMA((LAT_DEV + 1,)),
        ],
        compiler_params=pltpu.CompilerParams(vmem_limit_bytes=32 * 1024 * 1024),
        name="root_and_patterns",
    )(core, mine, theirs, turned)


def exchange(pieces, axes):
    return lax.all_to_all(pieces, axes, split_axis=0, concat_axis=0, tiled=True)


def exchange_packed(packed):
    pieces = packed.reshape(HALF, PACK // 2, 2, LANES)
    return exchange(pieces, SAME_CORE).reshape(packed.shape)


def swap_cores(x):
    return lax.ppermute(x, "core", [(0, 1), (1, 0)])


def local(monthly_field, half_width, land_mask):
    widths = exchange(jnp.broadcast_to(half_width, (N_LAT, 1, LAT_DEV)), LAT).reshape(N_LAT, LAT_DEV)
    windows = cut_windows(monthly_field)
    landed = exchange(smooth(widths, windows), BOTH)
    row_index = lax.axis_index(LAT) * LAT_DEV + jnp.arange(LAT_DEV)
    latitude = math.pi * ((row_index.astype(jnp.float32) + 0.5) / NLAT - 0.5)
    weight = jnp.sqrt(jnp.cos(latitude))[:, None] * land_mask.astype(jnp.float32)
    weight = jnp.pad(weight, ((0, 0), (0, 2 * LANES - LON_DEV)))
    core = lax.axis_index("core").reshape(1)
    mine, theirs, anomaly = gram_terms(core, landed, weight)
    terms = exchange_packed(mine + swap_cores(theirs))
    turned = turn(anomaly)
    mine = exchange_packed(add_terms(terms))
    patterns, whitener = root_and_patterns(core, mine, swap_cores(mine), turned)
    return (jnp.transpose(patterns, (2, 0, 1)), whitener)


def solution(mesh):
    fine = Mesh(mesh.devices.reshape(N_LON, N_LAT // 2, 2), BOTH)
    placed = (P(BOTH, None, None), P(LAT), P(LAT, "lon"))
    return jax.shard_map(
        local, mesh=fine, in_specs=placed, out_specs=(P(None, LAT, "lon"), P()), check_vma=False
    )
```

```python
import math

import jax
import jax.numpy as jnp
import numpy as np
from jax import lax
from jax.experimental import pallas as pl
from jax.experimental.pallas import tpu as pltpu
from jax.sharding import Mesh
from jax.sharding import PartitionSpec as P

HMAX = 64
HL = 2
ITERS = 8
LAT = ("chip", "core")
BOTH = ("lon", "chip", "core")
SAME_CORE = ("lon", "chip")
HALF = 64
N_LON = 8
N_LAT = 16
NLAT = 240
NLON = 1440
MONTHS = 512
MON_DEV = 4
LAT_DEV = 15
LON_DEV = 180
LANES = 128
GROUPS = 22
SECOND = 56
TAIL = 112
CHUNK = MON_DEV * GROUPS
WINDOWS = MON_DEV * N_LON
SROWS = 3 * WINDOWS
SSTRIDE = 97
VSTRIDE = 89
BLOCKS = [(i, j) for i in range(4) for j in range(i, 4)]
PACK = len(BLOCKS)
VMEM_LIMIT = 60 * 1024 * 1024


def lat_taps():
    offsets = np.arange(-HL, HL + 1).astype(np.float32)
    taps = np.exp(-(offsets * offsets) / np.float32(2.0)).astype(np.float32)
    taps = taps / taps.sum(dtype=np.float32)
    return [float(t) for t in taps.astype(jnp.bfloat16).astype(np.float32)]


def windows_kernel(field_hbm, out_hbm, field, windows, staged, in_sems, out_sems):
    steps = windows.shape[0] // 16
    lane16 = lax.broadcasted_iota(jnp.int32, (16, LANES), 1)

    def fetch(i):
        rows = pl.ds(pl.multiple_of(i * 16, 16), 16)
        return pltpu.make_async_copy(field_hbm.at[:, rows, :], field.at[:, rows, :], in_sems.at[i])

    def store(i):
        rows = pl.ds(pl.multiple_of(i * 16, 16), 16)
        return pltpu.make_async_copy(windows.at[rows], out_hbm.at[rows], out_sems.at[i])

    for i in range(steps):
        fetch(i).start()

    def step(i, carry):
        fetch(i).wait()
        for m in range(MON_DEV):
            rows = field[m, pl.ds(pl.multiple_of(i * 16, 16), 16), :]
            ring = jnp.concatenate([rows, rows[:, :352]], axis=1)
            for l in range(N_LON):
                start = (LON_DEV * l - HMAX) % NLON
                first_tile, shift = start // LANES, start % LANES
                tiles = [ring[:, t * LANES : (t + 1) * LANES] for t in range(first_tile, first_tile + 4)]
                if shift:
                    tiles = [pltpu.roll(t, LANES - shift, 1) for t in tiles]
                for j in range(3):
                    piece = jnp.where(lane16 < LANES - shift, tiles[j], tiles[j + 1]) if shift else tiles[j]
                    piece = piece.astype(jnp.float32)
                    for half in range(2):
                        first = half * 8 * SSTRIDE + j * WINDOWS + m * N_LON + l
                        staged[pl.ds(first, 8, stride=SSTRIDE), :] = piece[half * 8 : half * 8 + 8]
        for r in range(16):
            windows[i * 16 + r] = staged[r * SSTRIDE : r * SSTRIDE + SROWS, :].astype(jnp.bfloat16)
        store(i).start()
        return carry

    lax.fori_loop(0, steps, step, 0)
    for i in range(steps):
        store(i).wait()


def cut_windows(field):
    steps = NLAT // 16
    return pl.pallas_call(
        windows_kernel,
        out_shape=jax.ShapeDtypeStruct((steps * 16, SROWS, LANES), jnp.bfloat16),
        in_specs=[pl.BlockSpec(memory_space=pl.ANY)],
        out_specs=pl.BlockSpec(memory_space=pl.ANY),
        scratch_shapes=[
            pltpu.VMEM((MON_DEV, steps * 16, NLON), jnp.bfloat16),
            pltpu.VMEM((steps * 16, SROWS, LANES), jnp.bfloat16),
            pltpu.VMEM((16 * SSTRIDE + 8, LANES), jnp.float32),
            pltpu.SemaphoreType.DMA((steps,)),
            pltpu.SemaphoreType.DMA((steps,)),
        ],
        compiler_params=pltpu.CompilerParams(vmem_limit_bytes=VMEM_LIMIT),
        cost_estimate=pl.CostEstimate(flops=3000000000, bytes_accessed=9000000, transcendentals=0),
        name="cut_windows",
    )(field)


def smooth_kernel(widths_in, windows_hbm, out_hbm, widths, windows, out, taps, table, passed, staged, in_sems, out_sems, sem):
    bring = pltpu.make_async_copy(widths_in, widths, sem)
    bring.start()


    def fetch(i):
        rows = pl.ds(pl.multiple_of(i * 16, 16), 16)
        return pltpu.make_async_copy(windows_hbm.at[rows], windows.at[rows], in_sems.at[i])

    def store(b):
        return pltpu.make_async_copy(out.at[:, b], out_hbm.at[:, b], out_sems.at[b])

    for i in range(NLAT // 16):
        fetch(i).start()
    reach = (lax.broadcasted_iota(jnp.int32, (HMAX, LANES), 0) + 1).astype(jnp.float32)
    offset = (lax.broadcasted_iota(jnp.int32, (HMAX, LANES), 1) - HMAX).astype(jnp.float32)
    spread = 0.5 * reach
    value = jnp.exp(-(offset * offset) / (2.0 * spread * spread))
    value = jnp.where(jnp.abs(offset) <= reach, value, 0.0)
    total = jnp.sum(value, axis=1, keepdims=True) + value[:, 0:1]
    taps[...] = (value / total).astype(jnp.bfloat16).astype(jnp.float32)
    sub = lax.broadcasted_iota(jnp.int32, (LANES, LANES), 0)
    lane = lax.broadcasted_iota(jnp.int32, (LANES, LANES), 1)
    upper = jnp.where(sub >= lane, 1.0, 0.0).astype(jnp.bfloat16)
    lower = jnp.where(sub <= lane, 1.0, 0.0).astype(jnp.bfloat16)

    def build_matrix(h, carry):
        spread_taps = jnp.broadcast_to(taps[pl.ds(h, 1), :], (LANES, LANES))
        ring = pltpu.roll(spread_taps, 0, 1, stride=1, stride_axis=0).astype(jnp.bfloat16)
        table[h, 0:LANES, :] = ring * upper
        table[h, LANES:, :] = ring * lower
        return carry

    lax.fori_loop(0, HMAX, build_matrix, 0, unroll=8)
    edge = jnp.zeros((HL, 2 * WINDOWS, LANES), jnp.float32)
    passed[0:HL] = edge
    passed[NLAT + HL : NLAT + 2 * HL] = edge

    def lon_band(b):
        for rr in range(LAT_DEV):
            r = b * LAT_DEV + rr
            lhs = windows[r]
            left = jnp.concatenate([lhs[: 2 * WINDOWS], lhs[WINDOWS:]], axis=1)
            right = table[widths[b, rr] - 1]
            res = jnp.dot(left, right, preferred_element_type=jnp.float32)
            passed[r + HL] = res.astype(jnp.bfloat16).astype(jnp.float32)

    w0, w1, w2 = lat_taps()[:3]
    laneb = lax.broadcasted_iota(jnp.int32, (WINDOWS, LANES), 1)

    def lat_band(b):
        def smoothed(rr, lo, hi):
            r = b * LAT_DEV + rr
            outer = passed[r, lo:hi] + passed[r + 4, lo:hi]
            inner = passed[r + 1, lo:hi] + passed[r + 3, lo:hi]
            return w0 * outer + w1 * inner + w2 * passed[r + 2, lo:hi]

        def put(g, value):
            for m in range(MON_DEV):
                staged[pl.ds(m * GROUPS + g, N_LON, stride=VSTRIDE), :] = value[8 * m : 8 * m + 8]

        for rr in range(LAT_DEV):
            put(rr, smoothed(rr, 0, WINDOWS))
        last = smoothed(LAT_DEV - 1, WINDOWS, 2 * WINDOWS)
        for q in range(7):
            even = smoothed(2 * q, WINDOWS, 2 * WINDOWS)
            odd = smoothed(2 * q + 1, WINDOWS, 2 * WINDOWS)
            value = jnp.where(laneb < SECOND, even, pltpu.roll(odd, SECOND, 1))
            if q < 4:
                tail = pltpu.roll(last, TAIL - 16 * q, 1)
                value = jnp.where(laneb < TAIL, value, tail)
            put(LAT_DEV + q, value)
        for l in range(N_LON):
            out[l, b] = staged[l * VSTRIDE : l * VSTRIDE + CHUNK, :].astype(jnp.bfloat16)

    bring.wait()
    for b in range(2):
        fetch(b).wait()
        lon_band(b)

    def band(b, carry):
        fetch(b).wait()
        lat_band(b - 2)
        lon_band(b)
        store(b - 2).start()
        return carry

    lax.fori_loop(2, N_LAT - 1, band, 0)
    lat_band(N_LAT - 3)
    lon_band(N_LAT - 1)
    store(N_LAT - 3).start()
    for b in (N_LAT - 2, N_LAT - 1):
        lat_band(b)
        store(b).start()
    for b in range(N_LAT):
        store(b).wait()


def smooth(widths, windows):
    out = pl.pallas_call(
        smooth_kernel,
        out_shape=jax.ShapeDtypeStruct((N_LON, N_LAT, CHUNK, LANES), jnp.bfloat16),
        in_specs=[pl.BlockSpec(memory_space=pltpu.VMEM), pl.BlockSpec(memory_space=pl.ANY)],
        out_specs=pl.BlockSpec(memory_space=pl.ANY),
        scratch_shapes=[
            pltpu.SMEM((N_LAT, LAT_DEV), jnp.int32),
            pltpu.VMEM((NLAT, SROWS, LANES), jnp.bfloat16),
            pltpu.VMEM((N_LON, N_LAT, CHUNK, LANES), jnp.bfloat16),
            pltpu.VMEM((HMAX, LANES), jnp.float32),
            pltpu.VMEM((HMAX, 2 * LANES, LANES), jnp.bfloat16),
            pltpu.VMEM((NLAT + 2 * HL, 2 * WINDOWS, LANES), jnp.float32),
            pltpu.VMEM((N_LON * VSTRIDE + 8, LANES), jnp.float32),
            pltpu.SemaphoreType.DMA((NLAT // 16,)),
            pltpu.SemaphoreType.DMA((N_LAT,)),
            pltpu.SemaphoreType.DMA,
        ],
        compiler_params=pltpu.CompilerParams(vmem_limit_bytes=VMEM_LIMIT),
        name="smooth",
    )(widths, windows)
    return out.reshape(N_LON * N_LAT, CHUNK, LANES)


def gram_kernel(core, landed, weight, mine, theirs, anomaly, wide, square):
    def widen(s, carry):
        wide[pl.ds(pl.multiple_of(s * CHUNK, 8), CHUNK), :] = landed[s].astype(jnp.float32)
        return carry

    lax.fori_loop(0, N_LON * N_LAT, widen, 0, unroll=4)
    lane = lax.broadcasted_iota(jnp.int32, (1, LANES), 1)
    for g in range(GROUPS):
        if g < LAT_DEV:
            scale = weight[g : g + 1, :LANES]
        else:
            q = g - LAT_DEV
            scale = weight[2 * q : 2 * q + 1, LANES:]
            scale = scale + pltpu.roll(weight[2 * q + 1 : 2 * q + 2, LANES:], SECOND, 1)
            if q < 4:
                last = weight[LAT_DEV - 1 : LAT_DEV, LANES:]
                last = jnp.where((lane >= 16 * q) & (lane < 16 * q + 16), last, 0.0)
                scale = scale + pltpu.roll(last, TAIL - 16 * q, 1)
        cells = wide[pl.ds(g, MONTHS, stride=GROUPS), :]
        mean = jnp.sum(cells, axis=0, keepdims=True) * (1.0 / MONTHS)
        anomaly[:, g * LANES : (g + 1) * LANES] = ((cells - mean) * scale).astype(jnp.bfloat16)
    for i, j in ((0, 0), (0, 1), (1, 1)):
        block = lax.dot_general(
            anomaly[i * ROWB : (i + 1) * ROWB, :],
            anomaly[j * ROWB : (j + 1) * ROWB, :],
            (((1,), (1,)), ((), ())),
            preferred_element_type=jnp.float32,
        )
        for n, (bi, bj) in enumerate(BLOCKS):
            if bi // 2 == i and bj // 2 == j:
                a, c = (bi % 2) * LANES, (bj % 2) * LANES
                square[...] = block[a : a + LANES, c : c + LANES]
                for ref, half in ((mine, core[0]), (theirs, 1 - core[0])):
                    rows = pl.ds(pl.multiple_of(half * HALF, HALF), HALF)
                    ref[pl.ds(n, HALF, stride=PACK), :] = square[rows, :]


def gram_terms(core, landed, weight):
    part = jax.ShapeDtypeStruct((HALF * PACK, LANES), jnp.float32)
    return pl.pallas_call(
        gram_kernel,
        out_shape=(part, part, jax.ShapeDtypeStruct((MONTHS, GROUPS * LANES), jnp.bfloat16)),
        in_specs=[
            pl.BlockSpec(memory_space=pltpu.SMEM),
            pl.BlockSpec(memory_space=pltpu.VMEM),
            pl.BlockSpec(memory_space=pltpu.VMEM),
        ],
        out_specs=(pl.BlockSpec(memory_space=pltpu.VMEM),) * 3,
        scratch_shapes=[
            pltpu.VMEM((N_LON * N_LAT * CHUNK, LANES), jnp.float32),
            pltpu.VMEM((LANES, LANES), jnp.float32),
        ],
        compiler_params=pltpu.CompilerParams(vmem_limit_bytes=32 * 1024 * 1024),
        name="gram_terms",
    )(core, landed, weight)


def turn_kernel(anomaly, turned):
    for g in range(GROUPS):
        turned[g * LANES : (g + 1) * LANES, :] = anomaly[:, g * LANES : (g + 1) * LANES].T


def turn(anomaly):
    return pl.pallas_call(
        turn_kernel,
        out_shape=jax.ShapeDtypeStruct((GROUPS * LANES, MONTHS), jnp.bfloat16),
        in_specs=[pl.BlockSpec(memory_space=pltpu.VMEM)],
        out_specs=pl.BlockSpec(memory_space=pltpu.VMEM),
        compiler_params=pltpu.CompilerParams(vmem_limit_bytes=16 * 1024 * 1024),
        cost_estimate=pl.CostEstimate(flops=2000000000, bytes_accessed=6000000, transcendentals=0),
        name="turn",
    )(anomaly)


def add_kernel(terms, out):
    step = 4 * PACK
    total = terms[0:step, :]
    for s in range(1, HALF // 4):
        total = total + terms[s * step : (s + 1) * step, :]
    row = total[0:PACK] + total[PACK : 2 * PACK] + total[2 * PACK : 3 * PACK] + total[3 * PACK :]
    total = jnp.concatenate([row] * 4, axis=0)
    for s in range(HALF // 4):
        out[s * step : (s + 1) * step, :] = total


def add_terms(terms):
    return pl.pallas_call(
        add_kernel,
        out_shape=jax.ShapeDtypeStruct(terms.shape, jnp.float32),
        in_specs=[pl.BlockSpec(memory_space=pltpu.VMEM)],
        out_specs=pl.BlockSpec(memory_space=pltpu.VMEM),
        compiler_params=pltpu.CompilerParams(vmem_limit_bytes=8 * 1024 * 1024),
        name="add_terms",
    )(terms)


STEP = (2.25, -2.4375, 1.6875, -0.5625, 0.0625)
ROWB = 256
MIRROR = True


def root_kernel(core, mine, theirs, anomaly, patterns_hbm, whitener_hbm, patterns, whitener, ws, hs, ps, ss, zs, wb, out_sems):
    for n, (bi, bj) in enumerate(BLOCKS):
        for ref, half in ((mine, core[0]), (theirs, 1 - core[0])):
            rows = pl.ds(pl.multiple_of(bi * LANES + half * HALF, HALF), HALF)
            whitener[rows, bj * LANES : (bj + 1) * LANES] = ref[pl.ds(n, HALF, stride=PACK), :]
        if bi != bj:
            block = whitener[bi * LANES : (bi + 1) * LANES, bj * LANES : (bj + 1) * LANES]
            whitener[bj * LANES : (bj + 1) * LANES, bi * LANES : (bi + 1) * LANES] = block.T
    gram = whitener[...]
    squares = jnp.sum(gram * gram, axis=0, keepdims=True)
    frobenius = jnp.sqrt(jnp.sum(squares, axis=1, keepdims=True) + 1e-06)
    final_scale = jnp.sqrt(float(NLAT * NLON) / frobenius)

    def split(ref, start, value):
        size = value.shape[0]
        high = value.astype(jnp.bfloat16)
        ref[start : start + size, :] = high
        ref[MONTHS + start : MONTHS + start + size, :] = (value - high.astype(jnp.float32)).astype(jnp.bfloat16)
        if ref.shape[0] == 3 * MONTHS:
            ref[2 * MONTHS + start : 2 * MONTHS + start + size, :] = high

    def join(ref, start):
        high = ref[start : start + ROWB, :].astype(jnp.float32)
        return high + ref[MONTHS + start : MONTHS + start + ROWB, :].astype(jnp.float32)

    def product(left, right):
        def rows(start):
            high = left[start : start + ROWB, :]
            low = left[MONTHS + start : MONTHS + start + ROWB, :]
            return jnp.concatenate([high, high, low], axis=1)

        upper = jnp.dot(rows(0), right[...], preferred_element_type=jnp.float32)
        if not MIRROR:
            return upper, jnp.dot(rows(ROWB), right[...], preferred_element_type=jnp.float32)
        corner = jnp.dot(rows(ROWB), right[:, ROWB:], preferred_element_type=jnp.float32)
        return upper, jnp.concatenate([upper[:, ROWB:].T, corner], axis=1)

    def plus_eye(value, start, scale):
        row = lax.broadcasted_iota(jnp.int32, value.shape, 0) + start
        column = lax.broadcasted_iota(jnp.int32, value.shape, 1)
        return jnp.where(row == column, value + scale, value)

    split(ws, 0, gram * (1.0 / frobenius))
    c0, c1, c2, c3, c4 = STEP
    last = ITERS // 2 - 1

    def double_step(k):
        for n, square in enumerate(product(ws, ws)):
            start = n * ROWB
            split(ss, start, square)
            split(hs, start, plus_eye(c3 * join(ws, start) + c4 * square, start, c2))
        for n, value in enumerate(product(ss, hs)):
            start = n * ROWB
            value = plus_eye(value + c1 * join(ws, start), start, c0)
            split(ps, start, value)
            if k == 0:
                split(zs, start, value)

        if k > 0:
            for n, value in enumerate(product(zs, ps)):
                if k < last:
                    split(zs, n * ROWB, value)
                else:
                    whitener[n * ROWB : (n + 1) * ROWB, :] = value * final_scale

        if k < last:
            for n, value in enumerate(product(ws, ps)):
                split(ss, n * ROWB, value)
            for n, value in enumerate(product(ss, ps)):
                split(ws, n * ROWB, value)

    for k in range(last + 1):
        double_step(k)
    copies = [pltpu.make_async_copy(whitener, whitener_hbm, out_sems.at[LAT_DEV])]
    copies[0].start()
    wb[...] = whitener[...].astype(jnp.bfloat16)

    def group(g):
        return lax.dot_general(
            anomaly[g * LANES : (g + 1) * LANES, :],
            wb[...],
            (((1,), (0,)), ((), ())),
            preferred_element_type=jnp.float32,
        ).astype(jnp.bfloat16)

    def finish(r):
        copy = pltpu.make_async_copy(patterns.at[r], patterns_hbm.at[r], out_sems.at[r])
        copy.start()
        copies.append(copy)

    for q in range(7):
        value = group(LAT_DEV + q)
        patterns[2 * q, LANES:, :] = value[0 : LON_DEV - LANES]
        patterns[2 * q + 1, LANES:, :] = value[SECOND : SECOND + LON_DEV - LANES]
        if q < 4:
            first = LANES + 16 * q
            size = min(16, LON_DEV - first)
            patterns[LAT_DEV - 1, first : first + size, :] = value[TAIL : TAIL + size]
        for r in (2 * q, 2 * q + 1):
            patterns[r, 0:LANES, :] = group(r)
            finish(r)
    patterns[LAT_DEV - 1, 0:LANES, :] = group(LAT_DEV - 1)
    finish(LAT_DEV - 1)
    for copy in copies:
        copy.wait()


def root_and_patterns(core, mine, theirs, turned):
    return pl.pallas_call(
        root_kernel,
        out_shape=(
            jax.ShapeDtypeStruct((LAT_DEV, LON_DEV, MONTHS), jnp.bfloat16),
            jax.ShapeDtypeStruct((MONTHS, MONTHS), jnp.float32),
        ),
        in_specs=[
            pl.BlockSpec(memory_space=pltpu.SMEM),
            pl.BlockSpec(memory_space=pltpu.VMEM),
            pl.BlockSpec(memory_space=pltpu.VMEM),
            pl.BlockSpec(memory_space=pltpu.VMEM),
        ],
        out_specs=(pl.BlockSpec(memory_space=pl.ANY),) * 2,
        scratch_shapes=[
            pltpu.VMEM((LAT_DEV, LON_DEV, MONTHS), jnp.bfloat16),
            pltpu.VMEM((MONTHS, MONTHS), jnp.float32),
            pltpu.VMEM((3 * MONTHS, MONTHS), jnp.bfloat16),
            pltpu.VMEM((3 * MONTHS, MONTHS), jnp.bfloat16),
            pltpu.VMEM((3 * MONTHS, MONTHS), jnp.bfloat16),
            pltpu.VMEM((2 * MONTHS, MONTHS), jnp.bfloat16),
            pltpu.VMEM((2 * MONTHS, MONTHS), jnp.bfloat16),
            pltpu.VMEM((MONTHS, MONTHS), jnp.bfloat16),
            pltpu.SemaphoreType.DMA((LAT_DEV + 1,)),
        ],
        compiler_params=pltpu.CompilerParams(vmem_limit_bytes=32 * 1024 * 1024),
        name="root_and_patterns",
    )(core, mine, theirs, turned)


def exchange(pieces, axes):
    return lax.all_to_all(pieces, axes, split_axis=0, concat_axis=0, tiled=True)


def exchange_packed(packed):
    pieces = packed.reshape(HALF, PACK // 2, 2, LANES)
    return exchange(pieces, SAME_CORE).reshape(packed.shape)


def swap_cores(x):
    return lax.ppermute(x, "core", [(0, 1), (1, 0)])


def local(monthly_field, half_width, land_mask):
    widths = exchange(jnp.broadcast_to(half_width, (N_LAT, 1, LAT_DEV)), LAT).reshape(N_LAT, LAT_DEV)
    windows = cut_windows(monthly_field)
    landed = exchange(smooth(widths, windows), BOTH)
    row_index = lax.axis_index(LAT) * LAT_DEV + jnp.arange(LAT_DEV)
    latitude = math.pi * ((row_index.astype(jnp.float32) + 0.5) / NLAT - 0.5)
    weight = jnp.sqrt(jnp.cos(latitude))[:, None] * land_mask.astype(jnp.float32)
    weight = jnp.pad(weight, ((0, 0), (0, 2 * LANES - LON_DEV)))
    core = lax.axis_index("core").reshape(1)
    mine, theirs, anomaly = gram_terms(core, landed, weight)
    terms = exchange_packed(mine + swap_cores(theirs))
    turned = turn(anomaly)
    mine = exchange_packed(add_terms(terms))
    patterns, whitener = root_and_patterns(core, mine, swap_cores(mine), turned)
    return (jnp.transpose(patterns, (2, 0, 1)), whitener)


def solution(mesh):
    fine = Mesh(mesh.devices.reshape(N_LON, N_LAT // 2, 2), BOTH)
    placed = (P(BOTH, None, None), P(LAT), P(LAT, "lon"))
    return jax.shard_map(
        local, mesh=fine, in_specs=placed, out_specs=(P(None, LAT, "lon"), P()), check_vma=False
    )
```

```python
import math

import jax
import jax.numpy as jnp
import numpy as np
from jax import lax
from jax.experimental import pallas as pl
from jax.experimental.pallas import tpu as pltpu
from jax.sharding import Mesh
from jax.sharding import PartitionSpec as P

HMAX = 64
HL = 2
ITERS = 8
LAT = ("chip", "core")
BOTH = ("lon", "chip", "core")
SAME_CORE = ("lon", "chip")
HALF = 64
N_LON = 8
N_LAT = 16
NLAT = 240
NLON = 1440
MONTHS = 512
MON_DEV = 4
LAT_DEV = 15
LON_DEV = 180
LANES = 128
GROUPS = 22
SECOND = 56
TAIL = 112
CHUNK = MON_DEV * GROUPS
WINDOWS = MON_DEV * N_LON
SROWS = 3 * WINDOWS
SSTRIDE = 97
VSTRIDE = 89
BLOCKS = [(i, j) for i in range(4) for j in range(i, 4)]
PACK = len(BLOCKS)
VMEM_LIMIT = 60 * 1024 * 1024
SMOOTH_LIMIT = 52 * 1024 * 1024


def lat_taps():
    offsets = np.arange(-HL, HL + 1).astype(np.float32)
    taps = np.exp(-(offsets * offsets) / np.float32(2.0)).astype(np.float32)
    taps = taps / taps.sum(dtype=np.float32)
    return [float(t) for t in taps.astype(jnp.bfloat16).astype(np.float32)]


def windows_kernel(field_hbm, out_hbm, field, windows, staged, in_sems, out_sems):
    steps = windows.shape[0] // 16
    lane16 = lax.broadcasted_iota(jnp.int32, (16, LANES), 1)

    def fetch(i):
        rows = pl.ds(pl.multiple_of(i * 16, 16), 16)
        return pltpu.make_async_copy(field_hbm.at[:, rows, :], field.at[:, rows, :], in_sems.at[i])

    def store(i):
        rows = pl.ds(pl.multiple_of(i * 16, 16), 16)
        return pltpu.make_async_copy(windows.at[rows], out_hbm.at[rows], out_sems.at[i])

    for i in range(steps):
        fetch(i).start()

    def step(i, carry):
        fetch(i).wait()
        for m in range(MON_DEV):
            rows = field[m, pl.ds(pl.multiple_of(i * 16, 16), 16), :]
            ring = jnp.concatenate([rows, rows[:, :352]], axis=1)
            for l in range(N_LON):
                start = (LON_DEV * l - HMAX) % NLON
                first_tile, shift = start // LANES, start % LANES
                tiles = [ring[:, t * LANES : (t + 1) * LANES] for t in range(first_tile, first_tile + 4)]
                if shift:
                    tiles = [pltpu.roll(t, LANES - shift, 1) for t in tiles]
                for j in range(3):
                    piece = jnp.where(lane16 < LANES - shift, tiles[j], tiles[j + 1]) if shift else tiles[j]
                    piece = piece.astype(jnp.float32)
                    for half in range(2):
                        first = half * 8 * SSTRIDE + j * WINDOWS + m * N_LON + l
                        staged[pl.ds(first, 8, stride=SSTRIDE), :] = piece[half * 8 : half * 8 + 8]
        for r in range(16):
            windows[i * 16 + r] = staged[r * SSTRIDE : r * SSTRIDE + SROWS, :].astype(jnp.bfloat16)
        store(i).start()
        return carry

    lax.fori_loop(0, steps, step, 0)
    for i in range(steps):
        store(i).wait()


def cut_windows(field):
    steps = NLAT // 16
    return pl.pallas_call(
        windows_kernel,
        out_shape=jax.ShapeDtypeStruct((steps * 16, SROWS, LANES), jnp.bfloat16),
        in_specs=[pl.BlockSpec(memory_space=pl.ANY)],
        out_specs=pl.BlockSpec(memory_space=pl.ANY),
        scratch_shapes=[
            pltpu.VMEM((MON_DEV, steps * 16, NLON), jnp.bfloat16),
            pltpu.VMEM((steps * 16, SROWS, LANES), jnp.bfloat16),
            pltpu.VMEM((16 * SSTRIDE + 8, LANES), jnp.float32),
            pltpu.SemaphoreType.DMA((steps,)),
            pltpu.SemaphoreType.DMA((steps,)),
        ],
        compiler_params=pltpu.CompilerParams(vmem_limit_bytes=VMEM_LIMIT),
        cost_estimate=pl.CostEstimate(flops=3000000000, bytes_accessed=9000000, transcendentals=0),
        name="cut_windows",
    )(field)


def smooth_kernel(widths_in, windows_hbm, out_hbm, widths, windows, out, taps, table, passed, staged, in_sems, out_sems, sem):
    bring = pltpu.make_async_copy(widths_in, widths, sem)
    bring.start()


    def fetch(i):
        rows = pl.ds(pl.multiple_of(i * 16, 16), 16)
        return pltpu.make_async_copy(windows_hbm.at[rows], windows.at[rows], in_sems.at[i])

    def store(b):
        return pltpu.make_async_copy(out.at[:, b], out_hbm.at[:, b], out_sems.at[b])

    for i in range(NLAT // 16):
        fetch(i).start()
    reach = (lax.broadcasted_iota(jnp.int32, (HMAX, LANES), 0) + 1).astype(jnp.float32)
    offset = (lax.broadcasted_iota(jnp.int32, (HMAX, LANES), 1) - HMAX).astype(jnp.float32)
    spread = 0.5 * reach
    value = jnp.exp(-(offset * offset) / (2.0 * spread * spread))
    value = jnp.where(jnp.abs(offset) <= reach, value, 0.0)
    total = jnp.sum(value, axis=1, keepdims=True) + value[:, 0:1]
    taps[...] = (value / total).astype(jnp.bfloat16).astype(jnp.float32)
    sub = lax.broadcasted_iota(jnp.int32, (LANES, LANES), 0)
    lane = lax.broadcasted_iota(jnp.int32, (LANES, LANES), 1)
    upper = jnp.where(sub >= lane, 1.0, 0.0).astype(jnp.bfloat16)
    lower = jnp.where(sub <= lane, 1.0, 0.0).astype(jnp.bfloat16)

    def build_matrix(h, carry):
        spread_taps = jnp.broadcast_to(taps[pl.ds(h, 1), :], (LANES, LANES))
        ring = pltpu.roll(spread_taps, 0, 1, stride=1, stride_axis=0).astype(jnp.bfloat16)
        table[h, 0:LANES, :] = ring * upper
        table[h, LANES:, :] = ring * lower
        return carry

    lax.fori_loop(0, HMAX, build_matrix, 0, unroll=8)
    edge = jnp.zeros((HL, 2 * WINDOWS, LANES), jnp.float32)
    passed[0:HL] = edge
    passed[NLAT + HL : NLAT + 2 * HL] = edge

    def lon_band(b):
        for rr in range(LAT_DEV):
            r = b * LAT_DEV + rr
            lhs = windows[r]
            left = jnp.concatenate([lhs[: 2 * WINDOWS], lhs[WINDOWS:]], axis=1)
            right = table[widths[b, rr] - 1]
            res = jnp.dot(left, right, preferred_element_type=jnp.float32)
            passed[r + HL] = res.astype(jnp.bfloat16).astype(jnp.float32)

    w0, w1, w2 = lat_taps()[:3]
    laneb = lax.broadcasted_iota(jnp.int32, (WINDOWS, LANES), 1)

    def lat_band(b):
        def smoothed(rr, lo, hi):
            r = b * LAT_DEV + rr
            outer = passed[r, lo:hi] + passed[r + 4, lo:hi]
            inner = passed[r + 1, lo:hi] + passed[r + 3, lo:hi]
            return w0 * outer + w1 * inner + w2 * passed[r + 2, lo:hi]

        def put(g, value):
            for m in range(MON_DEV):
                staged[pl.ds(m * GROUPS + g, N_LON, stride=VSTRIDE), :] = value[8 * m : 8 * m + 8]

        for rr in range(LAT_DEV):
            put(rr, smoothed(rr, 0, WINDOWS))
        last = smoothed(LAT_DEV - 1, WINDOWS, 2 * WINDOWS)
        for q in range(7):
            even = smoothed(2 * q, WINDOWS, 2 * WINDOWS)
            odd = smoothed(2 * q + 1, WINDOWS, 2 * WINDOWS)
            value = jnp.where(laneb < SECOND, even, pltpu.roll(odd, SECOND, 1))
            if q < 4:
                tail = pltpu.roll(last, TAIL - 16 * q, 1)
                value = jnp.where(laneb < TAIL, value, tail)
            put(LAT_DEV + q, value)
        for l in range(N_LON):
            out[l, b] = staged[l * VSTRIDE : l * VSTRIDE + CHUNK, :].astype(jnp.bfloat16)

    bring.wait()
    for b in range(2):
        fetch(b).wait()
        lon_band(b)

    def band(b, carry):
        fetch(b).wait()
        lat_band(b - 2)
        lon_band(b)
        store(b - 2).start()
        return carry

    lax.fori_loop(2, N_LAT - 1, band, 0)
    lat_band(N_LAT - 3)
    lon_band(N_LAT - 1)
    store(N_LAT - 3).start()
    for b in (N_LAT - 2, N_LAT - 1):
        lat_band(b)
        store(b).start()
    for b in range(N_LAT):
        store(b).wait()


def smooth(widths, windows):
    out = pl.pallas_call(
        smooth_kernel,
        out_shape=jax.ShapeDtypeStruct((N_LON, N_LAT, CHUNK, LANES), jnp.bfloat16),
        in_specs=[pl.BlockSpec(memory_space=pltpu.VMEM), pl.BlockSpec(memory_space=pl.ANY)],
        out_specs=pl.BlockSpec(memory_space=pl.ANY),
        scratch_shapes=[
            pltpu.SMEM((N_LAT, LAT_DEV), jnp.int32),
            pltpu.VMEM((NLAT, SROWS, LANES), jnp.bfloat16),
            pltpu.VMEM((N_LON, N_LAT, CHUNK, LANES), jnp.bfloat16),
            pltpu.VMEM((HMAX, LANES), jnp.float32),
            pltpu.VMEM((HMAX, 2 * LANES, LANES), jnp.bfloat16),
            pltpu.VMEM((NLAT + 2 * HL, 2 * WINDOWS, LANES), jnp.float32),
            pltpu.VMEM((N_LON * VSTRIDE + 8, LANES), jnp.float32),
            pltpu.SemaphoreType.DMA((NLAT // 16,)),
            pltpu.SemaphoreType.DMA((N_LAT,)),
            pltpu.SemaphoreType.DMA,
        ],
        compiler_params=pltpu.CompilerParams(vmem_limit_bytes=SMOOTH_LIMIT),
        name="smooth",
    )(widths, windows)
    return out.reshape(N_LON * N_LAT, CHUNK, LANES)


def gram_kernel(core, landed, weight, mine, theirs, anomaly, wide, square):
    def widen(s, carry):
        wide[pl.ds(pl.multiple_of(s * CHUNK, 8), CHUNK), :] = landed[s].astype(jnp.float32)
        return carry

    lax.fori_loop(0, N_LON * N_LAT, widen, 0, unroll=4)
    lane = lax.broadcasted_iota(jnp.int32, (1, LANES), 1)
    for g in range(GROUPS):
        if g < LAT_DEV:
            scale = weight[g : g + 1, :LANES]
        else:
            q = g - LAT_DEV
            scale = weight[2 * q : 2 * q + 1, LANES:]
            scale = scale + pltpu.roll(weight[2 * q + 1 : 2 * q + 2, LANES:], SECOND, 1)
            if q < 4:
                last = weight[LAT_DEV - 1 : LAT_DEV, LANES:]
                last = jnp.where((lane >= 16 * q) & (lane < 16 * q + 16), last, 0.0)
                scale = scale + pltpu.roll(last, TAIL - 16 * q, 1)
        cells = wide[pl.ds(g, MONTHS, stride=GROUPS), :]
        mean = jnp.sum(cells, axis=0, keepdims=True) * (1.0 / MONTHS)
        anomaly[:, g * LANES : (g + 1) * LANES] = ((cells - mean) * scale).astype(jnp.bfloat16)
    for i, j in ((0, 0), (0, 1), (1, 1)):
        block = lax.dot_general(
            anomaly[i * ROWB : (i + 1) * ROWB, :],
            anomaly[j * ROWB : (j + 1) * ROWB, :],
            (((1,), (1,)), ((), ())),
            preferred_element_type=jnp.float32,
        )
        for n, (bi, bj) in enumerate(BLOCKS):
            if bi // 2 == i and bj // 2 == j:
                a, c = (bi % 2) * LANES, (bj % 2) * LANES
                square[...] = block[a : a + LANES, c : c + LANES]
                for ref, half in ((mine, core[0]), (theirs, 1 - core[0])):
                    rows = pl.ds(pl.multiple_of(half * HALF, HALF), HALF)
                    ref[pl.ds(n, HALF, stride=PACK), :] = square[rows, :]


def gram_terms(core, landed, weight):
    part = jax.ShapeDtypeStruct((HALF * PACK, LANES), jnp.float32)
    return pl.pallas_call(
        gram_kernel,
        out_shape=(part, part, jax.ShapeDtypeStruct((MONTHS, GROUPS * LANES), jnp.bfloat16)),
        in_specs=[
            pl.BlockSpec(memory_space=pltpu.SMEM),
            pl.BlockSpec(memory_space=pltpu.VMEM),
            pl.BlockSpec(memory_space=pltpu.VMEM),
        ],
        out_specs=(pl.BlockSpec(memory_space=pltpu.VMEM),) * 3,
        scratch_shapes=[
            pltpu.VMEM((N_LON * N_LAT * CHUNK, LANES), jnp.float32),
            pltpu.VMEM((LANES, LANES), jnp.float32),
        ],
        compiler_params=pltpu.CompilerParams(vmem_limit_bytes=32 * 1024 * 1024),
        name="gram_terms",
    )(core, landed, weight)


def turn_kernel(anomaly, turned):
    for g in range(GROUPS):
        turned[g * LANES : (g + 1) * LANES, :] = anomaly[:, g * LANES : (g + 1) * LANES].T


def turn(anomaly):
    return pl.pallas_call(
        turn_kernel,
        out_shape=jax.ShapeDtypeStruct((GROUPS * LANES, MONTHS), jnp.bfloat16),
        in_specs=[pl.BlockSpec(memory_space=pltpu.VMEM)],
        out_specs=pl.BlockSpec(memory_space=pltpu.VMEM),
        compiler_params=pltpu.CompilerParams(vmem_limit_bytes=16 * 1024 * 1024),
        cost_estimate=pl.CostEstimate(flops=2000000000, bytes_accessed=6000000, transcendentals=0),
        name="turn",
    )(anomaly)


def add_kernel(terms, out):
    step = 4 * PACK
    total = terms[0:step, :]
    for s in range(1, HALF // 4):
        total = total + terms[s * step : (s + 1) * step, :]
    row = total[0:PACK] + total[PACK : 2 * PACK] + total[2 * PACK : 3 * PACK] + total[3 * PACK :]
    total = jnp.concatenate([row] * 4, axis=0)
    for s in range(HALF // 4):
        out[s * step : (s + 1) * step, :] = total


def add_terms(terms):
    return pl.pallas_call(
        add_kernel,
        out_shape=jax.ShapeDtypeStruct(terms.shape, jnp.float32),
        in_specs=[pl.BlockSpec(memory_space=pltpu.VMEM)],
        out_specs=pl.BlockSpec(memory_space=pltpu.VMEM),
        compiler_params=pltpu.CompilerParams(vmem_limit_bytes=8 * 1024 * 1024),
        name="add_terms",
    )(terms)


STEP = (2.25, -2.4375, 1.6875, -0.5625, 0.0625)
ROWB = 256
MIRROR = True


def root_kernel(core, mine, theirs, anomaly, patterns_hbm, whitener_hbm, patterns, whitener, ws, hs, ps, ss, zs, wb, out_sems):
    for n, (bi, bj) in enumerate(BLOCKS):
        for ref, half in ((mine, core[0]), (theirs, 1 - core[0])):
            rows = pl.ds(pl.multiple_of(bi * LANES + half * HALF, HALF), HALF)
            whitener[rows, bj * LANES : (bj + 1) * LANES] = ref[pl.ds(n, HALF, stride=PACK), :]
        if bi != bj:
            block = whitener[bi * LANES : (bi + 1) * LANES, bj * LANES : (bj + 1) * LANES]
            whitener[bj * LANES : (bj + 1) * LANES, bi * LANES : (bi + 1) * LANES] = block.T
    gram = whitener[...]
    squares = jnp.sum(gram * gram, axis=0, keepdims=True)
    frobenius = jnp.sqrt(jnp.sum(squares, axis=1, keepdims=True) + 1e-06)
    final_scale = jnp.sqrt(float(NLAT * NLON) / frobenius)

    def split(ref, start, value):
        size = value.shape[0]
        high = value.astype(jnp.bfloat16)
        ref[start : start + size, :] = high
        ref[MONTHS + start : MONTHS + start + size, :] = (value - high.astype(jnp.float32)).astype(jnp.bfloat16)
        if ref.shape[0] == 3 * MONTHS:
            ref[2 * MONTHS + start : 2 * MONTHS + start + size, :] = high

    def join(ref, start):
        high = ref[start : start + ROWB, :].astype(jnp.float32)
        return high + ref[MONTHS + start : MONTHS + start + ROWB, :].astype(jnp.float32)

    def product(left, right):
        def rows(start):
            high = left[start : start + ROWB, :]
            low = left[MONTHS + start : MONTHS + start + ROWB, :]
            return jnp.concatenate([high, high, low], axis=1)

        upper = jnp.dot(rows(0), right[...], preferred_element_type=jnp.float32)
        if not MIRROR:
            return upper, jnp.dot(rows(ROWB), right[...], preferred_element_type=jnp.float32)
        corner = jnp.dot(rows(ROWB), right[:, ROWB:], preferred_element_type=jnp.float32)
        return upper, jnp.concatenate([upper[:, ROWB:].T, corner], axis=1)

    def plus_eye(value, start, scale):
        row = lax.broadcasted_iota(jnp.int32, value.shape, 0) + start
        column = lax.broadcasted_iota(jnp.int32, value.shape, 1)
        return jnp.where(row == column, value + scale, value)

    split(ws, 0, gram * (1.0 / frobenius))
    c0, c1, c2, c3, c4 = STEP
    last = ITERS // 2 - 1

    def double_step(k):
        for n, square in enumerate(product(ws, ws)):
            start = n * ROWB
            split(ss, start, square)
            split(hs, start, plus_eye(c3 * join(ws, start) + c4 * square, start, c2))
        for n, value in enumerate(product(ss, hs)):
            start = n * ROWB
            value = plus_eye(value + c1 * join(ws, start), start, c0)
            split(ps, start, value)
            if k == 0:
                split(zs, start, value)

        if k > 0:
            for n, value in enumerate(product(zs, ps)):
                if k < last:
                    split(zs, n * ROWB, value)
                else:
                    whitener[n * ROWB : (n + 1) * ROWB, :] = value * final_scale

        if k < last:
            for n, value in enumerate(product(ws, ps)):
                split(ss, n * ROWB, value)
            for n, value in enumerate(product(ss, ps)):
                split(ws, n * ROWB, value)

    for k in range(last + 1):
        double_step(k)
    copies = [pltpu.make_async_copy(whitener, whitener_hbm, out_sems.at[LAT_DEV])]
    copies[0].start()
    wb[...] = whitener[...].astype(jnp.bfloat16)

    def group(g):
        return lax.dot_general(
            anomaly[g * LANES : (g + 1) * LANES, :],
            wb[...],
            (((1,), (0,)), ((), ())),
            preferred_element_type=jnp.float32,
        ).astype(jnp.bfloat16)

    def finish(r):
        copy = pltpu.make_async_copy(patterns.at[r], patterns_hbm.at[r], out_sems.at[r])
        copy.start()
        copies.append(copy)

    for q in range(7):
        value = group(LAT_DEV + q)
        patterns[2 * q, LANES:, :] = value[0 : LON_DEV - LANES]
        patterns[2 * q + 1, LANES:, :] = value[SECOND : SECOND + LON_DEV - LANES]
        if q < 4:
            first = LANES + 16 * q
            size = min(16, LON_DEV - first)
            patterns[LAT_DEV - 1, first : first + size, :] = value[TAIL : TAIL + size]
        for r in (2 * q, 2 * q + 1):
            patterns[r, 0:LANES, :] = group(r)
            finish(r)
    patterns[LAT_DEV - 1, 0:LANES, :] = group(LAT_DEV - 1)
    finish(LAT_DEV - 1)
    for copy in copies:
        copy.wait()


def root_and_patterns(core, mine, theirs, turned):
    return pl.pallas_call(
        root_kernel,
        out_shape=(
            jax.ShapeDtypeStruct((LAT_DEV, LON_DEV, MONTHS), jnp.bfloat16),
            jax.ShapeDtypeStruct((MONTHS, MONTHS), jnp.float32),
        ),
        in_specs=[
            pl.BlockSpec(memory_space=pltpu.SMEM),
            pl.BlockSpec(memory_space=pltpu.VMEM),
            pl.BlockSpec(memory_space=pltpu.VMEM),
            pl.BlockSpec(memory_space=pltpu.VMEM),
        ],
        out_specs=(pl.BlockSpec(memory_space=pl.ANY),) * 2,
        scratch_shapes=[
            pltpu.VMEM((LAT_DEV, LON_DEV, MONTHS), jnp.bfloat16),
            pltpu.VMEM((MONTHS, MONTHS), jnp.float32),
            pltpu.VMEM((3 * MONTHS, MONTHS), jnp.bfloat16),
            pltpu.VMEM((3 * MONTHS, MONTHS), jnp.bfloat16),
            pltpu.VMEM((3 * MONTHS, MONTHS), jnp.bfloat16),
            pltpu.VMEM((2 * MONTHS, MONTHS), jnp.bfloat16),
            pltpu.VMEM((2 * MONTHS, MONTHS), jnp.bfloat16),
            pltpu.VMEM((MONTHS, MONTHS), jnp.bfloat16),
            pltpu.SemaphoreType.DMA((LAT_DEV + 1,)),
        ],
        compiler_params=pltpu.CompilerParams(vmem_limit_bytes=32 * 1024 * 1024),
        name="root_and_patterns",
    )(core, mine, theirs, turned)


def exchange(pieces, axes):
    return lax.all_to_all(pieces, axes, split_axis=0, concat_axis=0, tiled=True)


def exchange_packed(packed):
    pieces = packed.reshape(HALF, PACK // 2, 2, LANES)
    return exchange(pieces, SAME_CORE).reshape(packed.shape)


def swap_cores(x):
    return lax.ppermute(x, "core", [(0, 1), (1, 0)])


def local(monthly_field, half_width, land_mask):
    widths = exchange(jnp.broadcast_to(half_width, (N_LAT, 1, LAT_DEV)), LAT).reshape(N_LAT, LAT_DEV)
    windows = cut_windows(monthly_field)
    landed = exchange(smooth(widths, windows), BOTH)
    row_index = lax.axis_index(LAT) * LAT_DEV + jnp.arange(LAT_DEV)
    latitude = math.pi * ((row_index.astype(jnp.float32) + 0.5) / NLAT - 0.5)
    weight = jnp.sqrt(jnp.cos(latitude))[:, None] * land_mask.astype(jnp.float32)
    weight = jnp.pad(weight, ((0, 0), (0, 2 * LANES - LON_DEV)))
    core = lax.axis_index("core").reshape(1)
    mine, theirs, anomaly = gram_terms(core, landed, weight)
    terms = exchange_packed(mine + swap_cores(theirs))
    turned = turn(anomaly)
    mine = exchange_packed(add_terms(terms))
    patterns, whitener = root_and_patterns(core, mine, swap_cores(mine), turned)
    return (jnp.transpose(patterns, (2, 0, 1)), whitener)


def solution(mesh):
    fine = Mesh(mesh.devices.reshape(N_LON, N_LAT // 2, 2), BOTH)
    placed = (P(BOTH, None, None), P(LAT), P(LAT, "lon"))
    return jax.shard_map(
        local, mesh=fine, in_specs=placed, out_specs=(P(None, LAT, "lon"), P()), check_vma=False
    )
```

```python
import math

import jax
import jax.numpy as jnp
import numpy as np
from jax import lax
from jax.experimental import pallas as pl
from jax.experimental.pallas import tpu as pltpu
from jax.sharding import Mesh
from jax.sharding import PartitionSpec as P

HMAX = 64
HL = 2
ITERS = 8
LAT = ("chip", "core")
BOTH = ("lon", "chip", "core")
SAME_CORE = ("lon", "chip")
HALF = 64
N_LON = 8
N_LAT = 16
NLAT = 240
NLON = 1440
MONTHS = 512
MON_DEV = 4
LAT_DEV = 15
LON_DEV = 180
LANES = 128
GROUPS = 22
SECOND = 56
TAIL = 112
CHUNK = MON_DEV * GROUPS
WINDOWS = MON_DEV * N_LON
SROWS = 3 * WINDOWS
SSTRIDE = 97
VSTRIDE = 89
BLOCKS = [(i, j) for i in range(4) for j in range(i, 4)]
PACK = len(BLOCKS)
VMEM_LIMIT = 60 * 1024 * 1024
SMOOTH_LIMIT = 52 * 1024 * 1024


def lat_taps():
    offsets = np.arange(-HL, HL + 1).astype(np.float32)
    taps = np.exp(-(offsets * offsets) / np.float32(2.0)).astype(np.float32)
    taps = taps / taps.sum(dtype=np.float32)
    return [float(t) for t in taps.astype(jnp.bfloat16).astype(np.float32)]


def windows_kernel(field_hbm, out_hbm, field, windows, staged, in_sems, out_sems):
    steps = windows.shape[0] // 16
    lane16 = lax.broadcasted_iota(jnp.int32, (16, LANES), 1)

    def fetch(i):
        rows = pl.ds(pl.multiple_of(i * 16, 16), 16)
        return pltpu.make_async_copy(field_hbm.at[:, rows, :], field.at[:, rows, :], in_sems.at[i])

    def store(i):
        rows = pl.ds(pl.multiple_of(i * 16, 16), 16)
        return pltpu.make_async_copy(windows.at[rows], out_hbm.at[rows], out_sems.at[i])

    for i in range(steps):
        fetch(i).start()

    def step(i, carry):
        fetch(i).wait()
        for m in range(MON_DEV):
            rows = field[m, pl.ds(pl.multiple_of(i * 16, 16), 16), :]
            ring = jnp.concatenate([rows, rows[:, :352]], axis=1)
            for l in range(N_LON):
                start = (LON_DEV * l - HMAX) % NLON
                first_tile, shift = start // LANES, start % LANES
                tiles = [ring[:, t * LANES : (t + 1) * LANES] for t in range(first_tile, first_tile + 4)]
                if shift:
                    tiles = [pltpu.roll(t, LANES - shift, 1) for t in tiles]
                for j in range(3):
                    piece = jnp.where(lane16 < LANES - shift, tiles[j], tiles[j + 1]) if shift else tiles[j]
                    piece = piece.astype(jnp.float32)
                    for half in range(2):
                        first = half * 8 * SSTRIDE + j * WINDOWS + m * N_LON + l
                        staged[pl.ds(first, 8, stride=SSTRIDE), :] = piece[half * 8 : half * 8 + 8]
        for r in range(16):
            windows[i * 16 + r] = staged[r * SSTRIDE : r * SSTRIDE + SROWS, :].astype(jnp.bfloat16)
        store(i).start()
        return carry

    lax.fori_loop(0, steps, step, 0)
    for i in range(steps):
        store(i).wait()


def cut_windows(field):
    steps = NLAT // 16
    return pl.pallas_call(
        windows_kernel,
        out_shape=jax.ShapeDtypeStruct((steps * 16, SROWS, LANES), jnp.bfloat16),
        in_specs=[pl.BlockSpec(memory_space=pl.ANY)],
        out_specs=pl.BlockSpec(memory_space=pl.ANY),
        scratch_shapes=[
            pltpu.VMEM((MON_DEV, steps * 16, NLON), jnp.bfloat16),
            pltpu.VMEM((steps * 16, SROWS, LANES), jnp.bfloat16),
            pltpu.VMEM((16 * SSTRIDE + 8, LANES), jnp.float32),
            pltpu.SemaphoreType.DMA((steps,)),
            pltpu.SemaphoreType.DMA((steps,)),
        ],
        compiler_params=pltpu.CompilerParams(vmem_limit_bytes=VMEM_LIMIT),
        cost_estimate=pl.CostEstimate(flops=3000000000, bytes_accessed=9000000, transcendentals=0),
        name="cut_windows",
    )(field)


def smooth_kernel(widths_in, windows_hbm, out_hbm, widths, windows, out, taps, table, passed, staged, in_sems, out_sems, sem):
    bring = pltpu.make_async_copy(widths_in, widths, sem)
    bring.start()


    def fetch(i):
        rows = pl.ds(pl.multiple_of(i * 16, 16), 16)
        return pltpu.make_async_copy(windows_hbm.at[rows], windows.at[rows], in_sems.at[i])

    def store(b):
        return pltpu.make_async_copy(out.at[:, b], out_hbm.at[:, b], out_sems.at[b])

    for i in range(NLAT // 16):
        fetch(i).start()
    reach = (lax.broadcasted_iota(jnp.int32, (HMAX, LANES), 0) + 1).astype(jnp.float32)
    offset = (lax.broadcasted_iota(jnp.int32, (HMAX, LANES), 1) - HMAX).astype(jnp.float32)
    spread = 0.5 * reach
    value = jnp.exp(-(offset * offset) / (2.0 * spread * spread))
    value = jnp.where(jnp.abs(offset) <= reach, value, 0.0)
    total = jnp.sum(value, axis=1, keepdims=True) + value[:, 0:1]
    taps[...] = (value / total).astype(jnp.bfloat16).astype(jnp.float32)
    sub = lax.broadcasted_iota(jnp.int32, (LANES, LANES), 0)
    lane = lax.broadcasted_iota(jnp.int32, (LANES, LANES), 1)
    upper = jnp.where(sub >= lane, 1.0, 0.0).astype(jnp.bfloat16)
    lower = jnp.where(sub <= lane, 1.0, 0.0).astype(jnp.bfloat16)

    def build_matrix(h, carry):
        spread_taps = jnp.broadcast_to(taps[pl.ds(h, 1), :], (LANES, LANES))
        ring = pltpu.roll(spread_taps, 0, 1, stride=1, stride_axis=0).astype(jnp.bfloat16)
        table[h, 0:LANES, :] = ring * upper
        table[h, LANES:, :] = ring * lower
        return carry

    lax.fori_loop(0, HMAX, build_matrix, 0, unroll=8)
    edge = jnp.zeros((HL, 2 * WINDOWS, LANES), jnp.float32)
    passed[0:HL] = edge
    passed[NLAT + HL : NLAT + 2 * HL] = edge

    def lon_band(b):
        for rr in range(LAT_DEV):
            r = b * LAT_DEV + rr
            lhs = windows[r]
            left = jnp.concatenate([lhs[: 2 * WINDOWS], lhs[WINDOWS:]], axis=1)
            right = table[widths[b, rr] - 1]
            res = jnp.dot(left, right, preferred_element_type=jnp.float32)
            passed[r + HL] = res.astype(jnp.bfloat16).astype(jnp.float32)

    w0, w1, w2 = lat_taps()[:3]
    laneb = lax.broadcasted_iota(jnp.int32, (WINDOWS, LANES), 1)

    def lat_band(b):
        def smoothed(rr, lo, hi):
            r = b * LAT_DEV + rr
            outer = passed[r, lo:hi] + passed[r + 4, lo:hi]
            inner = passed[r + 1, lo:hi] + passed[r + 3, lo:hi]
            return w0 * outer + w1 * inner + w2 * passed[r + 2, lo:hi]

        def put(g, value):
            for m in range(MON_DEV):
                staged[pl.ds(m * GROUPS + g, N_LON, stride=VSTRIDE), :] = value[8 * m : 8 * m + 8]

        for rr in range(LAT_DEV):
            put(rr, smoothed(rr, 0, WINDOWS))
        last = smoothed(LAT_DEV - 1, WINDOWS, 2 * WINDOWS)
        for q in range(7):
            even = smoothed(2 * q, WINDOWS, 2 * WINDOWS)
            odd = smoothed(2 * q + 1, WINDOWS, 2 * WINDOWS)
            value = jnp.where(laneb < SECOND, even, pltpu.roll(odd, SECOND, 1))
            if q < 4:
                tail = pltpu.roll(last, TAIL - 16 * q, 1)
                value = jnp.where(laneb < TAIL, value, tail)
            put(LAT_DEV + q, value)
        for l in range(N_LON):
            out[l, b] = staged[l * VSTRIDE : l * VSTRIDE + CHUNK, :].astype(jnp.bfloat16)

    bring.wait()
    for b in range(2):
        fetch(b).wait()
        lon_band(b)

    def band(b, carry):
        fetch(b).wait()
        lat_band(b - 2)
        lon_band(b)
        store(b - 2).start()
        return carry

    lax.fori_loop(2, N_LAT - 1, band, 0)
    lat_band(N_LAT - 3)
    lon_band(N_LAT - 1)
    store(N_LAT - 3).start()
    for b in (N_LAT - 2, N_LAT - 1):
        lat_band(b)
        store(b).start()
    for b in range(N_LAT):
        store(b).wait()


def smooth(widths, windows):
    out = pl.pallas_call(
        smooth_kernel,
        out_shape=jax.ShapeDtypeStruct((N_LON, N_LAT, CHUNK, LANES), jnp.bfloat16),
        in_specs=[pl.BlockSpec(memory_space=pltpu.VMEM), pl.BlockSpec(memory_space=pl.ANY)],
        out_specs=pl.BlockSpec(memory_space=pl.ANY),
        scratch_shapes=[
            pltpu.SMEM((N_LAT, LAT_DEV), jnp.int32),
            pltpu.VMEM((NLAT, SROWS, LANES), jnp.bfloat16),
            pltpu.VMEM((N_LON, N_LAT, CHUNK, LANES), jnp.bfloat16),
            pltpu.VMEM((HMAX, LANES), jnp.float32),
            pltpu.VMEM((HMAX, 2 * LANES, LANES), jnp.bfloat16),
            pltpu.VMEM((NLAT + 2 * HL, 2 * WINDOWS, LANES), jnp.float32),
            pltpu.VMEM((N_LON * VSTRIDE + 8, LANES), jnp.float32),
            pltpu.SemaphoreType.DMA((NLAT // 16,)),
            pltpu.SemaphoreType.DMA((N_LAT,)),
            pltpu.SemaphoreType.DMA,
        ],
        compiler_params=pltpu.CompilerParams(vmem_limit_bytes=SMOOTH_LIMIT),
        name="smooth",
    )(widths, windows)
    return out.reshape(N_LON * N_LAT, CHUNK, LANES)


def gram_kernel(core, landed, weight, mine, theirs, anomaly, wide, square):
    def widen(s, carry):
        wide[pl.ds(pl.multiple_of(s * CHUNK, 8), CHUNK), :] = landed[s].astype(jnp.float32)
        return carry

    lax.fori_loop(0, N_LON * N_LAT, widen, 0, unroll=4)
    lane = lax.broadcasted_iota(jnp.int32, (1, LANES), 1)
    for g in range(GROUPS):
        if g < LAT_DEV:
            scale = weight[g : g + 1, :LANES]
        else:
            q = g - LAT_DEV
            scale = weight[2 * q : 2 * q + 1, LANES:]
            scale = scale + pltpu.roll(weight[2 * q + 1 : 2 * q + 2, LANES:], SECOND, 1)
            if q < 4:
                last = weight[LAT_DEV - 1 : LAT_DEV, LANES:]
                last = jnp.where((lane >= 16 * q) & (lane < 16 * q + 16), last, 0.0)
                scale = scale + pltpu.roll(last, TAIL - 16 * q, 1)
        cells = wide[pl.ds(g, MONTHS, stride=GROUPS), :]
        mean = jnp.sum(cells, axis=0, keepdims=True) * (1.0 / MONTHS)
        anomaly[:, g * LANES : (g + 1) * LANES] = ((cells - mean) * scale).astype(jnp.bfloat16)
    for i, j in ((0, 0), (0, 1), (1, 1)):
        block = lax.dot_general(
            anomaly[i * ROWB : (i + 1) * ROWB, :],
            anomaly[j * ROWB : (j + 1) * ROWB, :],
            (((1,), (1,)), ((), ())),
            preferred_element_type=jnp.float32,
        )
        for n, (bi, bj) in enumerate(BLOCKS):
            if bi // 2 == i and bj // 2 == j:
                a, c = (bi % 2) * LANES, (bj % 2) * LANES
                square[...] = block[a : a + LANES, c : c + LANES]
                for ref, half in ((mine, core[0]), (theirs, 1 - core[0])):
                    rows = pl.ds(pl.multiple_of(half * HALF, HALF), HALF)
                    ref[pl.ds(n, HALF, stride=PACK), :] = square[rows, :]


def gram_terms(core, landed, weight):
    part = jax.ShapeDtypeStruct((HALF * PACK, LANES), jnp.float32)
    return pl.pallas_call(
        gram_kernel,
        out_shape=(part, part, jax.ShapeDtypeStruct((MONTHS, GROUPS * LANES), jnp.bfloat16)),
        in_specs=[
            pl.BlockSpec(memory_space=pltpu.SMEM),
            pl.BlockSpec(memory_space=pltpu.VMEM),
            pl.BlockSpec(memory_space=pltpu.VMEM),
        ],
        out_specs=(pl.BlockSpec(memory_space=pltpu.VMEM),) * 3,
        scratch_shapes=[
            pltpu.VMEM((N_LON * N_LAT * CHUNK, LANES), jnp.float32),
            pltpu.VMEM((LANES, LANES), jnp.float32),
        ],
        compiler_params=pltpu.CompilerParams(vmem_limit_bytes=32 * 1024 * 1024),
        name="gram_terms",
    )(core, landed, weight)


def turn_kernel(anomaly, turned):
    for g in range(GROUPS):
        turned[g * LANES : (g + 1) * LANES, :] = anomaly[:, g * LANES : (g + 1) * LANES].T


def turn(anomaly):
    return pl.pallas_call(
        turn_kernel,
        out_shape=jax.ShapeDtypeStruct((GROUPS * LANES, MONTHS), jnp.bfloat16),
        in_specs=[pl.BlockSpec(memory_space=pltpu.VMEM)],
        out_specs=pl.BlockSpec(memory_space=pltpu.VMEM),
        compiler_params=pltpu.CompilerParams(vmem_limit_bytes=16 * 1024 * 1024),
        cost_estimate=pl.CostEstimate(flops=2000000000, bytes_accessed=6000000, transcendentals=0),
        name="turn",
    )(anomaly)


def add_kernel(terms, out):
    step = 4 * PACK
    total = terms[0:step, :]
    for s in range(1, HALF // 4):
        total = total + terms[s * step : (s + 1) * step, :]
    row = total[0:PACK] + total[PACK : 2 * PACK] + total[2 * PACK : 3 * PACK] + total[3 * PACK :]
    total = jnp.concatenate([row] * 4, axis=0)
    for s in range(HALF // 4):
        out[s * step : (s + 1) * step, :] = total


def add_terms(terms):
    return pl.pallas_call(
        add_kernel,
        out_shape=jax.ShapeDtypeStruct(terms.shape, jnp.float32),
        in_specs=[pl.BlockSpec(memory_space=pltpu.VMEM)],
        out_specs=pl.BlockSpec(memory_space=pltpu.VMEM),
        compiler_params=pltpu.CompilerParams(vmem_limit_bytes=8 * 1024 * 1024),
        name="add_terms",
    )(terms)


STEP = (2.25, -2.4375, 1.6875, -0.5625, 0.0625)
ROWB = 256
MIRROR = True


def root_kernel(core, mine, theirs, anomaly, patterns_hbm, whitener_hbm, patterns, whitener, ws, hs, ps, ss, zs, wb, out_sems):
    for n, (bi, bj) in enumerate(BLOCKS):
        for ref, half in ((mine, core[0]), (theirs, 1 - core[0])):
            rows = pl.ds(pl.multiple_of(bi * LANES + half * HALF, HALF), HALF)
            whitener[rows, bj * LANES : (bj + 1) * LANES] = ref[pl.ds(n, HALF, stride=PACK), :]
        if bi != bj:
            block = whitener[bi * LANES : (bi + 1) * LANES, bj * LANES : (bj + 1) * LANES]
            whitener[bj * LANES : (bj + 1) * LANES, bi * LANES : (bi + 1) * LANES] = block.T
    gram = whitener[...]
    squares = jnp.sum(gram * gram, axis=0, keepdims=True)
    frobenius = jnp.sqrt(jnp.sum(squares, axis=1, keepdims=True) + 1e-06)
    final_scale = jnp.sqrt(float(NLAT * NLON) / frobenius)

    def split(ref, start, value):
        size = value.shape[0]
        high = value.astype(jnp.bfloat16)
        ref[start : start + size, :] = high
        ref[MONTHS + start : MONTHS + start + size, :] = (value - high.astype(jnp.float32)).astype(jnp.bfloat16)
        if ref.shape[0] == 3 * MONTHS:
            ref[2 * MONTHS + start : 2 * MONTHS + start + size, :] = high

    def join(ref, start):
        high = ref[start : start + ROWB, :].astype(jnp.float32)
        return high + ref[MONTHS + start : MONTHS + start + ROWB, :].astype(jnp.float32)

    def product(left, right):
        def rows(start):
            high = left[start : start + ROWB, :]
            low = left[MONTHS + start : MONTHS + start + ROWB, :]
            return jnp.concatenate([high, high, low], axis=1)

        upper = jnp.dot(rows(0), right[...], preferred_element_type=jnp.float32)
        if not MIRROR:
            return upper, jnp.dot(rows(ROWB), right[...], preferred_element_type=jnp.float32)
        corner = jnp.dot(rows(ROWB), right[:, ROWB:], preferred_element_type=jnp.float32)
        return upper, jnp.concatenate([upper[:, ROWB:].T, corner], axis=1)

    def plus_eye(value, start, scale):
        row = lax.broadcasted_iota(jnp.int32, value.shape, 0) + start
        column = lax.broadcasted_iota(jnp.int32, value.shape, 1)
        return jnp.where(row == column, value + scale, value)

    split(ws, 0, gram * (1.0 / frobenius))
    c0, c1, c2, c3, c4 = STEP
    last = ITERS // 2 - 1

    def double_step(k):
        for n, square in enumerate(product(ws, ws)):
            start = n * ROWB
            split(ss, start, square)
            split(hs, start, plus_eye(c3 * join(ws, start) + c4 * square, start, c2))
        for n, value in enumerate(product(ss, hs)):
            start = n * ROWB
            value = plus_eye(value + c1 * join(ws, start), start, c0)
            split(ps, start, value)
            if k == 0:
                split(zs, start, value)

        if k > 0:
            for n, value in enumerate(product(zs, ps)):
                if k < last:
                    split(zs, n * ROWB, value)
                else:
                    whitener[n * ROWB : (n + 1) * ROWB, :] = value * final_scale

        if k < last:
            for n, value in enumerate(product(ws, ps)):
                split(ss, n * ROWB, value)
            for n, value in enumerate(product(ss, ps)):
                split(ws, n * ROWB, value)

    for k in range(last + 1):
        double_step(k)
    copies = [pltpu.make_async_copy(whitener, whitener_hbm, out_sems.at[LAT_DEV])]
    copies[0].start()
    wb[...] = whitener[...].astype(jnp.bfloat16)

    def group(g, count=1):
        return lax.dot_general(
            anomaly[g * LANES : (g + count) * LANES, :],
            wb[...],
            (((1,), (0,)), ((), ())),
            preferred_element_type=jnp.float32,
        ).astype(jnp.bfloat16)

    def finish(r):
        copy = pltpu.make_async_copy(patterns.at[r], patterns_hbm.at[r], out_sems.at[r])
        copy.start()
        copies.append(copy)

    for q in range(7):
        value = group(LAT_DEV + q)
        patterns[2 * q, LANES:, :] = value[0 : LON_DEV - LANES]
        patterns[2 * q + 1, LANES:, :] = value[SECOND : SECOND + LON_DEV - LANES]
        if q < 4:
            first = LANES + 16 * q
            size = min(16, LON_DEV - first)
            patterns[LAT_DEV - 1, first : first + size, :] = value[TAIL : TAIL + size]
        pair = group(2 * q, 2)
        for n in range(2):
            patterns[2 * q + n, 0:LANES, :] = pair[n * LANES : (n + 1) * LANES]
            finish(2 * q + n)
    patterns[LAT_DEV - 1, 0:LANES, :] = group(LAT_DEV - 1)
    finish(LAT_DEV - 1)
    for copy in copies:
        copy.wait()


def root_and_patterns(core, mine, theirs, turned):
    return pl.pallas_call(
        root_kernel,
        out_shape=(
            jax.ShapeDtypeStruct((LAT_DEV, LON_DEV, MONTHS), jnp.bfloat16),
            jax.ShapeDtypeStruct((MONTHS, MONTHS), jnp.float32),
        ),
        in_specs=[
            pl.BlockSpec(memory_space=pltpu.SMEM),
            pl.BlockSpec(memory_space=pltpu.VMEM),
            pl.BlockSpec(memory_space=pltpu.VMEM),
            pl.BlockSpec(memory_space=pltpu.VMEM),
        ],
        out_specs=(pl.BlockSpec(memory_space=pl.ANY),) * 2,
        scratch_shapes=[
            pltpu.VMEM((LAT_DEV, LON_DEV, MONTHS), jnp.bfloat16),
            pltpu.VMEM((MONTHS, MONTHS), jnp.float32),
            pltpu.VMEM((3 * MONTHS, MONTHS), jnp.bfloat16),
            pltpu.VMEM((3 * MONTHS, MONTHS), jnp.bfloat16),
            pltpu.VMEM((3 * MONTHS, MONTHS), jnp.bfloat16),
            pltpu.VMEM((2 * MONTHS, MONTHS), jnp.bfloat16),
            pltpu.VMEM((2 * MONTHS, MONTHS), jnp.bfloat16),
            pltpu.VMEM((MONTHS, MONTHS), jnp.bfloat16),
            pltpu.SemaphoreType.DMA((LAT_DEV + 1,)),
        ],
        compiler_params=pltpu.CompilerParams(vmem_limit_bytes=32 * 1024 * 1024),
        name="root_and_patterns",
    )(core, mine, theirs, turned)


def exchange(pieces, axes):
    return lax.all_to_all(pieces, axes, split_axis=0, concat_axis=0, tiled=True)


def exchange_packed(packed):
    pieces = packed.reshape(HALF, PACK // 2, 2, LANES)
    return exchange(pieces, SAME_CORE).reshape(packed.shape)


def swap_cores(x):
    return lax.ppermute(x, "core", [(0, 1), (1, 0)])


def local(monthly_field, half_width, land_mask):
    widths = exchange(jnp.broadcast_to(half_width, (N_LAT, 1, LAT_DEV)), LAT).reshape(N_LAT, LAT_DEV)
    windows = cut_windows(monthly_field)
    landed = exchange(smooth(widths, windows), BOTH)
    row_index = lax.axis_index(LAT) * LAT_DEV + jnp.arange(LAT_DEV)
    latitude = math.pi * ((row_index.astype(jnp.float32) + 0.5) / NLAT - 0.5)
    weight = jnp.sqrt(jnp.cos(latitude))[:, None] * land_mask.astype(jnp.float32)
    weight = jnp.pad(weight, ((0, 0), (0, 2 * LANES - LON_DEV)))
    core = lax.axis_index("core").reshape(1)
    mine, theirs, anomaly = gram_terms(core, landed, weight)
    terms = exchange_packed(mine + swap_cores(theirs))
    turned = turn(anomaly)
    mine = exchange_packed(add_terms(terms))
    patterns, whitener = root_and_patterns(core, mine, swap_cores(mine), turned)
    return (jnp.transpose(patterns, (2, 0, 1)), whitener)


def solution(mesh):
    fine = Mesh(mesh.devices.reshape(N_LON, N_LAT // 2, 2), BOTH)
    placed = (P(BOTH, None, None), P(LAT), P(LAT, "lon"))
    return jax.shard_map(
        local, mesh=fine, in_specs=placed, out_specs=(P(None, LAT, "lon"), P()), check_vma=False
    )
```

```python
import math

import jax
import jax.numpy as jnp
import numpy as np
from jax import lax
from jax.experimental import pallas as pl
from jax.experimental.pallas import tpu as pltpu
from jax.sharding import Mesh
from jax.sharding import PartitionSpec as P

HMAX = 64
HL = 2
ITERS = 8
LAT = ("chip", "core")
BOTH = ("lon", "chip", "core")
SAME_CORE = ("lon", "chip")
HALF = 64
N_LON = 8
N_LAT = 16
NLAT = 240
NLON = 1440
MONTHS = 512
MON_DEV = 4
LAT_DEV = 15
LON_DEV = 180
LANES = 128
GROUPS = 22
SECOND = 56
TAIL = 112
CHUNK = MON_DEV * GROUPS
WINDOWS = MON_DEV * N_LON
SROWS = 3 * WINDOWS
SSTRIDE = 97
VSTRIDE = 89
BLOCKS = [(i, j) for i in range(4) for j in range(i, 4)]
PACK = len(BLOCKS)
VMEM_LIMIT = 60 * 1024 * 1024
SMOOTH_LIMIT = 52 * 1024 * 1024


def lat_taps():
    offsets = np.arange(-HL, HL + 1).astype(np.float32)
    taps = np.exp(-(offsets * offsets) / np.float32(2.0)).astype(np.float32)
    taps = taps / taps.sum(dtype=np.float32)
    return [float(t) for t in taps.astype(jnp.bfloat16).astype(np.float32)]


def windows_kernel(field_hbm, out_hbm, field, windows, staged, in_sems, out_sems):
    steps = windows.shape[0] // 16
    lane16 = lax.broadcasted_iota(jnp.int32, (16, LANES), 1)

    def fetch(i):
        rows = pl.ds(pl.multiple_of(i * 16, 16), 16)
        return pltpu.make_async_copy(field_hbm.at[:, rows, :], field.at[:, rows, :], in_sems.at[i])

    def store(i):
        rows = pl.ds(pl.multiple_of(i * 16, 16), 16)
        return pltpu.make_async_copy(windows.at[rows], out_hbm.at[rows], out_sems.at[i])

    for i in range(steps):
        fetch(i).start()

    def step(i, carry):
        fetch(i).wait()
        for m in range(MON_DEV):
            rows = field[m, pl.ds(pl.multiple_of(i * 16, 16), 16), :]
            ring = jnp.concatenate([rows, rows[:, :352]], axis=1)
            for l in range(N_LON):
                start = (LON_DEV * l - HMAX) % NLON
                first_tile, shift = start // LANES, start % LANES
                tiles = [ring[:, t * LANES : (t + 1) * LANES] for t in range(first_tile, first_tile + 4)]
                if shift:
                    tiles = [pltpu.roll(t, LANES - shift, 1) for t in tiles]
                for j in range(3):
                    piece = jnp.where(lane16 < LANES - shift, tiles[j], tiles[j + 1]) if shift else tiles[j]
                    piece = piece.astype(jnp.float32)
                    for half in range(2):
                        first = half * 8 * SSTRIDE + j * WINDOWS + m * N_LON + l
                        staged[pl.ds(first, 8, stride=SSTRIDE), :] = piece[half * 8 : half * 8 + 8]
        for r in range(16):
            windows[i * 16 + r] = staged[r * SSTRIDE : r * SSTRIDE + SROWS, :].astype(jnp.bfloat16)
        store(i).start()
        return carry

    lax.fori_loop(0, steps, step, 0)
    for i in range(steps):
        store(i).wait()


def cut_windows(field):
    steps = NLAT // 16
    return pl.pallas_call(
        windows_kernel,
        out_shape=jax.ShapeDtypeStruct((steps * 16, SROWS, LANES), jnp.bfloat16),
        in_specs=[pl.BlockSpec(memory_space=pl.ANY)],
        out_specs=pl.BlockSpec(memory_space=pl.ANY),
        scratch_shapes=[
            pltpu.VMEM((MON_DEV, steps * 16, NLON), jnp.bfloat16),
            pltpu.VMEM((steps * 16, SROWS, LANES), jnp.bfloat16),
            pltpu.VMEM((16 * SSTRIDE + 8, LANES), jnp.float32),
            pltpu.SemaphoreType.DMA((steps,)),
            pltpu.SemaphoreType.DMA((steps,)),
        ],
        compiler_params=pltpu.CompilerParams(vmem_limit_bytes=VMEM_LIMIT),
        cost_estimate=pl.CostEstimate(flops=3000000000, bytes_accessed=9000000, transcendentals=0),
        name="cut_windows",
    )(field)


def smooth_kernel(widths_in, windows_hbm, out_hbm, widths, windows, out, taps, table, passed, staged, in_sems, out_sems, sem):
    bring = pltpu.make_async_copy(widths_in, widths, sem)
    bring.start()


    def fetch(i):
        rows = pl.ds(pl.multiple_of(i * 16, 16), 16)
        return pltpu.make_async_copy(windows_hbm.at[rows], windows.at[rows], in_sems.at[i])

    def store(b):
        return pltpu.make_async_copy(out.at[:, b], out_hbm.at[:, b], out_sems.at[b])

    for i in range(NLAT // 16):
        fetch(i).start()
    reach = (lax.broadcasted_iota(jnp.int32, (HMAX, LANES), 0) + 1).astype(jnp.float32)
    offset = (lax.broadcasted_iota(jnp.int32, (HMAX, LANES), 1) - HMAX).astype(jnp.float32)
    spread = 0.5 * reach
    value = jnp.exp(-(offset * offset) / (2.0 * spread * spread))
    value = jnp.where(jnp.abs(offset) <= reach, value, 0.0)
    total = jnp.sum(value, axis=1, keepdims=True) + value[:, 0:1]
    taps[...] = (value / total).astype(jnp.bfloat16).astype(jnp.float32)
    sub = lax.broadcasted_iota(jnp.int32, (LANES, LANES), 0)
    lane = lax.broadcasted_iota(jnp.int32, (LANES, LANES), 1)
    upper = jnp.where(sub >= lane, 1.0, 0.0).astype(jnp.bfloat16)
    lower = jnp.where(sub <= lane, 1.0, 0.0).astype(jnp.bfloat16)

    def build_matrix(h, carry):
        spread_taps = jnp.broadcast_to(taps[pl.ds(h, 1), :], (LANES, LANES))
        ring = pltpu.roll(spread_taps, 0, 1, stride=1, stride_axis=0).astype(jnp.bfloat16)
        table[h, 0:LANES, :] = ring * upper
        table[h, LANES:, :] = ring * lower
        return carry

    lax.fori_loop(0, HMAX, build_matrix, 0, unroll=8)
    edge = jnp.zeros((HL, 2 * WINDOWS, LANES), jnp.float32)
    passed[0:HL] = edge
    passed[NLAT + HL : NLAT + 2 * HL] = edge

    def lon_band(b):
        for rr in range(LAT_DEV):
            r = b * LAT_DEV + rr
            lhs = windows[r]
            left = jnp.concatenate([lhs[: 2 * WINDOWS], lhs[WINDOWS:]], axis=1)
            right = table[widths[b, rr] - 1]
            res = jnp.dot(left, right, preferred_element_type=jnp.float32)
            passed[r + HL] = res.astype(jnp.bfloat16).astype(jnp.float32)

    w0, w1, w2 = lat_taps()[:3]
    laneb = lax.broadcasted_iota(jnp.int32, (WINDOWS, LANES), 1)

    def lat_band(b):
        def smoothed(rr, lo, hi):
            r = b * LAT_DEV + rr
            outer = passed[r, lo:hi] + passed[r + 4, lo:hi]
            inner = passed[r + 1, lo:hi] + passed[r + 3, lo:hi]
            return w0 * outer + w1 * inner + w2 * passed[r + 2, lo:hi]

        def put(g, value):
            for m in range(MON_DEV):
                staged[pl.ds(m * GROUPS + g, N_LON, stride=VSTRIDE), :] = value[8 * m : 8 * m + 8]

        for rr in range(LAT_DEV):
            put(rr, smoothed(rr, 0, WINDOWS))
        last = smoothed(LAT_DEV - 1, WINDOWS, 2 * WINDOWS)
        for q in range(7):
            even = smoothed(2 * q, WINDOWS, 2 * WINDOWS)
            odd = smoothed(2 * q + 1, WINDOWS, 2 * WINDOWS)
            value = jnp.where(laneb < SECOND, even, pltpu.roll(odd, SECOND, 1))
            if q < 4:
                tail = pltpu.roll(last, TAIL - 16 * q, 1)
                value = jnp.where(laneb < TAIL, value, tail)
            put(LAT_DEV + q, value)
        for l in range(N_LON):
            out[l, b] = staged[l * VSTRIDE : l * VSTRIDE + CHUNK, :].astype(jnp.bfloat16)

    bring.wait()
    for b in range(2):
        fetch(b).wait()
        lon_band(b)

    def band(b, carry):
        fetch(b).wait()
        lat_band(b - 2)
        lon_band(b)
        store(b - 2).start()
        return carry

    lax.fori_loop(2, N_LAT - 1, band, 0)
    lat_band(N_LAT - 3)
    lon_band(N_LAT - 1)
    store(N_LAT - 3).start()
    for b in (N_LAT - 2, N_LAT - 1):
        lat_band(b)
        store(b).start()
    for b in range(N_LAT):
        store(b).wait()


def smooth(widths, windows):
    out = pl.pallas_call(
        smooth_kernel,
        out_shape=jax.ShapeDtypeStruct((N_LON, N_LAT, CHUNK, LANES), jnp.bfloat16),
        in_specs=[pl.BlockSpec(memory_space=pltpu.VMEM), pl.BlockSpec(memory_space=pl.ANY)],
        out_specs=pl.BlockSpec(memory_space=pl.ANY),
        scratch_shapes=[
            pltpu.SMEM((N_LAT, LAT_DEV), jnp.int32),
            pltpu.VMEM((NLAT, SROWS, LANES), jnp.bfloat16),
            pltpu.VMEM((N_LON, N_LAT, CHUNK, LANES), jnp.bfloat16),
            pltpu.VMEM((HMAX, LANES), jnp.float32),
            pltpu.VMEM((HMAX, 2 * LANES, LANES), jnp.bfloat16),
            pltpu.VMEM((NLAT + 2 * HL, 2 * WINDOWS, LANES), jnp.float32),
            pltpu.VMEM((N_LON * VSTRIDE + 8, LANES), jnp.float32),
            pltpu.SemaphoreType.DMA((NLAT // 16,)),
            pltpu.SemaphoreType.DMA((N_LAT,)),
            pltpu.SemaphoreType.DMA,
        ],
        compiler_params=pltpu.CompilerParams(vmem_limit_bytes=SMOOTH_LIMIT),
        name="smooth",
    )(widths, windows)
    return out.reshape(N_LON * N_LAT, CHUNK, LANES)


def gram_kernel(core, landed, weight, mine, theirs, anomaly, wide, square):
    def widen(s, carry):
        wide[pl.ds(pl.multiple_of(s * CHUNK, 8), CHUNK), :] = landed[s].astype(jnp.float32)
        return carry

    lax.fori_loop(0, N_LON * N_LAT, widen, 0, unroll=16)
    lane = lax.broadcasted_iota(jnp.int32, (1, LANES), 1)
    for g in range(GROUPS):
        if g < LAT_DEV:
            scale = weight[g : g + 1, :LANES]
        else:
            q = g - LAT_DEV
            scale = weight[2 * q : 2 * q + 1, LANES:]
            scale = scale + pltpu.roll(weight[2 * q + 1 : 2 * q + 2, LANES:], SECOND, 1)
            if q < 4:
                last = weight[LAT_DEV - 1 : LAT_DEV, LANES:]
                last = jnp.where((lane >= 16 * q) & (lane < 16 * q + 16), last, 0.0)
                scale = scale + pltpu.roll(last, TAIL - 16 * q, 1)
        cells = wide[pl.ds(g, MONTHS, stride=GROUPS), :]
        mean = jnp.sum(cells, axis=0, keepdims=True) * (1.0 / MONTHS)
        anomaly[:, g * LANES : (g + 1) * LANES] = ((cells - mean) * scale).astype(jnp.bfloat16)
    for i, j in ((0, 0), (0, 1), (1, 1)):
        block = lax.dot_general(
            anomaly[i * ROWB : (i + 1) * ROWB, :],
            anomaly[j * ROWB : (j + 1) * ROWB, :],
            (((1,), (1,)), ((), ())),
            preferred_element_type=jnp.float32,
        )
        for n, (bi, bj) in enumerate(BLOCKS):
            if bi // 2 == i and bj // 2 == j:
                a, c = (bi % 2) * LANES, (bj % 2) * LANES
                square[...] = block[a : a + LANES, c : c + LANES]
                for ref, half in ((mine, core[0]), (theirs, 1 - core[0])):
                    rows = pl.ds(pl.multiple_of(half * HALF, HALF), HALF)
                    ref[pl.ds(n, HALF, stride=PACK), :] = square[rows, :]


def gram_terms(core, landed, weight):
    part = jax.ShapeDtypeStruct((HALF * PACK, LANES), jnp.float32)
    return pl.pallas_call(
        gram_kernel,
        out_shape=(part, part, jax.ShapeDtypeStruct((MONTHS, GROUPS * LANES), jnp.bfloat16)),
        in_specs=[
            pl.BlockSpec(memory_space=pltpu.SMEM),
            pl.BlockSpec(memory_space=pltpu.VMEM),
            pl.BlockSpec(memory_space=pltpu.VMEM),
        ],
        out_specs=(pl.BlockSpec(memory_space=pltpu.VMEM),) * 3,
        scratch_shapes=[
            pltpu.VMEM((N_LON * N_LAT * CHUNK, LANES), jnp.float32),
            pltpu.VMEM((LANES, LANES), jnp.float32),
        ],
        compiler_params=pltpu.CompilerParams(vmem_limit_bytes=32 * 1024 * 1024),
        name="gram_terms",
    )(core, landed, weight)


def turn_kernel(anomaly, turned):
    for g in range(GROUPS):
        turned[g * LANES : (g + 1) * LANES, :] = anomaly[:, g * LANES : (g + 1) * LANES].T


def turn(anomaly):
    return pl.pallas_call(
        turn_kernel,
        out_shape=jax.ShapeDtypeStruct((GROUPS * LANES, MONTHS), jnp.bfloat16),
        in_specs=[pl.BlockSpec(memory_space=pltpu.VMEM)],
        out_specs=pl.BlockSpec(memory_space=pltpu.VMEM),
        compiler_params=pltpu.CompilerParams(vmem_limit_bytes=16 * 1024 * 1024),
        cost_estimate=pl.CostEstimate(flops=2000000000, bytes_accessed=6000000, transcendentals=0),
        name="turn",
    )(anomaly)


def add_kernel(terms, out):
    step = 4 * PACK
    total = terms[0:step, :]
    for s in range(1, HALF // 4):
        total = total + terms[s * step : (s + 1) * step, :]
    row = total[0:PACK] + total[PACK : 2 * PACK] + total[2 * PACK : 3 * PACK] + total[3 * PACK :]
    total = jnp.concatenate([row] * 4, axis=0)
    for s in range(HALF // 4):
        out[s * step : (s + 1) * step, :] = total


def add_terms(terms):
    return pl.pallas_call(
        add_kernel,
        out_shape=jax.ShapeDtypeStruct(terms.shape, jnp.float32),
        in_specs=[pl.BlockSpec(memory_space=pltpu.VMEM)],
        out_specs=pl.BlockSpec(memory_space=pltpu.VMEM),
        compiler_params=pltpu.CompilerParams(vmem_limit_bytes=8 * 1024 * 1024),
        name="add_terms",
    )(terms)


STEP = (2.25, -2.4375, 1.6875, -0.5625, 0.0625)
ROWB = 256
MIRROR = True


def root_kernel(core, mine, theirs, anomaly, patterns_hbm, whitener_hbm, patterns, whitener, ws, hs, ps, ss, zs, wb, out_sems):
    for n, (bi, bj) in enumerate(BLOCKS):
        for ref, half in ((mine, core[0]), (theirs, 1 - core[0])):
            rows = pl.ds(pl.multiple_of(bi * LANES + half * HALF, HALF), HALF)
            whitener[rows, bj * LANES : (bj + 1) * LANES] = ref[pl.ds(n, HALF, stride=PACK), :]
        if bi != bj:
            block = whitener[bi * LANES : (bi + 1) * LANES, bj * LANES : (bj + 1) * LANES]
            whitener[bj * LANES : (bj + 1) * LANES, bi * LANES : (bi + 1) * LANES] = block.T
    gram = whitener[...]
    squares = jnp.sum(gram * gram, axis=0, keepdims=True)
    frobenius = jnp.sqrt(jnp.sum(squares, axis=1, keepdims=True) + 1e-06)
    final_scale = jnp.sqrt(float(NLAT * NLON) / frobenius)

    def split(ref, start, value):
        size = value.shape[0]
        high = value.astype(jnp.bfloat16)
        ref[start : start + size, :] = high
        ref[MONTHS + start : MONTHS + start + size, :] = (value - high.astype(jnp.float32)).astype(jnp.bfloat16)
        if ref.shape[0] == 3 * MONTHS:
            ref[2 * MONTHS + start : 2 * MONTHS + start + size, :] = high

    def join(ref, start):
        high = ref[start : start + ROWB, :].astype(jnp.float32)
        return high + ref[MONTHS + start : MONTHS + start + ROWB, :].astype(jnp.float32)

    def product(left, right):
        def rows(start):
            high = left[start : start + ROWB, :]
            low = left[MONTHS + start : MONTHS + start + ROWB, :]
            return jnp.concatenate([high, high, low], axis=1)

        upper = jnp.dot(rows(0), right[...], preferred_element_type=jnp.float32)
        if not MIRROR:
            return upper, jnp.dot(rows(ROWB), right[...], preferred_element_type=jnp.float32)
        corner = jnp.dot(rows(ROWB), right[:, ROWB:], preferred_element_type=jnp.float32)
        return upper, jnp.concatenate([upper[:, ROWB:].T, corner], axis=1)

    def plus_eye(value, start, scale):
        row = lax.broadcasted_iota(jnp.int32, value.shape, 0) + start
        column = lax.broadcasted_iota(jnp.int32, value.shape, 1)
        return jnp.where(row == column, value + scale, value)

    split(ws, 0, gram * (1.0 / frobenius))
    c0, c1, c2, c3, c4 = STEP
    last = ITERS // 2 - 1

    def double_step(k):
        for n, square in enumerate(product(ws, ws)):
            start = n * ROWB
            split(ss, start, square)
            split(hs, start, plus_eye(c3 * join(ws, start) + c4 * square, start, c2))
        for n, value in enumerate(product(ss, hs)):
            start = n * ROWB
            value = plus_eye(value + c1 * join(ws, start), start, c0)
            split(ps, start, value)
            if k == 0:
                split(zs, start, value)

        if k > 0:
            for n, value in enumerate(product(zs, ps)):
                if k < last:
                    split(zs, n * ROWB, value)
                else:
                    whitener[n * ROWB : (n + 1) * ROWB, :] = value * final_scale

        if k < last:
            for n, value in enumerate(product(ws, ps)):
                split(ss, n * ROWB, value)
            for n, value in enumerate(product(ss, ps)):
                split(ws, n * ROWB, value)

    for k in range(last + 1):
        double_step(k)
    copies = [pltpu.make_async_copy(whitener, whitener_hbm, out_sems.at[LAT_DEV])]
    copies[0].start()
    wb[...] = whitener[...].astype(jnp.bfloat16)

    def group(g):
        return lax.dot_general(
            anomaly[g * LANES : (g + 1) * LANES, :],
            wb[...],
            (((1,), (0,)), ((), ())),
            preferred_element_type=jnp.float32,
        ).astype(jnp.bfloat16)

    def finish(r):
        copy = pltpu.make_async_copy(patterns.at[r], patterns_hbm.at[r], out_sems.at[r])
        copy.start()
        copies.append(copy)

    for q in range(7):
        value = group(LAT_DEV + q)
        patterns[2 * q, LANES:, :] = value[0 : LON_DEV - LANES]
        patterns[2 * q + 1, LANES:, :] = value[SECOND : SECOND + LON_DEV - LANES]
        if q < 4:
            first = LANES + 16 * q
            size = min(16, LON_DEV - first)
            patterns[LAT_DEV - 1, first : first + size, :] = value[TAIL : TAIL + size]
        for r in (2 * q, 2 * q + 1):
            patterns[r, 0:LANES, :] = group(r)
            finish(r)
    patterns[LAT_DEV - 1, 0:LANES, :] = group(LAT_DEV - 1)
    finish(LAT_DEV - 1)
    for copy in copies:
        copy.wait()


def root_and_patterns(core, mine, theirs, turned):
    return pl.pallas_call(
        root_kernel,
        out_shape=(
            jax.ShapeDtypeStruct((LAT_DEV, LON_DEV, MONTHS), jnp.bfloat16),
            jax.ShapeDtypeStruct((MONTHS, MONTHS), jnp.float32),
        ),
        in_specs=[
            pl.BlockSpec(memory_space=pltpu.SMEM),
            pl.BlockSpec(memory_space=pltpu.VMEM),
            pl.BlockSpec(memory_space=pltpu.VMEM),
            pl.BlockSpec(memory_space=pltpu.VMEM),
        ],
        out_specs=(pl.BlockSpec(memory_space=pl.ANY),) * 2,
        scratch_shapes=[
            pltpu.VMEM((LAT_DEV, LON_DEV, MONTHS), jnp.bfloat16),
            pltpu.VMEM((MONTHS, MONTHS), jnp.float32),
            pltpu.VMEM((3 * MONTHS, MONTHS), jnp.bfloat16),
            pltpu.VMEM((3 * MONTHS, MONTHS), jnp.bfloat16),
            pltpu.VMEM((3 * MONTHS, MONTHS), jnp.bfloat16),
            pltpu.VMEM((2 * MONTHS, MONTHS), jnp.bfloat16),
            pltpu.VMEM((2 * MONTHS, MONTHS), jnp.bfloat16),
            pltpu.VMEM((MONTHS, MONTHS), jnp.bfloat16),
            pltpu.SemaphoreType.DMA((LAT_DEV + 1,)),
        ],
        compiler_params=pltpu.CompilerParams(vmem_limit_bytes=32 * 1024 * 1024),
        name="root_and_patterns",
    )(core, mine, theirs, turned)


def exchange(pieces, axes):
    return lax.all_to_all(pieces, axes, split_axis=0, concat_axis=0, tiled=True)


def exchange_packed(packed):
    pieces = packed.reshape(HALF, PACK // 2, 2, LANES)
    return exchange(pieces, SAME_CORE).reshape(packed.shape)


def swap_cores(x):
    return lax.ppermute(x, "core", [(0, 1), (1, 0)])


def local(monthly_field, half_width, land_mask):
    widths = exchange(jnp.broadcast_to(half_width, (N_LAT, 1, LAT_DEV)), LAT).reshape(N_LAT, LAT_DEV)
    windows = cut_windows(monthly_field)
    landed = exchange(smooth(widths, windows), BOTH)
    row_index = lax.axis_index(LAT) * LAT_DEV + jnp.arange(LAT_DEV)
    latitude = math.pi * ((row_index.astype(jnp.float32) + 0.5) / NLAT - 0.5)
    weight = jnp.sqrt(jnp.cos(latitude))[:, None] * land_mask.astype(jnp.float32)
    weight = jnp.pad(weight, ((0, 0), (0, 2 * LANES - LON_DEV)))
    core = lax.axis_index("core").reshape(1)
    mine, theirs, anomaly = gram_terms(core, landed, weight)
    terms = exchange_packed(mine + swap_cores(theirs))
    turned = turn(anomaly)
    mine = exchange_packed(add_terms(terms))
    patterns, whitener = root_and_patterns(core, mine, swap_cores(mine), turned)
    return (jnp.transpose(patterns, (2, 0, 1)), whitener)


def solution(mesh):
    fine = Mesh(mesh.devices.reshape(N_LON, N_LAT // 2, 2), BOTH)
    placed = (P(BOTH, None, None), P(LAT), P(LAT, "lon"))
    return jax.shard_map(
        local, mesh=fine, in_specs=placed, out_specs=(P(None, LAT, "lon"), P()), check_vma=False
    )
```
